32 devices in a mesh: dp: 4 (over y, core), seq: 8 (over z, x).
Axes of the slice: x: 2, y: 2, z: 4, core: 2. Of those that a mesh axis runs over, the one named last changes fastest.
Arguments:
- inputs: float32 [8, 1024, 768], P('dp', 'seq'), may hold values from -6 to 6
- segments: int32 [8, 1024], P('dp', 'seq'), may hold values from 0 to 3
- padding: int32 [8, 1024], P('dp', 'seq'), may hold values 0 or 1
- type_table: float32 [4, 768], replicated, may hold values from -3 to 3
- ln_gain: float32 [2, 2, 768], replicated, may hold values from 0.5 to 1.5
- ln_bias: float32 [2, 2, 768], replicated, may hold values from -1 to 1
- up_weight: bfloat16 [2, 768, 3072], replicated, may hold values from -0.21875 to 0.21875
- up_bias: float32 [2, 3072], replicated, may hold values from -1 to 1
- down_weight: bfloat16 [2, 3072, 768], replicated, may hold values from -0.109375 to 0.109375
- down_bias: float32 [2, 768], replicated, may hold values from -1 to 1
- out_grad: float32 [8, 1024, 768], P('dp', 'seq'), may hold values from -6 to 6
Outputs:
- outputs: float32 [8, 1024, 768], P('dp', 'seq')
- input_grad: float32 [8, 1024, 768], P('dp', 'seq')
- table_grad: float32 [4, 768], replicated
- gain_grad: float32 [2, 2, 768], replicated
- bias_grad: float32 [2, 2, 768], replicated
- up_weight_grad: float32 [2, 768, 3072], P(None, None, 'seq')
- up_bias_grad: float32 [2, 3072], P(None, 'seq')
- down_weight_grad: float32 [2, 3072, 768], P(None, 'seq')
- down_bias_grad: float32 [2, 768], replicated
The draws below stay inside these ranges and needn't reach their ends.
All inputs are finite; a program needn't handle non-finite values. No bound on the sum of `padding` on one device may be relied on, other than what follows from the above.
Results may differ from the reference program's by a relative error of at most 0.0065.
Values sent between devices are 32-bit elements; how exact they have to be, the bound alone decides.
No kernel may reach another device: no remote copies, remote signals or barrier semaphores. Data moves between devices by JAX's collectives and lax.ppermute only.
A program may use at most 192 MiB of HBM per device.

```python
import math
import jax
import jax.numpy as jnp
from jax import lax

D = 768
FF = 3072
NTYPES = 4
L = 1024
LAYERS = 2
ROWS = 8


def plant(values, key, low, high):
    index_at = [jax.random.randint(jax.random.fold_in(key, axis), (), 0, length) for axis, length in enumerate(values.shape)]
    main_axis = values.shape.index(max(values.shape))
    next_to = index_at[:main_axis] + [(index_at[main_axis] + 1) % values.shape[main_axis]] + index_at[main_axis + 1:]
    return values.at[tuple(index_at)].set(low).at[tuple(next_to)].set(high)


def shard_levels(rng, dims, shards, least, largest):
    factor_of = 1.0
    for axis_at, parts in shards:
        steps = jax.random.uniform(jax.random.fold_in(jax.random.fold_in(rng, 6), axis_at), (parts,), jnp.float32, least / len(shards), largest / len(shards))
        factor_of = factor_of * jnp.repeat(jnp.exp(steps), dims[axis_at] // parts).reshape((-1,) + (1,) * (len(dims) - 1 - axis_at))
    return factor_of


def centred(key, extent, scale, most, cuts=(), kind=jnp.bfloat16):
    loudness = shard_levels(key, extent, cuts, -0.22, 0.18) if cuts else 1.0
    values = jax.random.normal(key, extent, jnp.float32) * scale * loudness
    return jnp.minimum(jnp.maximum(values, -most), most).astype(kind)


def setup_inputs(seed: int = 0) -> dict:
    streams_of = jax.random.split(jax.random.key(seed), 12)
    return {
        "inputs": centred(streams_of[0], (ROWS, L, D), 1.0, 6.0, ((0, 4), (1, 8)), jnp.float32),
        "segments": plant(jax.random.randint(streams_of[1], (ROWS, L), 0, NTYPES), jax.random.fold_in(streams_of[1], 1), 0, NTYPES - 1).astype(jnp.int32),
        "padding": plant((jax.random.randint(streams_of[2], (ROWS, L), 0, 8) < 7).astype(jnp.int32), jax.random.fold_in(streams_of[2], 1), 0, 1),
        "type_table": centred(streams_of[3], (NTYPES, D), 0.5, 3.0, (), jnp.float32),
        "ln_gain": jnp.clip(1.0 + 0.1 * jax.random.normal(streams_of[4], (LAYERS, 2, D), jnp.float32), 0.5, 1.5),
        "ln_bias": centred(streams_of[5], (LAYERS, 2, D), 0.2, 1.0, (), jnp.float32),
        "up_weight": centred(streams_of[6], (LAYERS, D, FF), D ** -0.5, 0.21875),
        "up_bias": centred(streams_of[7], (LAYERS, FF), 0.2, 1.0, (), jnp.float32),
        "down_weight": centred(streams_of[8], (LAYERS, FF, D), FF ** -0.5, 0.109375),
        "down_bias": centred(streams_of[9], (LAYERS, D), 0.2, 1.0, (), jnp.float32),
        "out_grad": centred(streams_of[10], (ROWS, L, D), 1.0, 6.0, ((0, 4), (1, 8)), jnp.float32),
    }


EPSILON = 1e-05

@jax.custom_vjp
def low(v):
    return lax.optimization_barrier(v.astype(jnp.bfloat16)).astype(jnp.float32)

@jax.custom_vjp
def low_back(v):
    return v

def low_keep(v):
    return (low(v), None)

def low_pass(kept, grad):
    return (grad,)

def back_keep(v):
    return (v, None)

def back_low(kept, grad):
    return (low(grad),)
low.defvjp(low_keep, low_pass)
low_back.defvjp(back_keep, back_low)

def highest(left, right):
    return jnp.matmul(left, right, precision=lax.Precision.HIGHEST)

def layer_norm(values, gain, shift):
    average = lax.optimization_barrier(jnp.mean(values, axis=-1, keepdims=True))
    centered = values - average
    variance = lax.optimization_barrier(jnp.mean(centered * centered, axis=-1, keepdims=True))
    return centered * lax.rsqrt(variance + EPSILON) * gain + shift

def fourier(values):
    spectrum = jnp.fft.fft2(values, axes=(1, 2))
    return jnp.real(spectrum) / math.sqrt(L * D)

def forward(embedded, table, gains, shifts, up_mat, up_vec, down_mat, down_vec, onehot, live_mask):
    carried = embedded + highest(onehot, table)
    for layer_at in range(LAYERS):
        summed = carried + fourier(carried * live_mask)
        normed = layer_norm(summed, gains[layer_at, 0], shifts[layer_at, 0])
        preact = low_back(highest(low(normed), up_mat[layer_at]) + up_vec[layer_at])
        hidden = low(jax.nn.gelu(preact, approximate=True))
        branch = low_back(highest(hidden, down_mat[layer_at]) + down_vec[layer_at])
        carried = layer_norm(normed + branch, gains[layer_at, 1], shifts[layer_at, 1])
    return carried

def reference(inputs, segments, padding, type_table, ln_gain, ln_bias, up_weight, up_bias, down_weight, down_bias, out_grad):
    group = math.gcd(ROWS, max(1, 4096 // L))
    count = ROWS // group
    params = (type_table.astype(jnp.float32), ln_gain.astype(jnp.float32), ln_bias.astype(jnp.float32), up_weight.astype(jnp.float32), up_bias.astype(jnp.float32), down_weight.astype(jnp.float32), down_bias.astype(jnp.float32))
    totals = jax.tree.map(jnp.zeros_like, params)

    def one_group(carry, number):
        first = number * group
        embedded = lax.dynamic_slice_in_dim(inputs, first, group, 0).astype(jnp.float32)
        types = lax.dynamic_slice_in_dim(segments, first, group, 0)
        live = lax.dynamic_slice_in_dim(padding, first, group, 0)
        cotangent = lax.dynamic_slice_in_dim(out_grad, first, group, 0).astype(jnp.float32)
        onehot = (types[..., None] == jnp.arange(NTYPES, dtype=jnp.int32)).astype(jnp.float32)
        live_mask = live[..., None].astype(jnp.float32)

        def apply_layers(emb, table, gains, shifts, up_mat, up_vec, down_mat, down_vec):
            return forward(emb, table, gains, shifts, up_mat, up_vec, down_mat, down_vec, onehot, live_mask)
        result, puller = jax.vjp(apply_layers, embedded, *params)
        grads = puller(cotangent)
        carry = jax.tree.map(lambda a, b: a + b, carry, tuple(grads[1:]))
        return (carry, (result, grads[0]))
    totals, (results, embed_grads) = lax.scan(one_group, totals, jnp.arange(count, dtype=jnp.int32))
    outputs = results.reshape(ROWS, L, D)
    input_grad = embed_grads.reshape(ROWS, L, D)
    return (outputs, input_grad, totals[0], totals[1], totals[2], totals[3], totals[4], totals[5], totals[6])
```

```python
import math

import jax
import jax.numpy as jnp
import numpy as np
from jax import lax
from jax.experimental import pallas as pl
from jax.experimental.pallas import tpu as pltpu
from jax.sharding import Mesh
from jax.sharding import PartitionSpec as P

EPSILON = 1e-05
DP = ("do", "dy", "core")
SEQ = ("zh", "zl", "x")
ROW = ("zl", "x")
PLANE = ("dy", "core", "x")
ALL = DP + SEQ


def owned(count, part, seq, at):
    step = 2 * count
    second = step - at if at else count
    pos = np.arange(seq * part).reshape(seq, part // step, step)
    return np.stack([pos[:, :, at], pos[:, :, second]], 1).reshape(-1)


def feature_table(width):
    half = width // 2
    angle = np.outer(np.arange(width), np.arange(width)) % width * (2.0 * math.pi / width)
    cos, sin = np.cos(angle) / math.sqrt(width), np.sin(angle) / math.sqrt(width)
    return np.concatenate([cos[:, :half], cos[:, half : half + 1], sin[:, 1:half]], 1)


def position_tables(count, part, seq):
    length = seq * part
    step = 2 * count
    span = length // step
    keep = span // step
    w = 2.0 * math.pi / length
    own = [owned(count, part, seq, i) for i in range(count)]
    local = length // count
    send = np.zeros((2, count, count, 2 * keep, local))
    recv = np.zeros((2, count, count, local, 2 * keep))
    block = np.zeros((2, count, local, local))
    scale = 1.0 / math.sqrt(length)

    def kept(i):
        if i:
            return [(i + step * s, 2) for s in range(keep)]
        ends = [(step * s, 1 if s in (0, keep // 2) else 2) for s in range(keep // 2 + 1)]
        return ends + [(count + step * s, 2) for s in range(keep // 2)]

    for j in range(count):
        n = own[j]
        first = n % step == j
        theta = 2.0 * math.pi * j / step
        for i in range(count):
            if i == j:
                angle = w * (np.outer(n, n) % length)
                block[0, i], block[1, i] = np.cos(angle) * scale, np.sin(angle) * scale
                continue
            at = 0
            slots = {}
            for kap, kinds in kept(i):
                cos, sin = np.cos(w * (kap * n % length)), np.sin(w * (kap * n % length))
                if j:
                    sign = np.where(first, 1.0, -1.0)
                    rows = (cos, sign * sin, sign * cos, sin)
                else:
                    rows = (cos * first, cos * ~first, sin * first, sin * ~first)
                if kinds == 2:
                    send[0, j, i, at], send[0, j, i, at + 1] = rows[:2]
                    send[1, j, i, at], send[1, j, i, at + 1] = rows[2:]
                    slots[kap] = (at, at + 1, 0.0)
                else:
                    phi = w * (kap * j % length)
                    send[0, j, i, at] = math.cos(phi) * rows[0] + math.sin(phi) * rows[1]
                    send[1, j, i, at] = math.cos(phi) * rows[2] + math.sin(phi) * rows[3]
                    slots[kap] = (at, at, phi)
                at += kinds
            for index, k in enumerate(own[i]):
                kap, turn = k % span, k // span
                mirrored = kap not in slots
                p_at, q_at, phi = slots[(span - kap) % span if mirrored else kap]
                pair = np.zeros((2, 2 * keep))
                if p_at == q_at:
                    pair[0, p_at], pair[1, p_at] = math.cos(phi), math.sin(phi)
                else:
                    pair[0, p_at], pair[1, q_at] = 1.0, 1.0
                even, odd = pair, pair
                if j:
                    if mirrored:
                        c, s = math.cos(theta), math.sin(theta)
                        even = odd = np.stack([c * pair[0] + s * pair[1], s * pair[0] - c * pair[1]])
                    c, s = math.cos(theta * turn), math.sin(theta * turn)
                    recv[0, i, j, index] = c * even[0] - s * even[1]
                    recv[1, i, j, index] = s * odd[0] + c * odd[1]
                else:
                    flip = (-1.0) ** turn
                    if mirrored:
                        even, odd = pair * np.array([[1.0], [-1.0]]), pair * np.array([[-1.0], [1.0]])
                    recv[0, i, j, index] = even[0] + flip * even[1]
                    recv[1, i, j, index] = odd[0] + flip * odd[1]
    rows = count * 2 * keep
    send = send.reshape(2, count, rows, local)
    recv = np.moveaxis(recv, 2, 3).reshape(2, count, local, rows) * scale
    return tuple(np.asarray(t, np.float32) for t in (send, recv, block))


def precise(left, right):
    return jnp.matmul(left, right, precision=lax.Precision.HIGHEST)


def wide(left, right, contract):
    return lax.dot_general(left, right, ((contract[:1], contract[1:]), ((), ())), preferred_element_type=jnp.float32)


def normalize(values, gain, shift):
    average = jnp.mean(values, axis=-1, keepdims=True)
    centered = values - average
    variance = jnp.mean(centered * centered, axis=-1, keepdims=True)
    inverse = lax.rsqrt(variance + EPSILON)
    unit = centered * inverse
    return unit * gain + shift, unit, inverse


def norm_back(upstream, unit, inverse, gain):
    scaled = upstream * gain
    first_term = jnp.mean(scaled, axis=-1, keepdims=True)
    second_term = jnp.mean(scaled * unit, axis=-1, keepdims=True)
    return inverse * (scaled - first_term - unit * second_term)


def gelu(values):
    return jax.nn.gelu(values, approximate=True)


def gelu_parts(p):
    c = math.sqrt(2.0 / math.pi)
    square = p * p
    t = jnp.tanh(c * p * (1.0 + 0.044715 * square))
    halves = 0.5 * (1.0 + t)
    slope = halves + 0.5 * p * (1.0 - t * t) * (c + 3.0 * 0.044715 * c * square)
    return p * halves, slope


def grads_kernel(normed_ref, delta_ref, up_ref, bias_ref, down_ref, out_ref):
    planes, rows = out_ref.shape[0], out_ref.shape[1] // 2
    normed = normed_ref[...].astype(jnp.bfloat16)
    delta = delta_ref[...].astype(jnp.bfloat16)
    pre = wide(normed, up_ref[...], (1, 0)) + bias_ref[...]
    value, slope = gelu_parts(pre)
    back = (wide(delta, down_ref[...], (1, 1)) * slope).astype(jnp.bfloat16)
    up = wide(back, normed, (0, 0))
    down = wide(value.astype(jnp.bfloat16), delta, (0, 0))
    parts = [(z, h, a[z * rows : (z + 1) * rows]) for z in range(planes) for h, a in enumerate((up, down))]

    @pl.when(pl.program_id(0) == 0)
    def _():
        for z, h, value in parts:
            out_ref[z, h * rows : (h + 1) * rows] = value

    @pl.when(pl.program_id(0) > 0)
    def _():
        for z, h, value in parts:
            out_ref[z, h * rows : (h + 1) * rows] += value


def weight_grads(normed, delta, up, bias, down, planes):
    tokens, width = normed.shape
    units = up.shape[1]
    block = min(tokens, 512)
    return pl.pallas_call(
        grads_kernel,
        grid=(tokens // block,),
        in_specs=[
            pl.BlockSpec((block, width), lambda i: (i, 0)),
            pl.BlockSpec((block, width), lambda i: (i, 0)),
            pl.BlockSpec((width, units), lambda i: (0, 0)),
            pl.BlockSpec((1, units), lambda i: (0, 0)),
            pl.BlockSpec((units, width), lambda i: (0, 0)),
        ],
        out_specs=pl.BlockSpec((planes, 2 * units // planes, width), lambda i: (0, 0, 0)),
        out_shape=jax.ShapeDtypeStruct((planes, 2 * units // planes, width), jnp.float32),
        compiler_params=pltpu.CompilerParams(vmem_limit_bytes=48 * 2**20),
        cost_estimate=pl.CostEstimate(
            flops=8 * tokens * width * units, bytes_accessed=8 * tokens * width, transcendentals=tokens * units
        ),
        name="weight_grads",
    )(normed, delta, up, bias.reshape(1, units), down)


def local(inputs, segments, padding, type_table, ln_gain, ln_bias, up_weight, up_bias, down_weight, down_bias, out_grad):
    rows, part, width = inputs.shape
    layers = ln_gain.shape[0]
    types = type_table.shape[0]
    hidden_width = up_weight.shape[2]
    seq = lax.axis_size(SEQ)
    count = lax.axis_size(ROW)
    step = 2 * count
    units = part // step
    tokens = rows * part
    half = width // 2
    at = lax.axis_index(ROW)

    feature = jnp.asarray(feature_table(width).astype(np.float32))
    send_t, recv_t, own_t = position_tables(count, part, seq)
    send_t, recv_t, own_t = (lax.dynamic_index_in_dim(jnp.asarray(t), at, 1, False) for t in (send_t, recv_t, own_t))
    chunk = send_t.shape[1] // count
    classes = np.array([[i, step - i if i else count] for i in range(count)])

    def spread(values):
        shaped = values.reshape(rows, units, step, width).transpose(0, 2, 1, 3)
        shaped = shaped[:, classes.reshape(-1)].reshape(seq, 2 * units, width)
        return lax.all_to_all(shaped, SEQ, 0, 0, tiled=True).reshape(tokens, width)

    def gather_back(values):
        shaped = lax.all_to_all(values.reshape(seq, 2 * units, width), SEQ, 0, 0, tiled=True)
        back = np.argsort(classes.reshape(-1))
        shaped = shaped.reshape(rows, step, units, width)[:, back].transpose(0, 2, 1, 3)
        return shaped.reshape(rows, part, width)

    def mark(values):
        whole = lax.all_gather(values, SEQ)[:, lax.axis_index("zh")]
        whole = whole.reshape(seq, units, step)
        pick = lax.dynamic_index_in_dim(jnp.asarray(classes), at, 0, False)
        return jnp.take(whole, pick, axis=2).transpose(0, 2, 1).reshape(tokens, 1)

    def mixer(values):
        spectrum = precise(values, feature)
        lower, upper = spectrum[:, :half], spectrum[:, half:]
        first = lax.broadcasted_iota(jnp.int32, (1, half), 1) == 0

        def stage(tables, low_part, up_part):
            even = precise(tables[0], low_part)
            odd = precise(tables[1], up_part)
            middle = precise(tables[0], up_part[:, :1])
            return even, jnp.where(first, middle, odd)

        even, odd = stage(send_t, lower, upper)
        sent = jnp.concatenate([even, odd], 1).reshape(count, chunk, width)
        got = lax.all_to_all(sent, ROW, 0, 0, tiled=True).reshape(count * chunk, width)
        even, odd = stage(recv_t, got[:, :half], got[:, half:])
        own_even, own_odd = stage(own_t, lower, upper)
        even, odd = even + own_even, odd + own_odd
        sine = jnp.where(first, 0.0, odd)
        head = even - sine
        tail = even + sine
        return jnp.concatenate([head, odd[:, :1], jnp.flip(tail[:, 1:], 1)], 1)

    onehot = segments[..., None] == jnp.arange(types, dtype=jnp.int32)
    embedded = inputs + sum(onehot[..., t : t + 1].astype(jnp.float32) * type_table[t] for t in range(types))
    live = mark(padding).astype(jnp.float32)
    kind = mark(segments)
    carried = spread(embedded)
    upstream = spread(out_grad)

    shares = lax.axis_size(("dy", "core"))
    planes = lax.axis_size(("zh", "zl"))
    columns = lax.axis_size("x")
    unit_block = hidden_width // seq
    piece = unit_block // shares
    starts = [
        (z * columns + lax.axis_index("x")) * unit_block + lax.axis_index(("dy", "core")) * piece for z in range(planes)
    ]

    def cut(array, axis):
        return jnp.concatenate([lax.dynamic_slice_in_dim(array, s, piece, axis) for s in starts], axis)

    saved = []
    for layer in range(layers):
        entered = carried
        mixed = entered + mixer(entered * live)
        normed, unit_first, inverse_first = normalize(mixed, ln_gain[layer, 0], ln_bias[layer, 0])
        normed_low = normed.astype(jnp.bfloat16)
        preact = wide(normed_low, up_weight[layer], (1, 0)) + up_bias[layer]
        hidden = gelu(preact).astype(jnp.bfloat16)
        branch = wide(hidden, down_weight[layer], (1, 0)) + down_bias[layer]
        carried, unit_second, inverse_second = normalize(normed + branch, ln_gain[layer, 1], ln_bias[layer, 1])
        all_normed = lax.all_gather(normed, PLANE, tiled=True)
        saved.append((unit_first, inverse_first, preact, unit_second, inverse_second, all_normed))
    outputs = gather_back(carried)

    minor = [None] * layers
    ups = [None] * layers
    downs = [None] * layers
    for layer in reversed(range(layers)):
        unit_first, inverse_first, preact, unit_second, inverse_second, all_normed = saved[layer]
        gain_second = jnp.sum(upstream * unit_second, 0)
        shift_second = jnp.sum(upstream, 0)
        delta_out = norm_back(upstream, unit_second, inverse_second, ln_gain[layer, 1])
        all_delta = lax.all_gather(delta_out, PLANE, tiled=True)
        delta_branch = delta_out.astype(jnp.bfloat16)
        down_vec = jnp.sum(delta_branch.astype(jnp.float32), 0)
        delta_hidden = wide(delta_branch, down_weight[layer], (1, 1))
        puller = jax.vjp(gelu, preact)[1]
        delta_preact = puller(delta_hidden)[0].astype(jnp.bfloat16)
        up_vec = jnp.sum(delta_preact.astype(jnp.float32), 0)
        delta_normed = delta_out + wide(delta_preact, up_weight[layer], (1, 1))
        gain_first = jnp.sum(delta_normed * unit_first, 0)
        shift_first = jnp.sum(delta_normed, 0)
        delta_mixed = norm_back(delta_normed, unit_first, inverse_first, ln_gain[layer, 0])
        upstream = delta_mixed + live * mixer(delta_mixed)

        up_cut, down_cut = cut(up_weight[layer], 1), cut(down_weight[layer], 0)
        bias_cut = cut(up_bias[layer], 0)
        both = weight_grads(all_normed, all_delta, up_cut, bias_cut, down_cut, planes)
        summed = lax.psum_scatter(both.reshape(planes * 2 * piece, width), ("zh", "zl"), scatter_dimension=0, tiled=True)
        whole = lax.all_gather(summed, ("dy", "core"))
        if lax.axis_size("do") > 1:
            whole = lax.psum(whole, "do")
        ups[layer] = whole[:, :piece].reshape(unit_block, width)
        downs[layer] = whole[:, piece:].reshape(unit_block, width)
        minor[layer] = lax.psum(
            jnp.concatenate(
                [jnp.stack([gain_first, gain_second, shift_first, shift_second, down_vec]), up_vec.reshape(-1, width)]
            ),
            ALL,
        )
    table_grad = lax.psum(jnp.stack([jnp.sum(jnp.where(kind == t, upstream, 0.0), 0) for t in range(types)]), ALL)
    input_grad = gather_back(upstream)
    minor = jnp.stack(minor)
    up_vec = minor[:, 5:].reshape(layers, hidden_width)
    up_vec = lax.dynamic_slice_in_dim(up_vec, lax.axis_index(SEQ) * unit_block, unit_block, 1)
    return (
        outputs,
        input_grad,
        table_grad,
        minor[:, 0:2],
        minor[:, 2:4],
        jnp.stack(ups).transpose(0, 2, 1),
        up_vec,
        jnp.stack(downs),
        minor[:, 4],
    )


def solution(mesh):
    dp, seq = mesh.shape["dp"], mesh.shape["seq"]
    shape = (dp // 4, 2, 2, 2, 2, seq // 4)
    finer = Mesh(mesh.devices.reshape(shape), ALL)
    in_specs = (P(DP, SEQ, None), P(DP, SEQ), P(DP, SEQ)) + (P(),) * 7 + (P(DP, SEQ, None),)
    out_specs = (
        P(DP, SEQ, None),
        P(DP, SEQ, None),
        P(),
        P(),
        P(),
        P(None, None, SEQ),
        P(None, SEQ),
        P(None, SEQ, None),
        P(),
    )
    return jax.shard_map(local, mesh=finer, in_specs=in_specs, out_specs=out_specs, check_vma=False)
```

```python
import functools
import math

import jax
import jax.numpy as jnp
import ml_dtypes
import numpy as np
from jax import lax
from jax.experimental import pallas as pl
from jax.experimental.pallas import tpu as pltpu
from jax.sharding import Mesh
from jax.sharding import PartitionSpec as P

EPSILON = 1e-05
DP = ("do", "dy", "core")
SEQ = ("zh", "zl", "x")
ROW = ("zl", "x")
PLANES = ("zh", "zl")
SHARES = ("dy", "core")
PLANE = ("dy", "core", "x")
ALL = DP + SEQ
MARK = 128
LOW = jnp.bfloat16
HIGH = jnp.float32
VMEM = pl.BlockSpec(memory_space=pltpu.VMEM)
SMEM = pl.BlockSpec(memory_space=pltpu.SMEM)


def split_table(values):
    head = values.astype(ml_dtypes.bfloat16)
    return np.stack([head, (values - head.astype(np.float64)).astype(ml_dtypes.bfloat16)])


def feature_table(width):
    half = width // 2
    angle = np.outer(np.arange(width), np.arange(width)) % width * (2.0 * math.pi / width)
    cos, sin = np.cos(angle) / math.sqrt(width), np.sin(angle) / math.sqrt(width)
    return split_table(np.concatenate([cos[:, :half], cos[:, half : half + 1], sin[:, 1:half]], 1))


def mirror_table(half):
    table = np.zeros((half, half), ml_dtypes.bfloat16)
    table[half - np.arange(1, half), np.arange(1, half)] = 1.0
    return table


def pair_of(count, at):
    return at, 2 * count - at if at else count


def owned(count, part, seq, at):
    first, second = pair_of(count, at)
    pos = np.arange(seq * part).reshape(seq, part // (2 * count), 2 * count)
    return np.stack([pos[:, :, first], pos[:, :, second]], 1).reshape(-1)


def position_tables(count, part, seq):
    length = seq * part
    step = 2 * count
    span = length // step
    keep = span // step
    w = 2.0 * math.pi / length
    own = [owned(count, part, seq, i) for i in range(count)]
    local = length // count
    send = np.zeros((2, count, count, 2 * keep, local))
    recv = np.zeros((2, count, count, local, 2 * keep))
    block = np.zeros((2, count, local, local))
    scale = 1.0 / math.sqrt(length)

    def kept(i):
        if i:
            return [(i + step * s, 2) for s in range(keep)]
        ends = [(step * s, 1 if s in (0, keep // 2) else 2) for s in range(keep // 2 + 1)]
        return ends + [(count + step * s, 2) for s in range(keep // 2)]

    for j in range(count):
        n = own[j]
        first = n % step == j
        theta = 2.0 * math.pi * j / step
        for i in range(count):
            if i == j:
                angle = w * (np.outer(n, n) % length)
                block[0, i], block[1, i] = np.cos(angle) * scale, np.sin(angle) * scale
                continue
            at = 0
            slots = {}
            for kap, kinds in kept(i):
                cos, sin = np.cos(w * (kap * n % length)), np.sin(w * (kap * n % length))
                if j:
                    sign = np.where(first, 1.0, -1.0)
                    rows = (cos, sign * sin, sign * cos, sin)
                else:
                    rows = (cos * first, cos * ~first, sin * first, sin * ~first)
                if kinds == 2:
                    send[0, j, i, at], send[0, j, i, at + 1] = rows[:2]
                    send[1, j, i, at], send[1, j, i, at + 1] = rows[2:]
                    slots[kap] = (at, at + 1, 0.0)
                else:
                    phi = w * (kap * j % length)
                    send[0, j, i, at] = math.cos(phi) * rows[0] + math.sin(phi) * rows[1]
                    send[1, j, i, at] = math.cos(phi) * rows[2] + math.sin(phi) * rows[3]
                    slots[kap] = (at, at, phi)
                at += kinds
            for index, k in enumerate(own[i]):
                kap, turn = k % span, k // span
                mirrored = kap not in slots
                p_at, q_at, phi = slots[(span - kap) % span if mirrored else kap]
                pair = np.zeros((2, 2 * keep))
                if p_at == q_at:
                    pair[0, p_at], pair[1, p_at] = math.cos(phi), math.sin(phi)
                else:
                    pair[0, p_at], pair[1, q_at] = 1.0, 1.0
                even, odd = pair, pair
                if j:
                    if mirrored:
                        c, s = math.cos(theta), math.sin(theta)
                        even = odd = np.stack([c * pair[0] + s * pair[1], s * pair[0] - c * pair[1]])
                    c, s = math.cos(theta * turn), math.sin(theta * turn)
                    recv[0, i, j, index] = c * even[0] - s * even[1]
                    recv[1, i, j, index] = s * odd[0] + c * odd[1]
                else:
                    flip = (-1.0) ** turn
                    if mirrored:
                        even, odd = pair * np.array([[1.0], [-1.0]]), pair * np.array([[-1.0], [1.0]])
                    recv[0, i, j, index] = even[0] + flip * even[1]
                    recv[1, i, j, index] = odd[0] + flip * odd[1]
    recv = recv * scale
    sends, recvs, blocks = [], [], []
    for at in range(seq):
        i = at % count
        order = np.arange(local).reshape(seq, -1)[[at ^ k for k in range(seq)]].reshape(-1)
        others = [i ^ k for k in range(1, count)]
        sends.append(send[:, i, others].reshape(2, -1, local)[:, :, order])
        cos = np.concatenate([recv[0, i, j] for j in others], 1)[order]
        sin = np.concatenate([recv[1, i, j] for j in others], 1)[order]
        recvs.append(np.stack([np.concatenate([cos, -sin], 1), np.concatenate([cos, sin], 1)]))
        cos, sin = (block[h, i][order][:, order] for h in range(2))
        blocks.append(np.stack([np.concatenate([cos, -sin], 1), np.concatenate([cos, sin], 1)]))
    return tuple(np.moveaxis(split_table(np.stack(t)), 0, 1) for t in (sends, recvs, blocks))


def wide(left, right, contract=(1, 0)):
    return lax.dot_general(left, right, ((contract[:1], contract[1:]), ((), ())), preferred_element_type=HIGH)


def split(values):
    head = values.astype(LOW)
    return head, (values - head.astype(HIGH)).astype(LOW)


def triple(left, right):
    return wide(left[0], right[0]) + wide(left[0], right[1]) + wide(left[1], right[0])


def first_lane(values):
    return lax.broadcasted_iota(jnp.int32, values.shape, 1) == 0


def mean(values):
    return jnp.mean(values, axis=-1, keepdims=True)


def normalize(values):
    centered = values - mean(values)
    inverse = lax.rsqrt(mean(centered * centered) + EPSILON)
    return centered * inverse, inverse


def norm_back(upstream, unit, inverse, gain):
    scaled = upstream * gain
    return inverse * (scaled - mean(scaled) - unit * mean(scaled * unit))


def gelu_parts(p):
    c = math.sqrt(2.0 / math.pi)
    square = p * p
    t = jnp.tanh(p * (c + 0.044715 * c * square))
    halves = 0.5 + 0.5 * t
    slope = halves + p * (0.5 - 0.5 * (t * t)) * (c + 3.0 * 0.044715 * c * square)
    return p * halves, slope


def stage_one(values, feature_ref, send_ref, spectrum_ref, sent_refs):
    half = values.shape[1] // 2
    parts = split(values)
    spectrum = triple(parts, (feature_ref[0], feature_ref[1]))
    spectrum_ref[...] = spectrum
    head, tail = split(spectrum)
    lanes = half + 128
    even = triple((send_ref[0, 0], send_ref[1, 0]), (head[:, :lanes], tail[:, :lanes]))
    odd = triple((send_ref[0, 1], send_ref[1, 1]), (head[:, half:], tail[:, half:]))
    middle = jnp.where(first_lane(even[:, half:]), even[:, half:], odd[:, :128])
    rows = sent_refs[0].shape[0]
    for k, ref in enumerate(sent_refs):
        at = slice(k * rows, (k + 1) * rows)
        ref[:, :half] = even[at, :half]
        ref[:, half:lanes] = middle[at]
        ref[:, lanes:] = odd[at, 128:]


def unpack(packed, mirror, table_ref):
    half = packed.shape[1] // 2
    head, tail = split(packed)

    def stack(part):
        low, high = part[:, :half], part[:, half:]
        back = wide(jnp.concatenate([low, high], 0), mirror).astype(LOW)
        count = low.shape[0]
        turned = back[:count]
        middle = jnp.where(first_lane(turned[:, :128]), high[:, :128].astype(HIGH), turned[:, :128].astype(HIGH))
        turned = jnp.concatenate([middle.astype(LOW), turned[:, 128:]], 1)
        edge = jnp.where(first_lane(high[:, :128]), 0.0, high[:, :128].astype(HIGH)).astype(LOW)
        high = jnp.concatenate([edge, high[:, 128:]], 1)
        return jnp.concatenate([low, high], 0), jnp.concatenate([turned, back[count:]], 0)

    head_pair, tail_pair = stack(head), stack(tail)
    sides = [
        triple((table_ref[0, side], table_ref[1, side]), (head_pair[side], tail_pair[side])) for side in range(2)
    ]
    return jnp.concatenate(sides, 1)


def stage_two(got_refs, mirror_ref, recv_ref):
    got = jnp.concatenate([ref[...] for ref in got_refs], 0)
    return unpack(got, mirror_ref[...], recv_ref)


def call(kernel, name, inputs, outs, flops=0, **more):
    size = sum(math.prod(a.shape) * a.dtype.itemsize for a in list(inputs) + list(outs))
    more.setdefault("in_specs", [SMEM if a.dtype == jnp.int32 and a.shape == (1,) else VMEM for a in inputs])
    more.setdefault("out_specs", [VMEM] * len(outs))
    results = pl.pallas_call(
        kernel,
        out_shape=list(outs),
        compiler_params=pltpu.CompilerParams(vmem_limit_bytes=32 * 2**20),
        cost_estimate=pl.CostEstimate(flops=flops, bytes_accessed=size, transcendentals=0),
        name=name,
        **more,
    )(*inputs)
    return list(results)


def array(*shape, dtype=HIGH):
    return jax.ShapeDtypeStruct(shape, dtype)


def class_rows(count, units, dest):
    row, i = dest // count, dest % count
    second = jnp.where(i == 0, count, 2 * count - i)
    return row, (i, second)


def spread_body(count, marked, at_ref, refs):
    if marked:
        values_ref, segments_ref, padding_ref, table_ref, *outs, held = refs
    else:
        values_ref, *outs, held = refs
    rows, part, width = values_ref.shape
    units = part // (2 * count)
    for row in range(rows):
        values = values_ref[row]
        if marked:
            kind = segments_ref[row]
            for t in range(table_ref.shape[0]):
                values = values + jnp.where(kind == t, table_ref[t : t + 1, :], 0.0)
            lane = lax.broadcasted_iota(jnp.int32, (part, MARK), 1)
            live = padding_ref[row].astype(HIGH)
            held[row, :, :, width:] = jnp.where(
                lane == 0, live, jnp.where(lane == 1, kind.astype(HIGH), 0.0)
            ).reshape(units, 2 * count, MARK)
        held[row, :, :, :width] = values.reshape(units, 2 * count, width)
    for k, out in enumerate(outs):
        row, classes = class_rows(count, units, at_ref[0] ^ k)
        for h, at in enumerate(classes):
            out[h * units : (h + 1) * units, :] = held[row, :, at, :]


def collect_kernel(count, at_ref, *refs):
    *blocks, out = refs
    rows, units, step, width = out.shape
    for k, ref in enumerate(blocks):
        row, classes = class_rows(count, units, at_ref[0] ^ k)
        for h, at in enumerate(classes):
            out[row, :, at, :] = ref[h * units : (h + 1) * units, :]


def enter_kernel(blocks, *refs):
    held = refs[:blocks]
    feature_ref, send_ref, carried_ref, marks_ref, spectrum_ref, *sent_refs = refs[blocks:]
    width = carried_ref.shape[1]
    values = jnp.concatenate([ref[...] for ref in held], 0)
    carried_ref[...] = values[:, :width]
    marks_ref[...] = values[:, width:]
    stage_one(values[:, :width] * values[:, width : width + 1], feature_ref, send_ref, spectrum_ref, sent_refs)


def own_kernel(masked, *refs):
    if masked:
        spectrum_ref, carried_ref, mirror_ref, block_ref, marks_ref, out_ref = refs
    else:
        spectrum_ref, carried_ref, mirror_ref, block_ref, out_ref = refs
    mixed = unpack(spectrum_ref[...], mirror_ref[...], block_ref)
    if masked:
        mixed = mixed * marks_ref[:, :1]
    out_ref[...] = carried_ref[...] + mixed


def forward_kernel(layer, last, got, *refs):
    got_refs, refs = refs[:got], refs[got:]
    base_ref, mirror_ref, recv_ref, up_ref, up_bias_ref, down_ref, down_bias_ref, gain_ref, shift_ref, *refs = refs
    if last:
        upstream_ref, *refs = refs
    else:
        marks_ref, feature_ref, send_ref, *refs = refs
    normed_ref, unit_ref, inverse_ref, slope_ref, *refs = refs
    *refs, low_ref, total_ref = refs
    chunk = pl.program_id(0)

    @pl.when(chunk == 0)
    def _():
        mixed = base_ref[...] + stage_two(got_refs, mirror_ref, recv_ref)
        unit, inverse = normalize(mixed)
        unit_ref[...] = unit
        inverse_ref[...] = inverse
        normed = unit * gain_ref[layer, 0:1, :] + shift_ref[layer, 0:1, :]
        normed_ref[...] = normed
        low_ref[...] = normed.astype(LOW)
        total_ref[...] = normed + down_bias_ref[layer : layer + 1, :]

    preact = wide(low_ref[...], up_ref[0]) + up_bias_ref[layer : layer + 1, :]
    value, slope = gelu_parts(preact)
    slope_ref[...] = slope
    total_ref[...] += wide(value.astype(LOW), down_ref[0])

    @pl.when(chunk == pl.num_programs(0) - 1)
    def _():
        unit, inverse = normalize(total_ref[...])
        gain = gain_ref[layer, 1:2, :]
        carried = unit * gain + shift_ref[layer, 1:2, :]
        if last:
            carried_ref, delta_ref, minor_ref = refs
            carried_ref[...] = carried
            delta_out(upstream_ref[...], unit, inverse, gain, delta_ref, minor_ref)
        else:
            unit_two_ref, inverse_two_ref, carried_ref, spectrum_ref, *sent_refs = refs
            unit_two_ref[...] = unit
            inverse_two_ref[...] = inverse
            carried_ref[...] = carried
            stage_one(carried * marks_ref[:, :1], feature_ref, send_ref, spectrum_ref, sent_refs)


def delta_out(upstream, unit, inverse, gain, delta_ref, minor_ref):
    delta = norm_back(upstream, unit, inverse, gain)
    delta_ref[...] = delta
    rows = [upstream * unit, upstream, delta.astype(LOW).astype(HIGH)]
    for at, value in enumerate(rows):
        minor_ref[at : at + 1, :] = jnp.sum(value, 0, keepdims=True)
    minor_ref[len(rows) :, :] = jnp.zeros_like(minor_ref[len(rows) :, :])


def delta_kernel(layer, got, *refs):
    got_refs, refs = refs[:got], refs[got:]
    base_ref, marks_ref, mirror_ref, recv_ref, unit_ref, inverse_ref, gain_ref, delta_ref, minor_ref = refs
    upstream = base_ref[...] + marks_ref[:, :1] * stage_two(got_refs, mirror_ref, recv_ref)
    delta_out(upstream, unit_ref[...], inverse_ref[...], gain_ref[layer, 1:2, :], delta_ref, minor_ref)


def backward_kernel(layer, *refs):
    delta_ref, slope_ref, up_ref, down_ref, unit_ref, inverse_ref, gain_ref, feature_ref, send_ref, *refs = refs
    mixed_ref, minor_ref, spectrum_ref, *sent_refs, low_ref, total_ref = refs
    chunk = pl.program_id(0)

    @pl.when(chunk == 0)
    def _():
        low_ref[...] = delta_ref[...].astype(LOW)
        total_ref[...] = delta_ref[...]
        minor_ref[...] = jnp.zeros_like(minor_ref)

    slope = (wide(low_ref[...], down_ref[0], (1, 1)) * slope_ref[...]).astype(LOW)
    minor_ref[pl.ds(2 + chunk, 1), :] = jnp.sum(slope.astype(HIGH), 0, keepdims=True)
    total_ref[...] += wide(slope, up_ref[0], (1, 1))

    @pl.when(chunk == pl.num_programs(0) - 1)
    def _():
        upstream = total_ref[...]
        unit = unit_ref[...]
        minor_ref[0:1, :] = jnp.sum(upstream * unit, 0, keepdims=True)
        minor_ref[1:2, :] = jnp.sum(upstream, 0, keepdims=True)
        mixed = norm_back(upstream, unit, inverse_ref[...], gain_ref[layer, 0:1, :])
        mixed_ref[...] = mixed
        stage_one(mixed, feature_ref, send_ref, spectrum_ref, sent_refs)


def leave_kernel(types, got, *refs):
    got_refs, refs = refs[:got], refs[got:]
    base_ref, marks_ref, mirror_ref, recv_ref, minor_ref, *outs = refs
    upstream = base_ref[...] + marks_ref[:, :1] * stage_two(got_refs, mirror_ref, recv_ref)
    kind = marks_ref[:, 1:2]
    for t in range(types):
        minor_ref[t : t + 1, :] = jnp.sum(jnp.where(kind == float(t), upstream, 0.0), 0, keepdims=True)
    minor_ref[types:, :] = jnp.zeros_like(minor_ref[types:, :])
    rows = outs[0].shape[0]
    for k, ref in enumerate(outs):
        ref[...] = upstream[k * rows : (k + 1) * rows]


def grads_kernel(normed_ref, delta_ref, up_ref, bias_ref, down_ref, out_ref):
    planes, rows = out_ref.shape[0], out_ref.shape[1] // 2
    normed = normed_ref[...].astype(LOW)
    delta = delta_ref[...].astype(LOW)
    pre = wide(normed, up_ref[...]) + bias_ref[...]
    value, slope = gelu_parts(pre)
    back = (wide(delta, down_ref[...], (1, 1)) * slope).astype(LOW)
    up = wide(back, normed, (0, 0))
    down = wide(value.astype(LOW), delta, (0, 0))
    parts = [(z, h, a[z * rows : (z + 1) * rows]) for z in range(planes) for h, a in enumerate((up, down))]

    @pl.when(pl.program_id(0) == 0)
    def _():
        for z, h, value in parts:
            out_ref[z, h * rows : (h + 1) * rows] = value

    @pl.when(pl.program_id(0) > 0)
    def _():
        for z, h, value in parts:
            out_ref[z, h * rows : (h + 1) * rows] += value


def finish_kernel(layer, at_ref, *refs):
    *pieces, up_ref, down_ref, turned = refs[: len(refs)]
    rows = pieces[0].shape[0] // 2
    for k, ref in enumerate(pieces):
        at = pl.multiple_of((at_ref[0] ^ k) * rows, 8)
        turned[pl.ds(at, rows), :] = ref[:rows, :]
        down_ref[0, pl.ds(at, rows), :] = ref[rows:, :]
    up_ref[0] = turned[...].T


def swap(values, axes, k):
    count = lax.axis_size(axes)
    return lax.ppermute(values, axes, [(i, i ^ k) for i in range(count)])


def exchange(blocks, axes, first=0):
    return [b if k == 0 else swap(b, axes, k) for k, b in enumerate(blocks, first)]


def all_sum(values):
    for axes in (("core",), ("dy", "x"), PLANES, ("do",)):
        moved = [swap(values, axes, k) for k in range(1, lax.axis_size(axes))]
        values = sum(moved, values)
    return values


def plane_gather(values):
    if lax.axis_size("x") > 2:
        return [lax.all_gather(values, PLANE, tiled=True)]
    rows = values.shape[0] // 2
    along_x, along_y = swap(values, "x", 1), swap(values, "dy", 1)
    head, tail = swap(along_x[:rows], "dy", 1), swap(along_y[rows:], "x", 1)
    found = [along_x, along_y, head, tail]
    return [values, swap(values, "core", 1)] + found + [swap(f, "core", 1) for f in found]


def local(inputs, segments, padding, type_table, ln_gain, ln_bias, up_weight, up_bias, down_weight, down_bias, out_grad):
    rows, part, width = inputs.shape
    layers, _, hidden_width = up_weight.shape
    types = type_table.shape[0]
    seq, count = lax.axis_size(SEQ), lax.axis_size(ROW)
    step = 2 * count
    units = part // step
    tokens = rows * part
    block = tokens // seq
    half = width // 2
    place = lax.axis_index(SEQ).reshape(1)

    feature = jnp.asarray(feature_table(width))
    mirror = jnp.asarray(mirror_table(half))
    send_t, recv_t, block_t = (
        lax.dynamic_index_in_dim(jnp.asarray(t), place[0], 0, False) for t in position_tables(count, part, seq)
    )
    chunk = send_t.shape[2] // (count - 1)
    sent_outs = [array(chunk, width)] * (count - 1)
    whole = array(tokens, width)
    thin = array(tokens, 1)
    minor_out = array(8, width)
    steps = hidden_width // width

    def spread(values, *marks):
        span = width + (MARK if marks else 0)
        blocks = call(
            lambda at_ref, *refs: spread_body(count, bool(marks), at_ref, refs),
            "spread",
            (place, values) + marks,
            [array(block, span)] * seq,
            scratch_shapes=[pltpu.VMEM((rows, units, step, span), HIGH)],
        )
        return exchange(blocks, SEQ)

    def collect(blocks):
        got = exchange(blocks, SEQ)
        out = call(
            functools.partial(collect_kernel, count),
            "collect",
            [place] + got,
            [array(rows, units, step, width)],
        )[0]
        return out.reshape(rows, part, width)

    def own(spectrum, carried, marks=None):
        inputs = [spectrum, carried, mirror, block_t] + ([] if marks is None else [marks])
        return call(functools.partial(own_kernel, marks is not None), "own_part", inputs, [whole])[0]

    def weights(layer):
        return [
            pl.BlockSpec((1, width, width), lambda c: (layer, 0, c)),
            pl.BlockSpec((2, width), lambda c: (0, c)),
            pl.BlockSpec((1, width, width), lambda c: (layer, c, 0)),
        ]

    column = pl.BlockSpec((tokens, width), lambda c: (0, c))
    slope_out = array(tokens, hidden_width)
    scratch = [pltpu.VMEM((tokens, width), LOW), pltpu.VMEM((tokens, width), HIGH)]
    flops = 4 * tokens * width * hidden_width

    def forward(layer, got, base, *more):
        last = layer == layers - 1
        inputs = got + [base, mirror, recv_t, up_weight, up_bias, down_weight, down_bias, ln_gain, ln_bias] + list(more)
        outs = [whole, whole, thin, slope_out]
        outs += [whole, whole, minor_out] if last else [whole, thin, whole, whole] + sent_outs
        at = len(got) + 3
        in_specs = [VMEM] * at + weights(layer) + [VMEM] * (len(inputs) - at - 3)
        out_specs = [VMEM] * 3 + [column] + [VMEM] * (len(outs) - 4)
        return call(
            functools.partial(forward_kernel, layer, last, len(got)),
            "layer_forward",
            inputs,
            outs,
            flops,
            grid=(steps,),
            in_specs=in_specs,
            out_specs=out_specs,
            scratch_shapes=scratch,
        )

    def backward(layer, delta, slope, unit, inverse):
        inputs = [delta, slope, up_weight, down_weight, unit, inverse, ln_gain, feature, send_t]
        outs = [whole, minor_out, whole] + sent_outs
        up_spec, _, down_spec = weights(layer)
        return call(
            functools.partial(backward_kernel, layer),
            "layer_backward",
            inputs,
            outs,
            flops,
            grid=(steps,),
            in_specs=[VMEM, column, up_spec, down_spec] + [VMEM] * 5,
            out_specs=[VMEM] * len(outs),
            scratch_shapes=scratch,
        )

    def delta(layer, got, base, marks, unit, inverse):
        inputs = got + [base, marks, mirror, recv_t, unit, inverse, ln_gain]
        return call(functools.partial(delta_kernel, layer, len(got)), "delta", inputs, [whole, minor_out])

    shares, planes, columns = lax.axis_size(SHARES), lax.axis_size(PLANES), lax.axis_size("x")
    unit_block = hidden_width // seq
    piece = unit_block // shares
    share = lax.axis_index(SHARES)
    starts = [(z * columns + lax.axis_index("x")) * unit_block + share * piece for z in range(planes)]

    def cut(values, axis):
        return jnp.concatenate([lax.dynamic_slice_in_dim(values, s, piece, axis) for s in starts], axis)

    cuts = [(cut(up_weight[l], 1), cut(up_bias[l : l + 1], 1), cut(down_weight[l], 0)) for l in range(layers)]

    def weight_grads(layer, normed, delta):
        normed, delta = jnp.concatenate(normed, 0), jnp.concatenate(delta, 0)
        total = normed.shape[0]
        size = min(total, 512)
        whole_of = lambda a: pl.BlockSpec(a.shape, lambda i: (0,) * len(a.shape))
        out = array(planes, 2 * piece, width)
        both = call(
            grads_kernel,
            "weight_grads",
            [normed, delta, *cuts[layer]],
            [out],
            8 * total * width * piece * planes,
            grid=(total // size,),
            in_specs=[pl.BlockSpec((size, width), lambda i: (i, 0))] * 2 + [whole_of(a) for a in cuts[layer]],
            out_specs=[whole_of(out)],
        )[0]
        summed = lax.psum_scatter(both.reshape(-1, width), PLANES, scatter_dimension=0, tiled=True)
        if lax.axis_size("do") > 1:
            summed = lax.psum(summed, "do")
        along = swap(summed, "dy", 1)
        return [summed, swap(summed, "core", 1), along, swap(along, "core", 1)]

    column_of = lambda a: a.reshape(rows, part, 1)
    held = spread(inputs, column_of(segments), column_of(padding), type_table)
    carried, marks, spectrum, *sent = call(
        functools.partial(enter_kernel, seq),
        "enter",
        held + [feature, send_t],
        [whole, array(tokens, MARK), whole] + sent_outs,
    )
    upstream = jnp.concatenate(spread(out_grad), 0)
    saved = []
    for layer in range(layers - 1):
        got = exchange(sent, ROW, 1)
        base = own(spectrum, carried)
        normed, unit, inverse, slope, unit_two, inverse_two, carried, spectrum, *sent = forward(
            layer, got, base, marks, feature, send_t
        )
        saved.append((plane_gather(normed), unit, inverse, slope, unit_two, inverse_two))
    got = exchange(sent, ROW, 1)
    base = own(spectrum, carried)
    normed, unit, inverse, slope, outputs, delta_two, minor_two = forward(layers - 1, got, base, upstream)
    saved.append((plane_gather(normed), unit, inverse, slope))
    outputs = collect([outputs[k * block : (k + 1) * block] for k in range(seq)])

    pieces = [None] * layers
    minors = []
    for layer in reversed(range(layers)):
        all_normed, unit, inverse, slope, *second = saved[layer]
        if second:
            delta_two, minor_two = delta(layer, got, base, marks, *second)
        pieces[layer] = weight_grads(layer, all_normed, plane_gather(delta_two))
        mixed, minor_one, spectrum, *sent = backward(layer, delta_two, slope, unit, inverse)
        minors += [minor_two, minor_one]
        got = exchange(sent, ROW, 1)
        base = own(spectrum, mixed, marks)
    minor_table, *blocks = call(
        functools.partial(leave_kernel, types, len(got)),
        "leave",
        got + [base, marks, mirror, recv_t],
        [minor_out] + [array(block, width)] * seq,
    )
    input_grad = collect(blocks)
    minor = all_sum(jnp.concatenate(minors + [minor_table], 0))
    ends = [minor[16 * (layers - 1 - l) :][:16] for l in range(layers)]
    table_grad = minor[16 * layers :][:types]
    gain_grad = jnp.stack([jnp.stack([e[8], e[0]]) for e in ends])
    shift_grad = jnp.stack([jnp.stack([e[9], e[1]]) for e in ends])
    down_vec = jnp.stack([e[2] for e in ends])
    up_vec = jnp.stack([e[10 : 10 + steps].reshape(-1) for e in ends])
    up_vec = lax.dynamic_slice_in_dim(up_vec, place[0] * unit_block, unit_block, 1)

    outs = [array(layers, width, unit_block), array(layers, unit_block, width)]
    grads = []
    for layer in reversed(range(layers)):
        at = len(pieces[layer]) + 1
        grads = call(
            functools.partial(finish_kernel if not grads else finish_more, layer),
            "finish",
            [share.reshape(1)] + pieces[layer] + grads,
            outs,
            in_specs=[SMEM] + [VMEM] * (at - 1) + [pl.BlockSpec(memory_space=pl.ANY)] * len(grads),
            out_specs=[
                pl.BlockSpec((1,) + o.shape[1:], functools.partial(lambda l, i: (l, 0, 0), layer)) for o in outs
            ],
            grid=(1,),
            input_output_aliases={at: 0, at + 1: 1} if grads else {},
            scratch_shapes=[pltpu.VMEM((unit_block, width), HIGH)],
        )
    up_grad, down_grad = grads
    return outputs, input_grad, table_grad, gain_grad, shift_grad, up_grad, up_vec, down_grad, down_vec


def finish_more(layer, at_ref, *refs):
    pieces = refs[:-5]
    finish_kernel(layer, at_ref, *pieces, *refs[-3:])


def solution(mesh):
    dp, seq = mesh.shape["dp"], mesh.shape["seq"]
    shape = (dp // 4, 2, 2, 2, 2, seq // 4)
    finer = Mesh(mesh.devices.reshape(shape), ALL)
    in_specs = (P(DP, SEQ, None), P(DP, SEQ), P(DP, SEQ)) + (P(),) * 7 + (P(DP, SEQ, None),)
    out_specs = (
        P(DP, SEQ, None),
        P(DP, SEQ, None),
        P(),
        P(),
        P(),
        P(None, None, SEQ),
        P(None, SEQ),
        P(None, SEQ, None),
        P(),
    )
    return jax.shard_map(local, mesh=finer, in_specs=in_specs, out_specs=out_specs, check_vma=False)
```

```python
import functools
import math

import jax
import jax.numpy as jnp
import ml_dtypes
import numpy as np
from jax import lax
from jax.experimental import pallas as pl
from jax.experimental.pallas import tpu as pltpu
from jax.sharding import Mesh
from jax.sharding import PartitionSpec as P

EPSILON = 1e-05
DP = ("do", "dy", "core")
SEQ = ("zh", "zl", "x")
ROW = ("zl", "x")
PLANES = ("zh", "zl")
SHARES = ("dy", "core")
PLANE = ("dy", "core", "x")
ALL = DP + SEQ
MARK = 128
LOW = jnp.bfloat16
HIGH = jnp.float32
VMEM = pl.BlockSpec(memory_space=pltpu.VMEM)
NEAR = pl.BlockSpec(memory_space=pltpu.VMEM)
SMEM = pl.BlockSpec(memory_space=pltpu.SMEM)
ANY = pl.BlockSpec(memory_space=pl.ANY)
HBM = pl.BlockSpec(memory_space=pltpu.HBM)


MICROSECONDS = {
    "spread_marked": 2.0,
    "pick": 1.5,
    "cut": 5.9,
    "enter": 1.7,
    "spread": 1.0,
    "own_part": 1.5,
    "own_fetch": 5.5,
    "mix": 2.2,
    "layer_forward": 12.0,
    "layer_backward": 7.5,
    "layer_feed": 7.5,
    "layer_stream": 12.0,
    "delta": 2.8,
    "weight_grads": 12.0,
    "leave": 0.9,
    "collect": 2.2,
    "finish": 3.3,
}


def split_table(values):
    head = values.astype(ml_dtypes.bfloat16)
    return np.stack([head, (values - head.astype(np.float64)).astype(ml_dtypes.bfloat16)])


def feature_table(width):
    half = width // 2
    angle = np.outer(np.arange(width), np.arange(width)) % width * (2.0 * math.pi / width)
    cos, sin = np.cos(angle) / math.sqrt(width), np.sin(angle) / math.sqrt(width)
    return split_table(np.concatenate([cos[:, :half], cos[:, half : half + 1], sin[:, 1:half]], 1))


def mirror_table(half):
    table = np.zeros((half, half), ml_dtypes.bfloat16)
    table[half - np.arange(1, half), np.arange(1, half)] = 1.0
    return table


def pair_of(count, at):
    return at, 2 * count - at if at else count


def owned(count, part, seq, at):
    first, second = pair_of(count, at)
    pos = np.arange(seq * part).reshape(seq, part // (2 * count), 2 * count)
    return np.stack([pos[:, :, first], pos[:, :, second]], 1).reshape(-1)


def position_tables(count, part, seq):
    length = seq * part
    step = 2 * count
    span = length // step
    keep = span // step
    w = 2.0 * math.pi / length
    own = [owned(count, part, seq, i) for i in range(count)]
    local = length // count
    send = np.zeros((2, count, count, 2 * keep, local))
    recv = np.zeros((2, count, count, local, 2 * keep))
    block = np.zeros((2, count, local, local))
    scale = 1.0 / math.sqrt(length)

    def kept(i):
        if i:
            return [(i + step * s, 2) for s in range(keep)]
        ends = [(step * s, 1 if s in (0, keep // 2) else 2) for s in range(keep // 2 + 1)]
        return ends + [(count + step * s, 2) for s in range(keep // 2)]

    for j in range(count):
        n = own[j]
        first = n % step == j
        theta = 2.0 * math.pi * j / step
        for i in range(count):
            if i == j:
                angle = w * (np.outer(n, n) % length)
                block[0, i], block[1, i] = np.cos(angle) * scale, np.sin(angle) * scale
                continue
            at = 0
            slots = {}
            for kap, kinds in kept(i):
                cos, sin = np.cos(w * (kap * n % length)), np.sin(w * (kap * n % length))
                if j:
                    sign = np.where(first, 1.0, -1.0)
                    rows = (cos, sign * sin, sign * cos, sin)
                else:
                    rows = (cos * first, cos * ~first, sin * first, sin * ~first)
                if kinds == 2:
                    send[0, j, i, at], send[0, j, i, at + 1] = rows[:2]
                    send[1, j, i, at], send[1, j, i, at + 1] = rows[2:]
                    slots[kap] = (at, at + 1, 0.0)
                else:
                    phi = w * (kap * j % length)
                    send[0, j, i, at] = math.cos(phi) * rows[0] + math.sin(phi) * rows[1]
                    send[1, j, i, at] = math.cos(phi) * rows[2] + math.sin(phi) * rows[3]
                    slots[kap] = (at, at, phi)
                at += kinds
            for index, k in enumerate(own[i]):
                kap, turn = k % span, k // span
                mirrored = kap not in slots
                p_at, q_at, phi = slots[(span - kap) % span if mirrored else kap]
                pair = np.zeros((2, 2 * keep))
                if p_at == q_at:
                    pair[0, p_at], pair[1, p_at] = math.cos(phi), math.sin(phi)
                else:
                    pair[0, p_at], pair[1, q_at] = 1.0, 1.0
                even, odd = pair, pair
                if j:
                    if mirrored:
                        c, s = math.cos(theta), math.sin(theta)
                        even = odd = np.stack([c * pair[0] + s * pair[1], s * pair[0] - c * pair[1]])
                    c, s = math.cos(theta * turn), math.sin(theta * turn)
                    recv[0, i, j, index] = c * even[0] - s * even[1]
                    recv[1, i, j, index] = s * odd[0] + c * odd[1]
                else:
                    flip = (-1.0) ** turn
                    if mirrored:
                        even, odd = pair * np.array([[1.0], [-1.0]]), pair * np.array([[-1.0], [1.0]])
                    recv[0, i, j, index] = even[0] + flip * even[1]
                    recv[1, i, j, index] = odd[0] + flip * odd[1]
    recv = recv * scale
    sends, recvs, blocks = [], [], []
    for at in range(seq):
        i = at % count
        order = np.arange(local).reshape(seq, -1)[[at ^ k for k in range(seq)]].reshape(-1)
        others = [i ^ k for k in range(1, count)]
        sends.append(send[:, i, others].reshape(2, -1, local)[:, :, order])
        cos = np.concatenate([recv[0, i, j] for j in others], 1)[order]
        sin = np.concatenate([recv[1, i, j] for j in others], 1)[order]
        recvs.append(np.stack([np.concatenate([cos, -sin], 1), np.concatenate([cos, sin], 1)]))
        cos, sin = (block[h, i][order][:, order] for h in range(2))
        blocks.append(np.stack([np.concatenate([cos, -sin], 1), np.concatenate([cos, sin], 1)]))
    return tuple(np.moveaxis(split_table(np.stack(t)), 0, 1) for t in (sends, recvs, blocks))


def wide(left, right, contract=(1, 0)):
    return lax.dot_general(left, right, ((contract[:1], contract[1:]), ((), ())), preferred_element_type=HIGH)


def split(values):
    head = values.astype(LOW)
    return head, (values - head.astype(HIGH)).astype(LOW)


def triple(left, right):
    return wide(left[0], right[0]) + wide(left[0], right[1]) + wide(left[1], right[0])


def first_lane(values):
    return lax.broadcasted_iota(jnp.int32, values.shape, 1) == 0


def mean(values):
    return jnp.mean(values, axis=-1, keepdims=True)


def normalize(values):
    centered = values - mean(values)
    inverse = lax.rsqrt(mean(centered * centered) + EPSILON)
    return centered * inverse, inverse


def norm_back(upstream, unit, inverse, gain):
    scaled = upstream * gain
    return inverse * (scaled - mean(scaled) - unit * mean(scaled * unit))


def gelu_parts(p):
    c = math.sqrt(2.0 / math.pi)
    square = p * p
    t = jnp.tanh(p * (c + 0.044715 * c * square))
    halves = 0.5 + 0.5 * t
    slope = halves + p * (0.5 - 0.5 * (t * t)) * (c + 3.0 * 0.044715 * c * square)
    return p * halves, slope


def stage_one(values, feature_ref, send_ref, spectrum_ref, sent_refs):
    half = values.shape[1] // 2
    parts = split(values)
    spectrum = triple(parts, (feature_ref[0], feature_ref[1]))
    spectrum_ref[...] = spectrum
    head, tail = split(spectrum)
    lanes = half + 128
    even = triple((send_ref[0, 0], send_ref[1, 0]), (head[:, :lanes], tail[:, :lanes]))
    odd = triple((send_ref[0, 1], send_ref[1, 1]), (head[:, half:], tail[:, half:]))
    middle = jnp.where(first_lane(even[:, half:]), even[:, half:], odd[:, :128])
    rows = sent_refs[0].shape[0]
    for k, ref in enumerate(sent_refs):
        at = slice(k * rows, (k + 1) * rows)
        ref[:, :half] = even[at, :half]
        ref[:, half:lanes] = middle[at]
        ref[:, lanes:] = odd[at, 128:]


def unpack(packed, mirror, table_ref):
    half = packed.shape[1] // 2
    head, tail = split(packed)

    def stack(part):
        low, high = part[:, :half], part[:, half:]
        back = wide(jnp.concatenate([low, high], 0), mirror).astype(LOW)
        count = low.shape[0]
        turned = back[:count]
        middle = jnp.where(first_lane(turned[:, :128]), high[:, :128].astype(HIGH), turned[:, :128].astype(HIGH))
        turned = jnp.concatenate([middle.astype(LOW), turned[:, 128:]], 1)
        edge = jnp.where(first_lane(high[:, :128]), 0.0, high[:, :128].astype(HIGH)).astype(LOW)
        high = jnp.concatenate([edge, high[:, 128:]], 1)
        return jnp.concatenate([low, high], 0), jnp.concatenate([turned, back[count:]], 0)

    head_pair, tail_pair = stack(head), stack(tail)
    sides = [
        triple((table_ref[0, side], table_ref[1, side]), (head_pair[side], tail_pair[side])) for side in range(2)
    ]
    return jnp.concatenate(sides, 1)


def stage_two(got_refs, mirror_ref, recv_ref):
    got = jnp.concatenate([ref[...] for ref in got_refs], 0)
    return unpack(got, mirror_ref[...], recv_ref)


def call(kernel, name, inputs, outs, after=(), limit=24, token=False, near=False, **more):
    count, end = len(after), len(after) + len(inputs) + len(outs)

    def body(*refs):
        if token:
            kernel(*refs[count:end], *refs[end + 1 :])
            refs[end][...] = jnp.zeros_like(refs[end])
        else:
            kernel(*refs[count:])

    in_specs = more.pop("in_specs", None)
    if in_specs is None:
        in_specs = [SMEM if a.dtype == jnp.int32 and len(a.shape) == 1 else VMEM for a in inputs]
    out_specs = list(more.pop("out_specs", [VMEM] * len(outs)))
    far = lambda s: s is HBM or s.block_shape is not None and not near
    place = lambda s: pltpu.HBM if far(s) else pltpu.VMEM if s is NEAR else None
    inputs = [pltpu.with_memory_space_constraint(a, place(s)) if place(s) else a for a, s in zip(inputs, in_specs)]
    out_shape = [place(s)(o.shape, o.dtype) if place(s) else o for o, s in zip(outs, out_specs)]
    results = pl.pallas_call(
        body,
        in_specs=[ANY] * count + list(in_specs),
        out_specs=out_specs + [VMEM] * token,
        out_shape=out_shape + [array(8, 128)] * token,
        compiler_params=pltpu.CompilerParams(vmem_limit_bytes=limit * 2**20),
        cost_estimate=pl.CostEstimate(flops=int(MICROSECONDS[name] * 1.15e+09), bytes_accessed=0, transcendentals=0),
        name=name,
        **more,
    )(*after, *inputs)
    return list(results)


def hold(values, after):
    count = len(after)
    after = [pltpu.with_memory_space_constraint(a, pltpu.HBM) if math.prod(a.shape) > 8192 else a for a in after]
    return pl.pallas_call(
        lambda *refs: None,
        in_specs=[ANY] * (count + 1),
        out_specs=ANY,
        out_shape=array(*values.shape),
        input_output_aliases={count: 0},
        compiler_params=pltpu.CompilerParams(vmem_limit_bytes=2**20),
        name="hold",
    )(*after, values)


def array(*shape, dtype=HIGH):
    return jax.ShapeDtypeStruct(shape, dtype)


def pick_kernel(at_ref, *refs):
    *refs, sems = refs
    half = len(refs) // 2
    wait_all(start_all([(source.at[at_ref[0]], target) for source, target in zip(refs[:half], refs[half:])], sems))


def cut_kernel(layer, order, piece, blocks_ref, shares_ref, up_ref, down_ref, up_out, down_out, held, chosen_up, chosen_down, sems, down_sems):
    count, _, block = held.shape
    copies = []
    for b in range(count):
        start = pl.multiple_of(blocks_ref[b] * block, 128)
        copies.append(start_all([(up_ref.at[layer, :, pl.ds(start, block)], held.at[b])], sems.at[pl.ds(b, 1)]))
    downs = []
    for p, (b, h) in enumerate(order):
        start = pl.multiple_of(blocks_ref[b] * block + shares_ref[h] * piece, 16)
        target = chosen_down.at[p * piece : (p + 1) * piece]
        downs.append(pltpu.make_async_copy(down_ref.at[layer, pl.ds(start, piece), :], target, down_sems.at[p]))
        downs[-1].start()
    row = lax.broadcasted_iota(jnp.int32, (piece, block), 0)
    lane = lax.broadcasted_iota(jnp.int32, (piece, block), 1)
    chosen = [(lane == row + share * piece).astype(HIGH).astype(LOW) for share in (shares_ref[0], shares_ref[1])]
    wait_all(downs)
    outs = start_all([(chosen_down, down_out)], sems.at[pl.ds(count, 1)])
    for b in range(count):
        wait_all(copies[b])
        for p, (of, h) in enumerate(order):
            if of == b:
                chosen_up[p * piece : (p + 1) * piece] = wide(chosen[h], held[b], (1, 1)).astype(LOW)
    wait_all(outs + start_all([(chosen_up, up_out)], sems.at[pl.ds(0, 1)]))


def class_rows(count, dest):
    row, i = dest // count, dest % count
    if isinstance(dest, int):
        return row, pair_of(count, i)
    return row, (i, jnp.where(i == 0, count, 2 * count - i))


def spread_marked_kernel(count, at_ref, *rest):
    sources, (*outs, held), targets, sems = rest[:4], rest[4:-5], rest[-5:-1], rest[-1]
    wait_all(start_all(zip(sources, targets), sems))
    values_ref, segments_ref, padding_ref, table_ref = targets
    rows, part, width = values_ref.shape
    units = part // (2 * count)
    flags = jnp.concatenate([padding_ref[...], segments_ref[...], jnp.zeros((8 - 2 * rows, part), jnp.int32)], 0)
    flags = flags.astype(HIGH).astype(LOW)
    at = lax.broadcasted_iota(jnp.int32, (8, MARK), 0)
    lane = lax.broadcasted_iota(jnp.int32, (8, MARK), 1)
    for row in range(rows):
        pick = ((at == row) & (lane == 0)) | ((at == rows + row) & (lane == 1))
        marks = wide(flags, pick.astype(HIGH).astype(LOW), (0, 0))
        kind = marks[:, 1:2]
        values = values_ref[row]
        for t in range(table_ref.shape[0]):
            values = values + jnp.where(kind == float(t), table_ref[t : t + 1, :], 0.0)
        held[row, :, :, :width] = values.reshape(units, 2 * count, width)
        held[row, :, :, width:] = marks.reshape(units, 2 * count, MARK)
    for k, out in enumerate(outs):
        row, classes = class_rows(count, at_ref[0] ^ k)
        for h, at in enumerate(classes):
            out[h * units : (h + 1) * units, :] = held[row, :, at, :]


def spread_kernel(count, values_ref, out):
    rows, units, step, width = values_ref.shape
    for dest in range(rows * count):
        row, classes = class_rows(count, dest)
        for h, at in enumerate(classes):
            out[dest, h * units : (h + 1) * units, :] = values_ref[row, :, at, :]


def collect_kernel(count, blocks, *outs):
    rows, units, step, width = outs[0].shape
    part = blocks.shape[1] // len(outs)
    for source in range(rows * count):
        row, classes = class_rows(count, source)
        for n, out in enumerate(outs):
            for h, at in enumerate(classes):
                first = n * part + h * units
                out[row, :, at, :] = blocks[source, first : first + units, :]


def turned(at_ref, blocks):
    return [at_ref[0] ^ k for k in range(blocks)]


def enter_kernel(blocks, *refs):
    sources = refs[:blocks]
    feature_ref, send_ref, carried_ref, marks_ref, spectrum_ref, *sent_refs, held, sems = refs[blocks:]
    width = carried_ref.shape[1]
    rows = held.shape[0] // blocks
    wait_all(start_all([(ref, held.at[k * rows : (k + 1) * rows]) for k, ref in enumerate(sources)], sems))
    values = held[:, :width]
    carried_ref[...] = values
    marks_ref[...] = held[:, width:]
    stage_one(values * held[:, width : width + 1], feature_ref, send_ref, spectrum_ref, sent_refs)


def own_kernel(masked, layer, *refs):
    if layer is not None:
        *refs, up_in, down_in, out_ref, up_out, down_out, sems = refs
        copies = start_all([(up_in.at[layer], up_out), (down_in.at[layer], down_out)], sems)
    else:
        *refs, out_ref = refs
        copies = []
    spectrum_ref, carried_ref, mirror_ref, block_ref, *marks = refs
    mixed = unpack(spectrum_ref[...], mirror_ref[...], block_ref)
    if masked:
        mixed = mixed * marks[0][:, :1]
    out_ref[...] = carried_ref[...] + mixed
    wait_all(copies)


LANES = 4


def copies_of(pairs, sems):
    found = []
    for k, (source, target) in enumerate(pairs):
        rows = source.shape[0]
        parts = LANES if rows % (16 * LANES) == 0 else 1
        for part in range(parts):
            at = pl.ds(part * (rows // parts), rows // parts)
            found.append(pltpu.make_async_copy(source.at[at], target.at[at], sems.at[k, part]))
    return found


def start_all(pairs, sems):
    copies = copies_of(pairs, sems)
    for copy in copies:
        copy.start()
    return copies


def wait_all(copies):
    for copy in copies:
        copy.wait()


def keep(unit, inverse, held):
    width = unit.shape[1]
    held[:, :width] = unit
    held[:, width:] = jnp.broadcast_to(inverse, (unit.shape[0], held.shape[1] - width))


def weight_copies(layer, up_ref, down_ref, up_held, down_held, sems, chunk):
    width = up_held.shape[1]
    at = pl.ds(pl.multiple_of(chunk * width, 128), width)
    return (
        pltpu.make_async_copy(up_ref.at[layer, :, at], up_held.at[chunk], sems.at[0, chunk]),
        pltpu.make_async_copy(down_ref.at[layer, at, :], down_held.at[chunk], sems.at[1, chunk]),
    )


def next_weights(layer, refs, chunk):
    wait_all(weight_copies(layer, *refs, chunk))

    @pl.when(chunk + 1 < pl.num_programs(0))
    def _():
        for copy in weight_copies(layer, *refs, chunk + 1):
            copy.start()


def mix_kernel(layer, got, *refs):
    got_refs, refs = refs[:got], refs[got:]
    base_ref, mirror_ref, recv_ref, gain_ref, shift_ref, normed_out, unit_out, held_normed, held, sems = refs
    mixed = base_ref[...] + stage_two(got_refs, mirror_ref, recv_ref)
    unit, inverse = normalize(mixed)
    held_normed[...] = unit * gain_ref[layer, 0:1, :] + shift_ref[layer, 0:1, :]
    copies = start_all([(held_normed, normed_out)], sems)
    keep(unit, inverse, held)
    wait_all(copies + start_all([(held, unit_out)], sems.at[pl.ds(1, 1)]))


def chunk_of(chunk, width):
    return pl.ds(pl.multiple_of(chunk * width, 128), width)


def feed_kernel(layer, last, *refs):
    if last:
        *refs, held, delta_ref, low_ref, total_ref, more_sems, out_sems = refs
    else:
        *refs, held, low_ref, total_ref, up_held, down_held, feature_ref, send_ref, sems, more_sems, out_sems = refs
    normed_in, up_ref, up_bias_ref, down_ref, down_bias_ref, gain_ref, shift_ref, *refs = refs
    chunk = pl.program_id(0)
    width = low_ref.shape[1]
    if last:
        at_ref, upstream_ref, slope_ref, minor_ref, delta_far, carried_out = refs
        fetched = [(normed_in, total_ref)]
    else:
        marks_ref, feature_in, send_in, slope_ref, carried_ref, spectrum_ref, *sent_refs, unit_out = refs
        fetched = [(normed_in, total_ref), (feature_in, feature_ref), (send_in, send_ref)]
        weights = (up_ref, down_ref, up_held, down_held, sems)

    @pl.when(chunk == 0)
    def _():
        copies = start_all(fetched[:1], more_sems)
        if not last:
            for copy in weight_copies(layer, *weights, 0):
                copy.start()
        wait_all(copies)
        normed = total_ref[...]
        low_ref[...] = normed.astype(LOW)
        total_ref[...] = normed + down_bias_ref[layer : layer + 1, :]

    if last:
        at = chunk_of(chunk, width)
        up, down = up_ref[:, at], down_ref[at, :]
    else:
        next_weights(layer, weights, chunk)
        up, down = up_held[chunk], down_held[chunk]

        @pl.when(chunk == 1)
        def _():
            start_all(fetched[1:], more_sems.at[pl.ds(1, 2)])

    preact = wide(low_ref[...], up) + up_bias_ref[layer : layer + 1, :]
    value, slope = gelu_parts(preact)
    slope_ref[...] = slope.astype(slope_ref.dtype)
    total_ref[...] += wide(value.astype(LOW), down)

    @pl.when(chunk == pl.num_programs(0) - 1)
    def _():
        unit, inverse = normalize(total_ref[...])
        gain = gain_ref[layer, 1:2, :]
        carried = unit * gain + shift_ref[layer, 1:2, :]
        if last:
            blocks, rows, _ = upstream_ref.shape
            order = turned(at_ref, blocks)
            upstream = jnp.concatenate([upstream_ref[at] for at in order], 0)
            delta_out(upstream, unit, inverse, gain, delta_ref, minor_ref)
            copies = start_all([(delta_ref, delta_far)], out_sems)
            for k, at in enumerate(order):
                held[at] = carried[k * rows : (k + 1) * rows]
            wait_all(copies + start_all([(held, carried_out)], out_sems.at[pl.ds(1, 1)]))
        else:
            keep(unit, inverse, held)
            copies = start_all([(held, unit_out)], out_sems)
            carried_ref[...] = carried
            wait_all(copies_of(fetched[1:], more_sems.at[pl.ds(1, 2)]))
            stage_one(carried * marks_ref[:, :1], feature_ref, send_ref, spectrum_ref, sent_refs)
            wait_all(copies)


def delta_out(upstream, unit, inverse, gain, delta_ref, minor_ref):
    delta = norm_back(upstream, unit, inverse, gain)
    delta_ref[...] = delta
    rows = [upstream * unit, upstream, delta.astype(LOW).astype(HIGH)]
    for at, value in enumerate(rows):
        minor_ref[at : at + 1, :] = jnp.sum(value, 0, keepdims=True)
    minor_ref[len(rows) :, :] = jnp.zeros_like(minor_ref[len(rows) :, :])


def delta_kernel(layer, got, *refs):
    got_refs, refs = refs[:got], refs[got:]
    base_ref, marks_ref, mirror_ref, recv_ref, unit_in, gain_ref, minor_ref, delta_far, delta_ref, held, sems = refs
    copies = start_all([(unit_in, held)], sems)
    upstream = base_ref[...] + marks_ref[:, :1] * stage_two(got_refs, mirror_ref, recv_ref)
    wait_all(copies)
    width = upstream.shape[1]
    unit, inverse = held[:, :width], held[:, width : width + 1]
    delta_out(upstream, unit, inverse, gain_ref[layer, 1:2, :], delta_ref, minor_ref)
    wait_all(start_all([(delta_ref, delta_far)], sems))


def backward_kernel(layer, near, *refs):
    if near:
        *refs, low_ref, total_ref, held_unit, feature_ref, send_ref, more_sems = refs
    else:
        *refs, low_ref, total_ref, held_unit, feature_ref, send_ref, more_sems, up_held, down_held, sems = refs
    delta_in, slope_ref, up_ref, down_ref, unit_in, gain_ref, feature_in, send_in, *refs = refs
    mixed_ref, minor_ref, spectrum_ref, *sent_refs = refs
    chunk = pl.program_id(0)
    width = low_ref.shape[1]
    fetched = [(unit_in, held_unit), (feature_in, feature_ref), (send_in, send_ref)]

    @pl.when(chunk == 0)
    def _():
        copies = start_all([(delta_in, total_ref)], more_sems)
        if not near:
            for copy in weight_copies(layer, up_ref, down_ref, up_held, down_held, sems, 0):
                copy.start()
        wait_all(copies)
        low_ref[...] = total_ref[...].astype(LOW)
        minor_ref[...] = jnp.zeros_like(minor_ref)

    if near:
        at = chunk_of(chunk, width)
        up, down = up_ref[:, at], down_ref[at, :]
    else:
        next_weights(layer, (up_ref, down_ref, up_held, down_held, sems), chunk)
        up, down = up_held[chunk], down_held[chunk]

    @pl.when(chunk == 1)
    def _():
        start_all(fetched, more_sems.at[pl.ds(1, 3)])

    slope = (wide(low_ref[...], down, (1, 1)) * slope_ref[...].astype(HIGH)).astype(LOW)
    minor_ref[pl.ds(2 + chunk, 1), :] = jnp.sum(slope.astype(HIGH), 0, keepdims=True)
    total_ref[...] += wide(slope, up, (1, 1))

    @pl.when(chunk == pl.num_programs(0) - 1)
    def _():
        upstream = total_ref[...]
        wait_all(copies_of(fetched, more_sems.at[pl.ds(1, 3)]))
        unit, inverse = held_unit[:, :width], held_unit[:, width : width + 1]
        minor_ref[0:1, :] = jnp.sum(upstream * unit, 0, keepdims=True)
        minor_ref[1:2, :] = jnp.sum(upstream, 0, keepdims=True)
        mixed = norm_back(upstream, unit, inverse, gain_ref[layer, 0:1, :])
        mixed_ref[...] = mixed
        stage_one(mixed, feature_ref, send_ref, spectrum_ref, sent_refs)


def leave_kernel(types, got, *refs):
    got_refs, refs = refs[:got], refs[got:]
    at_ref, base_ref, marks_ref, mirror_ref, recv_ref, minor_ref, out, held, sems = refs
    upstream = base_ref[...] + marks_ref[:, :1] * stage_two(got_refs, mirror_ref, recv_ref)
    kind = marks_ref[:, 1:2]
    for t in range(types):
        minor_ref[t : t + 1, :] = jnp.sum(jnp.where(kind == float(t), upstream, 0.0), 0, keepdims=True)
    minor_ref[types:, :] = jnp.zeros_like(minor_ref[types:, :])
    blocks, rows, _ = held.shape
    for k, at in enumerate(turned(at_ref, blocks)):
        held[at] = upstream[k * rows : (k + 1) * rows]
    wait_all(start_all([(held, out)], sems))


def grads_kernel(plan, places, counts, *refs):
    starts_ref, refs = refs[0], refs[1:]
    normed_refs, refs = refs[: counts[0]], refs[counts[0] :]
    delta_refs, refs = refs[: counts[1]], refs[counts[1] :]
    up_in, bias_ref, down_in, *refs = refs
    *refs, normed_held, delta_held, up_ref, down_ref, normed_low, delta_low, hidden, back, sems, more_sems, out_sems = refs
    results, outs = refs[: len(refs) // 2], refs[len(refs) // 2 :]
    step = pl.program_id(0)
    blocks = len(plan)
    rows = normed_held.shape[1]
    units = up_ref.shape[0]
    piece = units // len(places)
    share = units // (pl.num_programs(0) - blocks)

    def copies(b):
        found = []
        for refs, held, parts in ((normed_refs, normed_held, plan[b][0]), (delta_refs, delta_held, plan[b][1])):
            at = 0
            for index, start, count in parts:
                source = refs[index]
                if start is not None:
                    source = source.at[pl.ds(pl.multiple_of(starts_ref[start], 8), count)]
                target = held.at[b % 2, at : at + count]
                found.append(pltpu.make_async_copy(source, target, sems.at[b, len(found)]))
                at += count
        return found

    def start(b):
        for copy in copies(b):
            copy.start()

    for b in range(blocks):

        @pl.when(step == b)
        def _():
            if b == 0:
                start(0)
                fetched = start_all([(up_in, up_ref), (down_in, down_ref)], more_sems)
            wait_all(copies(b))
            if b + 1 < blocks:
                start(b + 1)
            if b == 0:
                wait_all(fetched)
            at = slice(b * rows, (b + 1) * rows)
            normed = normed_held[b % 2].astype(LOW)
            delta = delta_held[b % 2].astype(LOW)
            normed_low[at] = normed
            delta_low[at] = delta
            value, slope = gelu_parts(wide(normed, up_ref[...], (1, 1)) + bias_ref[...])
            hidden[at] = value.astype(LOW)
            back[at] = (wide(delta, down_ref[...], (1, 1)) * slope).astype(LOW)

    def sent(c):
        found = []
        for p in range(c * share // piece, (c + 1) * share // piece):
            for h, (out, slot, first) in enumerate(places[p]):
                at = (slot, pl.ds(first, piece))
                found.append(pltpu.make_async_copy(outs[out].at[at], results[out].at[at], out_sems.at[p, h]))
        return found

    chunks = units // share
    for c in range(chunks):

        @pl.when(step == blocks + c)
        def _():
            at = slice(c * share, (c + 1) * share)
            both = (wide(back[:, at], normed_low[...], (0, 0)), wide(hidden[:, at], delta_low[...], (0, 0)))
            for p in range(c * share // piece, (c + 1) * share // piece):
                first_row = p * piece - c * share
                for (out, slot, first), a in zip(places[p], both):
                    outs[out][slot, first : first + piece] = a[first_row : first_row + piece]
            for copy in sent(c):
                copy.start()
            if c == chunks - 1:
                for k in range(chunks):
                    wait_all(sent(k))


def finish_kernel(layer, at_ref, *refs):
    *pieces, up_ref, down_ref, turned_ref = refs
    rows = pieces[0].shape[0] // 2
    for k, ref in enumerate(pieces[:4]):
        at = pl.multiple_of((at_ref[0] ^ k) * rows, 8)
        turned_ref[pl.ds(at, rows), :] = ref[:rows, :]
        down_ref[0, pl.ds(at, rows), :] = ref[rows:, :]
    up_ref[0] = turned_ref[...].T


def swap(values, axes, k):
    count = lax.axis_size(axes)
    return lax.ppermute(values, axes, [(i, i ^ k) for i in range(count)])


def exchange(blocks, axes, first=0):
    return [b if k == 0 else swap(b, axes, k) for k, b in enumerate(blocks, first)]


def sum_over(values, groups):
    for axes in groups:
        moved = [swap(values, axes, k) for k in range(1, lax.axis_size(axes))]
        values = sum(moved, values)
    return values


def local(inputs, segments, padding, type_table, ln_gain, ln_bias, up_weight, up_bias, down_weight, down_bias, out_grad):
    rows, part, width = inputs.shape
    layers, _, hidden_width = up_weight.shape
    types = type_table.shape[0]
    seq, count = lax.axis_size(SEQ), lax.axis_size(ROW)
    step = 2 * count
    units = part // step
    tokens = rows * part
    block = tokens // seq
    half = width // 2
    place = lax.axis_index(SEQ).reshape(1)

    feature = jnp.asarray(feature_table(width))
    mirror = jnp.asarray(mirror_table(half))
    tables = position_tables(count, part, seq)
    chunk = tables[0].shape[3] // (count - 1)
    sent_outs = [array(chunk, width)] * (count - 1)
    whole = array(tokens, width)
    kept = array(tokens, width + MARK)
    blocks_out = array(seq, block, width)
    minor_out = array(8, width)
    steps = hidden_width // width

    def spread(values, after):
        shaped = values.reshape(rows, units, step, width)
        out, token = call(functools.partial(spread_kernel, count), "spread", [shaped], [blocks_out], after, token=True)
        return lax.all_to_all(out, SEQ, 0, 0, tiled=True), token

    def collect(got, after):
        out = array(rows, units, step, width)
        *back, token = call(functools.partial(collect_kernel, count), "collect", [got], [out], after, token=True)
        return [b.reshape(inputs.shape) for b in back] + [token]

    weight_outs = [array(width, hidden_width, dtype=LOW), array(hidden_width, width, dtype=LOW)]

    def own(spectrum, carried, marks=None, after=(), token=False, layer=None):
        inputs = [spectrum, carried, mirror, block_t] + ([] if marks is None else [marks])
        kernel = functools.partial(own_kernel, marks is not None, layer)
        if layer is None:
            return call(kernel, "own_part", inputs, [whole], after, token=token)
        return call(
            kernel,
            "own_fetch",
            inputs + [up_weight, down_weight],
            [whole] + weight_outs,
            after,
            token=token,
            limit=8,
            in_specs=[VMEM] * len(inputs) + [HBM] * 2,
            out_specs=[VMEM, NEAR, NEAR],
            scratch_shapes=[pltpu.SemaphoreType.DMA((2, LANES))],
        )

    column = pl.BlockSpec((tokens, width), lambda c: (0, c))
    slope_out = array(tokens, hidden_width)
    scratch = [pltpu.VMEM((tokens, width), LOW), pltpu.VMEM((tokens, width), HIGH)]
    scratch += [pltpu.VMEM((steps, width, width), LOW)] * 2
    bias_spec = pl.BlockSpec((layers, width), lambda c: (0, c))

    held_kept = pltpu.VMEM(kept.shape, HIGH)
    dma = lambda n: pltpu.SemaphoreType.DMA((n, LANES))

    held_whole = pltpu.VMEM(whole.shape, HIGH)
    held_tables = [pltpu.VMEM(t, LOW) for t in (feature.shape, tables[0].shape[1:])]

    def mix(layer, got, base, after=()):
        inputs = got + [base, mirror, recv_t, ln_gain, ln_bias]
        return call(
            functools.partial(mix_kernel, layer, len(got)),
            "mix",
            inputs,
            [whole, kept],
            after,
            out_specs=[ANY, ANY] if layer == layers - 1 else [HBM, HBM],
            scratch_shapes=[held_whole, held_kept, dma(2)],
        )

    def feed(layer, normed, up, down, *more, after=(), token=False):
        last = layer == layers - 1
        inputs = [normed, up, up_bias, down, down_bias, ln_gain, ln_bias] + list(more)
        outs = [slope_out]
        outs += [minor_out, whole, blocks_out] if last else [whole, whole] + sent_outs + [kept]
        far = 2 if last else 1
        held = [pltpu.VMEM(blocks_out.shape, HIGH), held_whole] if last else [held_kept]
        fetches = [] if last else scratch[2:] + held_tables + [pltpu.SemaphoreType.DMA((2, steps))]
        weights = NEAR if last else HBM
        return call(
            functools.partial(feed_kernel, layer, last),
            "layer_feed" if last else "layer_forward",
            inputs,
            outs,
            after,
            near=last,
            token=token,
            grid=(steps,),
            in_specs=[ANY if last else HBM, weights, bias_spec, weights]
            + [VMEM] * 3
            + ([SMEM, VMEM] if last else [VMEM, HBM, HBM]),
            out_specs=[column] + [VMEM] * (len(outs) - 1 - far) + ([ANY, HBM] if last else [HBM]),
            scratch_shapes=held + scratch[:2] + fetches + [dma(3), dma(2)],
        )

    def backward(layer, delta, slope, up, down, kept, after=(), token=False):
        inputs = [delta, slope, up, down, kept, ln_gain, feature, send_t]
        outs = [whole, minor_out, whole] + sent_outs
        last = layer == layers - 1
        return call(
            functools.partial(backward_kernel, layer, last),
            "layer_backward" if last else "layer_stream",
            inputs,
            outs,
            after,
            near=last,
            token=token,
            grid=(steps,),
            in_specs=[ANY, column, NEAR, NEAR, ANY, VMEM, HBM, HBM]
            if last
            else [HBM, column, HBM, HBM, HBM, VMEM, HBM, HBM],
            out_specs=[VMEM] * len(outs),
            scratch_shapes=scratch[:2]
            + [held_kept]
            + held_tables
            + [dma(4)]
            + ([] if last else scratch[2:] + [pltpu.SemaphoreType.DMA((2, steps))]),
        )

    def delta(layer, got, base, marks, kept, after=()):
        inputs = got + [base, marks, mirror, recv_t, kept, ln_gain]
        return call(
            functools.partial(delta_kernel, layer, len(got)),
            "delta",
            inputs,
            [minor_out, whole],
            after,
            in_specs=[VMEM] * (len(got) + 4) + [HBM, VMEM],
            out_specs=[VMEM, HBM],
            scratch_shapes=[held_whole, held_kept, dma(1)],
        )

    columns = lax.axis_size("x")
    planes, shares = lax.axis_size(PLANES), lax.axis_size(SHARES)
    unit_block = hidden_width // seq
    piece = unit_block // shares
    x, dy, core, zh, zl = (lax.axis_index(a) for a in ("x", "dy", "core", "zh", "zl"))
    swapped = columns == 2

    def pair_pieces():
        nearby = [0, 1] if swapped else list(range(columns))
        own_x, own_dy, own_zh = (x, dy, zh) if swapped else (0, 0, 0)
        blocks = [((own_zh ^ b) * 2 + zl) * columns + (own_x ^ a) for a in nearby for b in (0, 1)]
        order = [(a * 2 + b, c) for a in nearby for c in (0, 1) for b in (0, 1)]
        return blocks, [(own_dy ^ c) * 2 + core for c in (0, 1)], order

    def plane_pieces():
        blocks = [z * columns + x for z in range(planes)]
        return blocks, [dy * 2 + (core ^ c) for c in (1, 0)], [(z, c) for c in (0, 1) for z in range(planes)]

    def cut(layer, after):
        blocks, shared, order = pair_pieces() if layer == layers - 1 else plane_pieces()
        starts = [blocks[b] * unit_block + shared[h] * piece for b, h in order]
        bias = jnp.concatenate([lax.dynamic_slice(up_bias, (layer, s), (1, piece)) for s in starts], 1)
        if unit_block % 128:
            up = [lax.dynamic_slice_in_dim(up_weight[layer], s, piece, 1).T for s in starts]
            down = [lax.dynamic_slice_in_dim(down_weight[layer], s, piece, 0) for s in starts]
            return jnp.concatenate(up, 0), bias, jnp.concatenate(down, 0), bias
        out = array(piece * len(order), width, dtype=LOW)
        up, down, token = call(
            functools.partial(cut_kernel, layer, order, piece),
            "cut",
            [jnp.stack(blocks).astype(jnp.int32), jnp.stack(shared).astype(jnp.int32), up_weight, down_weight],
            [out, out],
            after,
            token=True,
            in_specs=[SMEM, SMEM, HBM, HBM],
            out_specs=[HBM, HBM],
            scratch_shapes=[
                pltpu.VMEM((len(blocks), width, unit_block), LOW),
                pltpu.VMEM(out.shape, LOW),
                pltpu.VMEM(out.shape, LOW),
                dma(len(blocks) + 1),
                pltpu.SemaphoreType.DMA((len(order),)),
            ],
        )
        return up, bias, down, token

    def weight_grads(normed, starts, deltas, plan, cuts, places, outs, after=()):
        size = sum(r for _, _, r in plan[0][0])
        chosen = cuts[0].shape[0]
        share = max(384 // piece, 1) * piece
        total = len(plan) * size
        inputs = [jnp.stack(starts).astype(jnp.int32)] + normed + deltas + list(cuts[:3])
        return call(
            functools.partial(grads_kernel, plan, places, (len(normed), len(deltas))),
            "weight_grads",
            inputs,
            outs,
            after,
            token=True,
            limit=56,
            grid=(len(plan) + chosen // share,),
            in_specs=[SMEM] + [HBM] * (len(normed) + len(deltas)) + [HBM, VMEM, HBM],
            out_specs=[HBM] * len(outs),
            scratch_shapes=[pltpu.VMEM(o.shape, HIGH) for o in outs]
            + [pltpu.VMEM((2, size, width), HIGH)] * 2
            + [pltpu.VMEM(cuts[0].shape, LOW)] * 2
            + [pltpu.VMEM((total, width), LOW)] * 2
            + [pltpu.VMEM((total, chosen), LOW)] * 2
            + [pltpu.SemaphoreType.DMA((len(plan), 4)), dma(2), pltpu.SemaphoreType.DMA((len(places), 2))],
        )

    def shared_out(summed):
        along = swap(summed, "dy", 1)
        return [summed, swap(summed, "core", 1), along, swap(along, "core", 1)]

    def pair_grads(normed, deltas, cuts, after):
        plan = [([(b, None, tokens)], [(b, None, tokens)]) for b in range(4)]
        order = [(a, c, b) for a in range(columns) for c in (0, 1) for b in (0, 1)]
        if not swapped:
            places = [((0, p, 0), (0, p, piece)) for p in range(len(order))]
            out = array(len(order), 2 * piece, width)
            return weight_grads(normed, [0], deltas, plan, cuts, places, [out], after)
        places = [((a, 2 * c + b, 0), (2 + c, 2 * a + b, 0)) for a, c, b in order]
        return weight_grads(normed, [0], deltas, plan, cuts, places, [array(4, piece, width)] * 4, after)

    def pair_first(sums):
        if not swapped:
            return [lax.psum_scatter(sums[0], ("x", "dy", "zh"), scatter_dimension=0, tiled=True)], []
        up, up_far, down, down_far = sums
        got_up, got_down = swap(up_far, "x", 1), swap(down_far, "dy", 1)
        return [up[2:] + got_up[2:], down[2:] + got_down[2:]], [up[:2] + got_up[:2], down[:2] + got_down[:2]]

    def pair_step(far, near):
        if not swapped:
            return far, near
        got_up, got_down = swap(far[0], "dy", 1), swap(far[1], "x", 1)
        up, down = near
        far = jnp.concatenate([up[1] + got_up[1], down[1] + got_down[1]], 0)
        return [far], [jnp.concatenate([up[0] + got_up[0], down[0] + got_down[0]], 0)]

    def pair_last(far, near):
        if not swapped:
            summed = far[0].reshape(2 * piece, width)
            return lax.psum(summed, "do") if lax.axis_size("do") > 1 else summed
        return near[0] + swap(far[0], "zh", 1)

    def plane_first(values):
        if not swapped:
            return [lax.all_gather(values, ("dy", "x"), tiled=True)]
        return [swap(values, "x", 1), swap(values, "dy", 1)]

    def plane_rest(found):
        if not swapped:
            return []
        rows = tokens // 2
        return [swap(found[0][:rows], "dy", 1), swap(found[1][rows:], "x", 1)]

    def plane_grads(normed, deltas, cuts, after):
        group = lax.axis_size(("dy", "x"))
        out = array(planes, 2 * piece, width)
        places = [((h, z, 0), (h, z, piece)) for h in range(2) for z in range(planes)]
        rows = tokens // 2
        parts = [[(0, None, tokens)], [(1, None, tokens)], [(2, None, tokens)], [(3, None, rows), (4, None, rows)]]
        starts = [((dy ^ a) * columns + (x ^ b)) * tokens for a, b in ((0, 0), (0, 1), (1, 0), (1, 1))]
        if not swapped:
            parts = [[(0, b, tokens)] for b in range(group)]
            starts = [b * tokens for b in range(group)]
        starts = [jnp.asarray(s, jnp.int32) for s in starts]
        plan = [([(0, b, tokens)], parts[b]) for b in range(group)]
        return weight_grads([normed], starts, deltas, plan, cuts, places, [out, out], after)

    def plane_sum(both):
        summed = lax.psum_scatter(both.reshape(-1, width), PLANES, scatter_dimension=0, tiled=True)
        return lax.psum(summed, "do") if lax.axis_size("do") > 1 else summed

    def alone(stage, *operands):
        shapes = jax.eval_shape(stage, *operands)
        blank = lambda *_: jax.tree.map(lambda a: jnp.zeros(a.shape, a.dtype), shapes)
        return lax.cond(place[0] < 1000000, stage, blank, *operands)

    def send_and_own(sent, spectrum, mixed, marks):
        return exchange(sent, ROW, 1), own(spectrum, mixed, marks, token=True)

    held = call(
        functools.partial(spread_marked_kernel, count),
        "spread_marked",
        [place, inputs, segments, padding, type_table],
        [array(block, width + MARK)] * seq,
        in_specs=[SMEM] + [HBM] * 4,
        scratch_shapes=[pltpu.VMEM((rows, units, step, width + MARK), HIGH)]
        + [pltpu.VMEM(a.shape, a.dtype) for a in (inputs, segments, padding, type_table)]
        + [dma(4)],
    )
    held = exchange(held, SEQ)
    send_t, recv_t, block_t = call(
        pick_kernel,
        "pick",
        [place] + [jnp.asarray(t) for t in tables],
        [array(*t.shape[1:], dtype=LOW) for t in tables],
        held[1:4],
        in_specs=[SMEM] + [HBM] * 3,
        scratch_shapes=[dma(3)],
    )
    cuts = [None] * (layers - 1) + [cut(layers - 1, held[1:4])]
    carried, marks, spectrum, *sent = call(
        functools.partial(enter_kernel, seq),
        "enter",
        held + [feature, send_t],
        [whole, array(tokens, MARK), whole] + sent_outs,
        [cuts[-1][3]],
        in_specs=[HBM] * seq + [VMEM] * 2,
        scratch_shapes=[pltpu.VMEM((tokens, width + MARK), HIGH), dma(seq)],
    )
    upstream, made = spread(out_grad, sent[:1])
    saved = []
    for layer in range(layers - 1):
        got = exchange(sent, ROW, 1)
        base = own(spectrum, carried, after=[made])[0]
        normed, kept_one = mix(layer, got, base)
        all_normed = lax.all_gather(normed, ("dy", "x"), tiled=True)
        slope, carried, spectrum, *sent, kept_two = feed(layer, normed, up_weight, down_weight, marks, feature, send_t)
        saved.append((all_normed, kept_one, slope, kept_two))
    got = exchange(sent, ROW, 1)
    base, up, down = own(spectrum, carried, after=[upstream], layer=layers - 1)
    normed, kept_one = mix(layers - 1, got, base)

    def feed_stage(normed, kept, up, down, upstream):
        moved = swap(normed, "core", 1), swap(normed, "zl", 1)
        slope, minor_two, delta, outputs = feed(layers - 1, normed, up, down, place, upstream)
        return moved, minor_two, delta, outputs, backward(layers - 1, delta, slope, up, down, kept)

    moved_normed, minor_two, delta_two, outputs, (mixed, minor_one, spectrum, *sent) = alone(
        feed_stage, normed, kept_one, up, down, upstream
    )
    minors = [minor_two, minor_one]

    def send_and_swap(sent, spectrum, mixed, marks, normed_far, delta_two):
        got = exchange(sent, ROW, 1)
        return got, own(spectrum, mixed, marks)[0], swap(normed_far, "core", 1), swap(delta_two, "core", 1)

    got, base, *moved_delta = alone(send_and_swap, sent, spectrum, mixed, marks, moved_normed[1], delta_two)
    there, kept_one, slope, kept_two = saved[0]

    minor_two, delta_one = delta(0, got, base, marks, kept_two)

    def back_stage(delta_two, delta_one, kept_one, slope):
        cuts = cut(0, [delta_one])
        back = backward(0, delta_one, slope, up_weight, down_weight, kept_one, [cuts[3]])
        return swap(delta_two, "zl", 1), plane_first(delta_one), cuts, back

    delta_far, found, cuts[0], (mixed, minor_one, spectrum, *sent) = alone(
        back_stage, delta_two, delta_one, kept_one, slope
    )
    minors += [minor_two, minor_one]

    def send_and_rest(sent, spectrum, mixed, marks, found):
        return exchange(sent, ROW, 1), own(spectrum, mixed, marks)[0], plane_rest(found)

    got, base, rest = alone(send_and_rest, sent, spectrum, mixed, marks, found)
    found = ([delta_one] if swapped else []) + found + rest

    def grads_stage(normed, delta_two, delta_far, there, found, cuts, outputs):
        deltas = delta_two + [delta_far, swap(delta_far, "core", 1)]
        outputs = lax.all_to_all(outputs, SEQ, 0, 0, tiled=True)
        far, near, token = plane_grads(there, found, cuts[0], [])
        far = swap(far, "core", 1)
        *sums, token = pair_grads(normed, deltas, cuts[1], [token])
        return near + far, sums, outputs

    both, sums, outputs = alone(
        grads_stage,
        [normed, moved_normed[0], moved_normed[1], moved_delta[0]],
        [delta_two, moved_delta[1]],
        delta_far,
        there,
        found,
        cuts,
        outputs,
    )
    whole_sum = plane_sum(both)

    def first_stage(sums, got, base, marks):
        left = call(
            functools.partial(leave_kernel, types, len(got)),
            "leave",
            got + [place, base, marks, mirror, recv_t],
            [minor_out, blocks_out],
            out_specs=[VMEM, HBM],
            scratch_shapes=[pltpu.VMEM(blocks_out.shape, HIGH), dma(1)],
        )
        return pair_first(sums), left

    (far, near), (minor_table, blocks) = alone(first_stage, sums, got, base, marks)

    def middle_stage(far, near, outputs, minors):
        minor = sum_over(jnp.concatenate(minors, 0), [("core",)])
        return pair_step(far, near), minor, collect(outputs, [])[0]

    (far, near), minor, outputs = alone(middle_stage, far, near, outputs, minors + [minor_table])

    share = lax.axis_index(SHARES).reshape(1)
    outs = [array(layers, width, unit_block), array(layers, unit_block, width)]

    def finish(layer, pieces, grads):
        return call(
            functools.partial(finish_kernel, layer),
            "finish",
            [share] + pieces + grads,
            outs,
            in_specs=[SMEM] + [VMEM] * len(pieces) + [ANY] * len(grads),
            out_specs=[
                pl.BlockSpec((1,) + o.shape[1:], functools.partial(lambda l, i: (l, 0, 0), layer)) for o in outs
            ],
            grid=(1,),
            input_output_aliases={5: 0, 6: 1} if grads else {},
            scratch_shapes=[pltpu.VMEM((unit_block, width), HIGH)],
        )

    def last_stage(far, near, minor, whole_sum):
        grads = finish(0, shared_out(whole_sum), [])
        return pair_last(far, near), sum_over(minor, [("dy", "x"), ("do",)]), grads

    summed, minor, grads = alone(last_stage, far, near, minor, whole_sum)

    pieces = shared_out(summed)
    blocks = lax.all_to_all(hold(blocks, [summed]), SEQ, 0, 0, tiled=True)
    minor = sum_over(minor, [PLANES])
    input_grad, _ = collect(blocks, [])
    up_grad, down_grad = finish(1, pieces, grads)
    ends = [minor[16 * (layers - 1 - l) :][:16] for l in range(layers)]
    table_grad = minor[16 * layers :][:types]
    gain_grad = jnp.stack([jnp.stack([e[8], e[0]]) for e in ends])
    shift_grad = jnp.stack([jnp.stack([e[9], e[1]]) for e in ends])
    down_vec = jnp.stack([e[2] for e in ends])
    up_vec = jnp.stack([e[10 : 10 + steps].reshape(-1) for e in ends])
    up_vec = lax.dynamic_slice_in_dim(up_vec, place[0] * unit_block, unit_block, 1)

    return outputs, input_grad, table_grad, gain_grad, shift_grad, up_grad, up_vec, down_grad, down_vec


def solution(mesh):
    dp, seq = mesh.shape["dp"], mesh.shape["seq"]
    shape = (dp // 4, 2, 2, 2, 2, seq // 4)
    finer = Mesh(mesh.devices.reshape(shape), ALL)
    in_specs = (P(DP, SEQ, None), P(DP, SEQ), P(DP, SEQ)) + (P(),) * 7 + (P(DP, SEQ, None),)
    out_specs = (
        P(DP, SEQ, None),
        P(DP, SEQ, None),
        P(),
        P(),
        P(),
        P(None, None, SEQ),
        P(None, SEQ),
        P(None, SEQ, None),
        P(),
    )
    return jax.shard_map(local, mesh=finer, in_specs=in_specs, out_specs=out_specs, check_vma=False)
```

```python
import functools
import math

import jax
import jax.numpy as jnp
import ml_dtypes
import numpy as np
from jax import lax
from jax.experimental import pallas as pl
from jax.experimental.pallas import tpu as pltpu
from jax.sharding import Mesh
from jax.sharding import PartitionSpec as P

EPSILON = 1e-05
DP = ("do", "dy", "core")
SEQ = ("zh", "zl", "x")
ROW = ("zl", "x")
PLANES = ("zh", "zl")
SHARES = ("dy", "core")
PLANE = ("dy", "core", "x")
ALL = DP + SEQ
MARK = 128
LOW = jnp.bfloat16
HIGH = jnp.float32
VMEM = pl.BlockSpec(memory_space=pltpu.VMEM)
NEAR = pl.BlockSpec(memory_space=pltpu.VMEM)
SMEM = pl.BlockSpec(memory_space=pltpu.SMEM)
ANY = pl.BlockSpec(memory_space=pl.ANY)
HBM = pl.BlockSpec(memory_space=pltpu.HBM)


MICROSECONDS = {
    "spread_marked": 2.0,
    "pick": 1.5,
    "cut": 5.9,
    "enter": 1.7,
    "spread": 1.0,
    "own_part": 1.5,
    "own_fetch": 5.5,
    "mix": 2.2,
    "layer_forward": 12.0,
    "layer_backward": 7.5,
    "layer_feed": 7.5,
    "layer_stream": 12.0,
    "delta": 2.8,
    "weight_grads": 3.0,
    "leave": 0.9,
    "collect": 2.2,
    "finish": 3.3,
}


def split_table(values):
    head = values.astype(ml_dtypes.bfloat16)
    return np.stack([head, (values - head.astype(np.float64)).astype(ml_dtypes.bfloat16)])


def feature_table(width):
    half = width // 2
    angle = np.outer(np.arange(width), np.arange(width)) % width * (2.0 * math.pi / width)
    cos, sin = np.cos(angle) / math.sqrt(width), np.sin(angle) / math.sqrt(width)
    return split_table(np.concatenate([cos[:, :half], cos[:, half : half + 1], sin[:, 1:half]], 1))


def mirror_table(half):
    table = np.zeros((half, half), ml_dtypes.bfloat16)
    table[half - np.arange(1, half), np.arange(1, half)] = 1.0
    return table


def pair_of(count, at):
    return at, 2 * count - at if at else count


def owned(count, part, seq, at):
    first, second = pair_of(count, at)
    pos = np.arange(seq * part).reshape(seq, part // (2 * count), 2 * count)
    return np.stack([pos[:, :, first], pos[:, :, second]], 1).reshape(-1)


def position_tables(count, part, seq):
    length = seq * part
    step = 2 * count
    span = length // step
    keep = span // step
    w = 2.0 * math.pi / length
    own = [owned(count, part, seq, i) for i in range(count)]
    local = length // count
    send = np.zeros((2, count, count, 2 * keep, local))
    recv = np.zeros((2, count, count, local, 2 * keep))
    block = np.zeros((2, count, local, local))
    scale = 1.0 / math.sqrt(length)

    def kept(i):
        if i:
            return [(i + step * s, 2) for s in range(keep)]
        ends = [(step * s, 1 if s in (0, keep // 2) else 2) for s in range(keep // 2 + 1)]
        return ends + [(count + step * s, 2) for s in range(keep // 2)]

    for j in range(count):
        n = own[j]
        first = n % step == j
        theta = 2.0 * math.pi * j / step
        for i in range(count):
            if i == j:
                angle = w * (np.outer(n, n) % length)
                block[0, i], block[1, i] = np.cos(angle) * scale, np.sin(angle) * scale
                continue
            at = 0
            slots = {}
            for kap, kinds in kept(i):
                cos, sin = np.cos(w * (kap * n % length)), np.sin(w * (kap * n % length))
                if j:
                    sign = np.where(first, 1.0, -1.0)
                    rows = (cos, sign * sin, sign * cos, sin)
                else:
                    rows = (cos * first, cos * ~first, sin * first, sin * ~first)
                if kinds == 2:
                    send[0, j, i, at], send[0, j, i, at + 1] = rows[:2]
                    send[1, j, i, at], send[1, j, i, at + 1] = rows[2:]
                    slots[kap] = (at, at + 1, 0.0)
                else:
                    phi = w * (kap * j % length)
                    send[0, j, i, at] = math.cos(phi) * rows[0] + math.sin(phi) * rows[1]
                    send[1, j, i, at] = math.cos(phi) * rows[2] + math.sin(phi) * rows[3]
                    slots[kap] = (at, at, phi)
                at += kinds
            for index, k in enumerate(own[i]):
                kap, turn = k % span, k // span
                mirrored = kap not in slots
                p_at, q_at, phi = slots[(span - kap) % span if mirrored else kap]
                pair = np.zeros((2, 2 * keep))
                if p_at == q_at:
                    pair[0, p_at], pair[1, p_at] = math.cos(phi), math.sin(phi)
                else:
                    pair[0, p_at], pair[1, q_at] = 1.0, 1.0
                even, odd = pair, pair
                if j:
                    if mirrored:
                        c, s = math.cos(theta), math.sin(theta)
                        even = odd = np.stack([c * pair[0] + s * pair[1], s * pair[0] - c * pair[1]])
                    c, s = math.cos(theta * turn), math.sin(theta * turn)
                    recv[0, i, j, index] = c * even[0] - s * even[1]
                    recv[1, i, j, index] = s * odd[0] + c * odd[1]
                else:
                    flip = (-1.0) ** turn
                    if mirrored:
                        even, odd = pair * np.array([[1.0], [-1.0]]), pair * np.array([[-1.0], [1.0]])
                    recv[0, i, j, index] = even[0] + flip * even[1]
                    recv[1, i, j, index] = odd[0] + flip * odd[1]
    recv = recv * scale
    sends, recvs, blocks = [], [], []
    for at in range(seq):
        i = at % count
        order = np.arange(local).reshape(seq, -1)[[at ^ k for k in range(seq)]].reshape(-1)
        others = [i ^ k for k in range(1, count)]
        sends.append(send[:, i, others].reshape(2, -1, local)[:, :, order])
        cos = np.concatenate([recv[0, i, j] for j in others], 1)[order]
        sin = np.concatenate([recv[1, i, j] for j in others], 1)[order]
        recvs.append(np.stack([np.concatenate([cos, -sin], 1), np.concatenate([cos, sin], 1)]))
        cos, sin = (block[h, i][order][:, order] for h in range(2))
        blocks.append(np.stack([np.concatenate([cos, -sin], 1), np.concatenate([cos, sin], 1)]))
    return tuple(np.moveaxis(split_table(np.stack(t)), 0, 1) for t in (sends, recvs, blocks))


def wide(left, right, contract=(1, 0)):
    return lax.dot_general(left, right, ((contract[:1], contract[1:]), ((), ())), preferred_element_type=HIGH)


def split(values):
    head = values.astype(LOW)
    return head, (values - head.astype(HIGH)).astype(LOW)


def triple(left, right):
    return wide(left[0], right[0]) + wide(left[0], right[1]) + wide(left[1], right[0])


def first_lane(values):
    return lax.broadcasted_iota(jnp.int32, values.shape, 1) == 0


def mean(values):
    return jnp.mean(values, axis=-1, keepdims=True)


def normalize(values):
    centered = values - mean(values)
    inverse = lax.rsqrt(mean(centered * centered) + EPSILON)
    return centered * inverse, inverse


def norm_back(upstream, unit, inverse, gain):
    scaled = upstream * gain
    return inverse * (scaled - mean(scaled) - unit * mean(scaled * unit))


def gelu_parts(p):
    c = math.sqrt(2.0 / math.pi)
    square = p * p
    t = jnp.tanh(p * (c + 0.044715 * c * square))
    halves = 0.5 + 0.5 * t
    slope = halves + p * (0.5 - 0.5 * (t * t)) * (c + 3.0 * 0.044715 * c * square)
    return p * halves, slope


def stage_one(values, feature_ref, send_ref, spectrum_ref, sent_refs):
    half = values.shape[1] // 2
    parts = split(values)
    spectrum = triple(parts, (feature_ref[0], feature_ref[1]))
    spectrum_ref[...] = spectrum
    head, tail = split(spectrum)
    lanes = half + 128
    even = triple((send_ref[0, 0], send_ref[1, 0]), (head[:, :lanes], tail[:, :lanes]))
    odd = triple((send_ref[0, 1], send_ref[1, 1]), (head[:, half:], tail[:, half:]))
    middle = jnp.where(first_lane(even[:, half:]), even[:, half:], odd[:, :128])
    rows = sent_refs[0].shape[0]
    for k, ref in enumerate(sent_refs):
        at = slice(k * rows, (k + 1) * rows)
        ref[:, :half] = even[at, :half]
        ref[:, half:lanes] = middle[at]
        ref[:, lanes:] = odd[at, 128:]


def unpack(packed, mirror, table_ref):
    half = packed.shape[1] // 2
    head, tail = split(packed)

    def stack(part):
        low, high = part[:, :half], part[:, half:]
        back = wide(jnp.concatenate([low, high], 0), mirror).astype(LOW)
        count = low.shape[0]
        turned = back[:count]
        middle = jnp.where(first_lane(turned[:, :128]), high[:, :128].astype(HIGH), turned[:, :128].astype(HIGH))
        turned = jnp.concatenate([middle.astype(LOW), turned[:, 128:]], 1)
        edge = jnp.where(first_lane(high[:, :128]), 0.0, high[:, :128].astype(HIGH)).astype(LOW)
        high = jnp.concatenate([edge, high[:, 128:]], 1)
        return jnp.concatenate([low, high], 0), jnp.concatenate([turned, back[count:]], 0)

    head_pair, tail_pair = stack(head), stack(tail)
    sides = [
        triple((table_ref[0, side], table_ref[1, side]), (head_pair[side], tail_pair[side])) for side in range(2)
    ]
    return jnp.concatenate(sides, 1)


def stage_two(got_refs, mirror_ref, recv_ref):
    got = jnp.concatenate([ref[...] for ref in got_refs], 0)
    return unpack(got, mirror_ref[...], recv_ref)


def call(kernel, name, inputs, outs, after=(), limit=24, token=False, near=False, **more):
    count, end = len(after), len(after) + len(inputs) + len(outs)

    def body(*refs):
        if token:
            kernel(*refs[count:end], *refs[end + 1 :])
            refs[end][...] = jnp.zeros_like(refs[end])
        else:
            kernel(*refs[count:])

    in_specs = more.pop("in_specs", None)
    if in_specs is None:
        in_specs = [SMEM if a.dtype == jnp.int32 and len(a.shape) == 1 else VMEM for a in inputs]
    out_specs = list(more.pop("out_specs", [VMEM] * len(outs)))
    far = lambda s: s is HBM or s.block_shape is not None and not near
    place = lambda s: pltpu.HBM if far(s) else pltpu.VMEM if s is NEAR else None
    inputs = [pltpu.with_memory_space_constraint(a, place(s)) if place(s) else a for a, s in zip(inputs, in_specs)]
    out_shape = [place(s)(o.shape, o.dtype) if place(s) else o for o, s in zip(outs, out_specs)]
    results = pl.pallas_call(
        body,
        in_specs=[ANY] * count + list(in_specs),
        out_specs=out_specs + [VMEM] * token,
        out_shape=out_shape + [array(8, 128)] * token,
        compiler_params=pltpu.CompilerParams(vmem_limit_bytes=limit * 2**20),
        cost_estimate=pl.CostEstimate(flops=int(MICROSECONDS[name] * 1.15e+09), bytes_accessed=0, transcendentals=0),
        name=name,
        **more,
    )(*after, *inputs)
    return list(results)


def hold(values, after):
    count = len(after)
    after = [pltpu.with_memory_space_constraint(a, pltpu.HBM) if math.prod(a.shape) > 8192 else a for a in after]
    return pl.pallas_call(
        lambda *refs: None,
        in_specs=[ANY] * (count + 1),
        out_specs=ANY,
        out_shape=array(*values.shape),
        input_output_aliases={count: 0},
        compiler_params=pltpu.CompilerParams(vmem_limit_bytes=2**20),
        name="hold",
    )(*after, values)


def array(*shape, dtype=HIGH):
    return jax.ShapeDtypeStruct(shape, dtype)


def pick_kernel(at_ref, *refs):
    *refs, sems = refs
    half = len(refs) // 2
    wait_all(start_all([(source.at[at_ref[0]], target) for source, target in zip(refs[:half], refs[half:])], sems))


def cut_kernel(layer, order, piece, blocks_ref, shares_ref, up_ref, down_ref, up_out, down_out, held, chosen_up, chosen_down, sems, down_sems):
    count, _, block = held.shape
    copies = []
    for b in range(count):
        start = pl.multiple_of(blocks_ref[b] * block, 128)
        copies.append(start_all([(up_ref.at[layer, :, pl.ds(start, block)], held.at[b])], sems.at[pl.ds(b, 1)]))
    downs = []
    for p, (b, h) in enumerate(order):
        start = pl.multiple_of(blocks_ref[b] * block + shares_ref[h] * piece, 16)
        target = chosen_down.at[p * piece : (p + 1) * piece]
        downs.append(pltpu.make_async_copy(down_ref.at[layer, pl.ds(start, piece), :], target, down_sems.at[p]))
        downs[-1].start()
    row = lax.broadcasted_iota(jnp.int32, (piece, block), 0)
    lane = lax.broadcasted_iota(jnp.int32, (piece, block), 1)
    chosen = [(lane == row + share * piece).astype(HIGH).astype(LOW) for share in (shares_ref[0], shares_ref[1])]
    wait_all(downs)
    outs = start_all([(chosen_down, down_out)], sems.at[pl.ds(count, 1)])
    for b in range(count):
        wait_all(copies[b])
        for p, (of, h) in enumerate(order):
            if of == b:
                chosen_up[p * piece : (p + 1) * piece] = wide(chosen[h], held[b], (1, 1)).astype(LOW)
    wait_all(outs + start_all([(chosen_up, up_out)], sems.at[pl.ds(0, 1)]))


def class_rows(count, dest):
    row, i = dest // count, dest % count
    if isinstance(dest, int):
        return row, pair_of(count, i)
    return row, (i, jnp.where(i == 0, count, 2 * count - i))


def spread_marked_kernel(count, at_ref, *rest):
    sources, (*outs, held), targets, sems = rest[:4], rest[4:-5], rest[-5:-1], rest[-1]
    wait_all(start_all(zip(sources, targets), sems))
    values_ref, segments_ref, padding_ref, table_ref = targets
    rows, part, width = values_ref.shape
    units = part // (2 * count)
    flags = jnp.concatenate([padding_ref[...], segments_ref[...], jnp.zeros((8 - 2 * rows, part), jnp.int32)], 0)
    flags = flags.astype(HIGH).astype(LOW)
    at = lax.broadcasted_iota(jnp.int32, (8, MARK), 0)
    lane = lax.broadcasted_iota(jnp.int32, (8, MARK), 1)
    for row in range(rows):
        pick = ((at == row) & (lane == 0)) | ((at == rows + row) & (lane == 1))
        marks = wide(flags, pick.astype(HIGH).astype(LOW), (0, 0))
        kind = marks[:, 1:2]
        values = values_ref[row]
        for t in range(table_ref.shape[0]):
            values = values + jnp.where(kind == float(t), table_ref[t : t + 1, :], 0.0)
        held[row, :, :, :width] = values.reshape(units, 2 * count, width)
        held[row, :, :, width:] = marks.reshape(units, 2 * count, MARK)
    for k, out in enumerate(outs):
        row, classes = class_rows(count, at_ref[0] ^ k)
        for h, at in enumerate(classes):
            out[h * units : (h + 1) * units, :] = held[row, :, at, :]


def spread_kernel(count, values_ref, out):
    rows, units, step, width = values_ref.shape
    for dest in range(rows * count):
        row, classes = class_rows(count, dest)
        for h, at in enumerate(classes):
            out[dest, h * units : (h + 1) * units, :] = values_ref[row, :, at, :]


def collect_kernel(count, blocks, *outs):
    rows, units, step, width = outs[0].shape
    part = blocks.shape[1] // len(outs)
    for source in range(rows * count):
        row, classes = class_rows(count, source)
        for n, out in enumerate(outs):
            for h, at in enumerate(classes):
                first = n * part + h * units
                out[row, :, at, :] = blocks[source, first : first + units, :]


def turned(at_ref, blocks):
    return [at_ref[0] ^ k for k in range(blocks)]


def enter_kernel(blocks, *refs):
    sources = refs[:blocks]
    feature_ref, send_ref, carried_ref, marks_ref, spectrum_ref, *sent_refs, held, sems = refs[blocks:]
    width = carried_ref.shape[1]
    rows = held.shape[0] // blocks
    wait_all(start_all([(ref, held.at[k * rows : (k + 1) * rows]) for k, ref in enumerate(sources)], sems))
    values = held[:, :width]
    carried_ref[...] = values
    marks_ref[...] = held[:, width:]
    stage_one(values * held[:, width : width + 1], feature_ref, send_ref, spectrum_ref, sent_refs)


def own_kernel(masked, layer, *refs):
    if layer is not None:
        *refs, up_in, down_in, out_ref, up_out, down_out, sems = refs
        copies = start_all([(up_in.at[layer], up_out), (down_in.at[layer], down_out)], sems)
    else:
        *refs, out_ref = refs
        copies = []
    spectrum_ref, carried_ref, mirror_ref, block_ref, *marks = refs
    mixed = unpack(spectrum_ref[...], mirror_ref[...], block_ref)
    if masked:
        mixed = mixed * marks[0][:, :1]
    out_ref[...] = carried_ref[...] + mixed
    wait_all(copies)


LANES = 4


def copies_of(pairs, sems):
    found = []
    for k, (source, target) in enumerate(pairs):
        rows = source.shape[0]
        parts = LANES if rows % (16 * LANES) == 0 else 1
        for part in range(parts):
            at = pl.ds(part * (rows // parts), rows // parts)
            found.append(pltpu.make_async_copy(source.at[at], target.at[at], sems.at[k, part]))
    return found


def start_all(pairs, sems):
    copies = copies_of(pairs, sems)
    for copy in copies:
        copy.start()
    return copies


def wait_all(copies):
    for copy in copies:
        copy.wait()


def keep(unit, inverse, held):
    width = unit.shape[1]
    held[:, :width] = unit
    held[:, width:] = jnp.broadcast_to(inverse, (unit.shape[0], held.shape[1] - width))


def weight_copies(layer, up_ref, down_ref, up_held, down_held, sems, chunk):
    width = up_held.shape[1]
    at = pl.ds(pl.multiple_of(chunk * width, 128), width)
    return (
        pltpu.make_async_copy(up_ref.at[layer, :, at], up_held.at[chunk], sems.at[0, chunk]),
        pltpu.make_async_copy(down_ref.at[layer, at, :], down_held.at[chunk], sems.at[1, chunk]),
    )


def next_weights(layer, refs, chunk):
    wait_all(weight_copies(layer, *refs, chunk))

    @pl.when(chunk + 1 < pl.num_programs(0))
    def _():
        for copy in weight_copies(layer, *refs, chunk + 1):
            copy.start()


def mix_kernel(layer, got, *refs):
    got_refs, refs = refs[:got], refs[got:]
    base_ref, mirror_ref, recv_ref, gain_ref, shift_ref, normed_out, unit_out, held_normed, held, sems = refs
    mixed = base_ref[...] + stage_two(got_refs, mirror_ref, recv_ref)
    unit, inverse = normalize(mixed)
    held_normed[...] = unit * gain_ref[layer, 0:1, :] + shift_ref[layer, 0:1, :]
    copies = start_all([(held_normed, normed_out)], sems)
    keep(unit, inverse, held)
    wait_all(copies + start_all([(held, unit_out)], sems.at[pl.ds(1, 1)]))


def chunk_of(chunk, width):
    return pl.ds(pl.multiple_of(chunk * width, 128), width)


def feed_kernel(layer, last, *refs):
    if last:
        *refs, held, delta_ref, low_ref, total_ref, more_sems, out_sems = refs
    else:
        *refs, held, low_ref, total_ref, up_held, down_held, feature_ref, send_ref, sems, more_sems, out_sems = refs
    normed_in, up_ref, up_bias_ref, down_ref, down_bias_ref, gain_ref, shift_ref, *refs = refs
    chunk = pl.program_id(0)
    width = low_ref.shape[1]
    if last:
        at_ref, upstream_ref, slope_ref, minor_ref, delta_far, carried_out = refs
        fetched = [(normed_in, total_ref)]
    else:
        marks_ref, feature_in, send_in, slope_ref, carried_ref, spectrum_ref, *sent_refs, unit_out = refs
        fetched = [(normed_in, total_ref), (feature_in, feature_ref), (send_in, send_ref)]
        weights = (up_ref, down_ref, up_held, down_held, sems)

    @pl.when(chunk == 0)
    def _():
        copies = start_all(fetched[:1], more_sems)
        if not last:
            for copy in weight_copies(layer, *weights, 0):
                copy.start()
        wait_all(copies)
        normed = total_ref[...]
        low_ref[...] = normed.astype(LOW)
        total_ref[...] = normed + down_bias_ref[layer : layer + 1, :]

    if last:
        at = chunk_of(chunk, width)
        up, down = up_ref[:, at], down_ref[at, :]
    else:
        next_weights(layer, weights, chunk)
        up, down = up_held[chunk], down_held[chunk]

        @pl.when(chunk == 1)
        def _():
            start_all(fetched[1:], more_sems.at[pl.ds(1, 2)])

    preact = wide(low_ref[...], up) + up_bias_ref[layer : layer + 1, :]
    value, slope = gelu_parts(preact)
    slope_ref[...] = slope.astype(slope_ref.dtype)
    total_ref[...] += wide(value.astype(LOW), down)

    @pl.when(chunk == pl.num_programs(0) - 1)
    def _():
        unit, inverse = normalize(total_ref[...])
        gain = gain_ref[layer, 1:2, :]
        carried = unit * gain + shift_ref[layer, 1:2, :]
        if last:
            blocks, rows, _ = upstream_ref.shape
            order = turned(at_ref, blocks)
            upstream = jnp.concatenate([upstream_ref[at] for at in order], 0)
            delta_out(upstream, unit, inverse, gain, delta_ref, minor_ref)
            copies = start_all([(delta_ref, delta_far)], out_sems)
            for k, at in enumerate(order):
                held[at] = carried[k * rows : (k + 1) * rows]
            wait_all(copies + start_all([(held, carried_out)], out_sems.at[pl.ds(1, 1)]))
        else:
            keep(unit, inverse, held)
            copies = start_all([(held, unit_out)], out_sems)
            carried_ref[...] = carried
            wait_all(copies_of(fetched[1:], more_sems.at[pl.ds(1, 2)]))
            stage_one(carried * marks_ref[:, :1], feature_ref, send_ref, spectrum_ref, sent_refs)
            wait_all(copies)


def delta_out(upstream, unit, inverse, gain, delta_ref, minor_ref):
    delta = norm_back(upstream, unit, inverse, gain)
    delta_ref[...] = delta
    rows = [upstream * unit, upstream, delta.astype(LOW).astype(HIGH)]
    for at, value in enumerate(rows):
        minor_ref[at : at + 1, :] = jnp.sum(value, 0, keepdims=True)
    minor_ref[len(rows) :, :] = jnp.zeros_like(minor_ref[len(rows) :, :])


def delta_kernel(layer, got, *refs):
    got_refs, refs = refs[:got], refs[got:]
    base_ref, marks_ref, mirror_ref, recv_ref, unit_in, gain_ref, minor_ref, delta_far, delta_ref, held, sems = refs
    copies = start_all([(unit_in, held)], sems)
    upstream = base_ref[...] + marks_ref[:, :1] * stage_two(got_refs, mirror_ref, recv_ref)
    wait_all(copies)
    width = upstream.shape[1]
    unit, inverse = held[:, :width], held[:, width : width + 1]
    delta_out(upstream, unit, inverse, gain_ref[layer, 1:2, :], delta_ref, minor_ref)
    wait_all(start_all([(delta_ref, delta_far)], sems))


def backward_kernel(layer, near, *refs):
    if near:
        *refs, low_ref, total_ref, held_unit, feature_ref, send_ref, more_sems = refs
    else:
        *refs, low_ref, total_ref, held_unit, feature_ref, send_ref, more_sems, up_held, down_held, sems = refs
    delta_in, slope_ref, up_ref, down_ref, unit_in, gain_ref, feature_in, send_in, *refs = refs
    mixed_ref, minor_ref, spectrum_ref, *sent_refs = refs
    chunk = pl.program_id(0)
    width = low_ref.shape[1]
    fetched = [(unit_in, held_unit), (feature_in, feature_ref), (send_in, send_ref)]

    @pl.when(chunk == 0)
    def _():
        copies = start_all([(delta_in, total_ref)], more_sems)
        if not near:
            for copy in weight_copies(layer, up_ref, down_ref, up_held, down_held, sems, 0):
                copy.start()
        wait_all(copies)
        low_ref[...] = total_ref[...].astype(LOW)
        minor_ref[...] = jnp.zeros_like(minor_ref)

    if near:
        at = chunk_of(chunk, width)
        up, down = up_ref[:, at], down_ref[at, :]
    else:
        next_weights(layer, (up_ref, down_ref, up_held, down_held, sems), chunk)
        up, down = up_held[chunk], down_held[chunk]

    @pl.when(chunk == 1)
    def _():
        start_all(fetched, more_sems.at[pl.ds(1, 3)])

    slope = (wide(low_ref[...], down, (1, 1)) * slope_ref[...].astype(HIGH)).astype(LOW)
    minor_ref[pl.ds(2 + chunk, 1), :] = jnp.sum(slope.astype(HIGH), 0, keepdims=True)
    total_ref[...] += wide(slope, up, (1, 1))

    @pl.when(chunk == pl.num_programs(0) - 1)
    def _():
        upstream = total_ref[...]
        wait_all(copies_of(fetched, more_sems.at[pl.ds(1, 3)]))
        unit, inverse = held_unit[:, :width], held_unit[:, width : width + 1]
        minor_ref[0:1, :] = jnp.sum(upstream * unit, 0, keepdims=True)
        minor_ref[1:2, :] = jnp.sum(upstream, 0, keepdims=True)
        mixed = norm_back(upstream, unit, inverse, gain_ref[layer, 0:1, :])
        mixed_ref[...] = mixed
        stage_one(mixed, feature_ref, send_ref, spectrum_ref, sent_refs)


def leave_kernel(types, got, *refs):
    got_refs, refs = refs[:got], refs[got:]
    at_ref, base_ref, marks_ref, mirror_ref, recv_ref, minor_ref, out, held, sems = refs
    upstream = base_ref[...] + marks_ref[:, :1] * stage_two(got_refs, mirror_ref, recv_ref)
    kind = marks_ref[:, 1:2]
    for t in range(types):
        minor_ref[t : t + 1, :] = jnp.sum(jnp.where(kind == float(t), upstream, 0.0), 0, keepdims=True)
    minor_ref[types:, :] = jnp.zeros_like(minor_ref[types:, :])
    blocks, rows, _ = held.shape
    for k, at in enumerate(turned(at_ref, blocks)):
        held[at] = upstream[k * rows : (k + 1) * rows]
    wait_all(start_all([(held, out)], sems))


def grads_kernel(plan, places, counts, *refs):
    starts_ref, refs = refs[0], refs[1:]
    normed_refs, refs = refs[: counts[0]], refs[counts[0] :]
    delta_refs, refs = refs[: counts[1]], refs[counts[1] :]
    up_in, bias_ref, down_in, *refs = refs
    *refs, normed_held, delta_held, up_ref, down_ref, normed_low, delta_low, hidden, back, sems, more_sems, out_sems = refs
    results, outs = refs[: len(refs) // 2], refs[len(refs) // 2 :]
    step = pl.program_id(0)
    blocks = len(plan)
    rows = normed_held.shape[1]
    units = up_ref.shape[0]
    piece = units // len(places)
    share = units // (pl.num_programs(0) - blocks)

    def copies(b):
        found = []
        for refs, held, parts in ((normed_refs, normed_held, plan[b][0]), (delta_refs, delta_held, plan[b][1])):
            at = 0
            for index, start, count in parts:
                source = refs[index]
                if start is not None:
                    source = source.at[pl.ds(pl.multiple_of(starts_ref[start], 8), count)]
                target = held.at[b % 2, at : at + count]
                found.append(pltpu.make_async_copy(source, target, sems.at[b, len(found)]))
                at += count
        return found

    def start(b):
        for copy in copies(b):
            copy.start()

    for b in range(blocks):

        @pl.when(step == b)
        def _():
            if b == 0:
                start(0)
                fetched = start_all([(up_in, up_ref), (down_in, down_ref)], more_sems)
            wait_all(copies(b))
            if b + 1 < blocks:
                start(b + 1)
            if b == 0:
                wait_all(fetched)
            at = slice(b * rows, (b + 1) * rows)
            normed = normed_held[b % 2].astype(LOW)
            delta = delta_held[b % 2].astype(LOW)
            normed_low[at] = normed
            delta_low[at] = delta
            value, slope = gelu_parts(wide(normed, up_ref[...], (1, 1)) + bias_ref[...])
            hidden[at] = value.astype(LOW)
            back[at] = (wide(delta, down_ref[...], (1, 1)) * slope).astype(LOW)

    def sent(c):
        found = []
        for p in range(c * share // piece, (c + 1) * share // piece):
            for h, (out, slot, first) in enumerate(places[p]):
                at = (slot, pl.ds(first, piece))
                found.append(pltpu.make_async_copy(outs[out].at[at], results[out].at[at], out_sems.at[p, h]))
        return found

    chunks = units // share
    for c in range(chunks):

        @pl.when(step == blocks + c)
        def _():
            at = slice(c * share, (c + 1) * share)
            both = (wide(back[:, at], normed_low[...], (0, 0)), wide(hidden[:, at], delta_low[...], (0, 0)))
            for p in range(c * share // piece, (c + 1) * share // piece):
                first_row = p * piece - c * share
                for (out, slot, first), a in zip(places[p], both):
                    outs[out][slot, first : first + piece] = a[first_row : first_row + piece]
            for copy in sent(c):
                copy.start()
            if c == chunks - 1:
                for k in range(chunks):
                    wait_all(sent(k))


def finish_kernel(layer, at_ref, *refs):
    *pieces, up_ref, down_ref, turned_ref = refs
    rows = pieces[0].shape[0] // 2
    for k, ref in enumerate(pieces[:4]):
        at = pl.multiple_of((at_ref[0] ^ k) * rows, 8)
        turned_ref[pl.ds(at, rows), :] = ref[:rows, :]
        down_ref[0, pl.ds(at, rows), :] = ref[rows:, :]
    up_ref[0] = turned_ref[...].T


def swap(values, axes, k):
    count = lax.axis_size(axes)
    return lax.ppermute(values, axes, [(i, i ^ k) for i in range(count)])


def exchange(blocks, axes, first=0):
    return [b if k == 0 else swap(b, axes, k) for k, b in enumerate(blocks, first)]


def sum_over(values, groups):
    for axes in groups:
        moved = [swap(values, axes, k) for k in range(1, lax.axis_size(axes))]
        values = sum(moved, values)
    return values


def local(inputs, segments, padding, type_table, ln_gain, ln_bias, up_weight, up_bias, down_weight, down_bias, out_grad):
    rows, part, width = inputs.shape
    layers, _, hidden_width = up_weight.shape
    types = type_table.shape[0]
    seq, count = lax.axis_size(SEQ), lax.axis_size(ROW)
    step = 2 * count
    units = part // step
    tokens = rows * part
    block = tokens // seq
    half = width // 2
    place = lax.axis_index(SEQ).reshape(1)

    feature = jnp.asarray(feature_table(width))
    mirror = jnp.asarray(mirror_table(half))
    tables = position_tables(count, part, seq)
    chunk = tables[0].shape[3] // (count - 1)
    sent_outs = [array(chunk, width)] * (count - 1)
    whole = array(tokens, width)
    kept = array(tokens, width + MARK)
    blocks_out = array(seq, block, width)
    minor_out = array(8, width)
    steps = hidden_width // width

    def spread(values, after):
        shaped = values.reshape(rows, units, step, width)
        out, token = call(functools.partial(spread_kernel, count), "spread", [shaped], [blocks_out], after, token=True)
        return lax.all_to_all(out, SEQ, 0, 0, tiled=True), token

    def collect(got, after):
        out = array(rows, units, step, width)
        *back, token = call(functools.partial(collect_kernel, count), "collect", [got], [out], after, token=True)
        return [b.reshape(inputs.shape) for b in back] + [token]

    weight_outs = [array(width, hidden_width, dtype=LOW), array(hidden_width, width, dtype=LOW)]

    def own(spectrum, carried, marks=None, after=(), token=False, layer=None):
        inputs = [spectrum, carried, mirror, block_t] + ([] if marks is None else [marks])
        kernel = functools.partial(own_kernel, marks is not None, layer)
        if layer is None:
            return call(kernel, "own_part", inputs, [whole], after, token=token)
        return call(
            kernel,
            "own_fetch",
            inputs + [up_weight, down_weight],
            [whole] + weight_outs,
            after,
            token=token,
            limit=8,
            in_specs=[VMEM] * len(inputs) + [HBM] * 2,
            out_specs=[VMEM, NEAR, NEAR],
            scratch_shapes=[pltpu.SemaphoreType.DMA((2, LANES))],
        )

    column = pl.BlockSpec((tokens, width), lambda c: (0, c))
    slope_out = array(tokens, hidden_width)
    scratch = [pltpu.VMEM((tokens, width), LOW), pltpu.VMEM((tokens, width), HIGH)]
    scratch += [pltpu.VMEM((steps, width, width), LOW)] * 2
    bias_spec = pl.BlockSpec((layers, width), lambda c: (0, c))

    held_kept = pltpu.VMEM(kept.shape, HIGH)
    dma = lambda n: pltpu.SemaphoreType.DMA((n, LANES))

    held_whole = pltpu.VMEM(whole.shape, HIGH)
    held_tables = [pltpu.VMEM(t, LOW) for t in (feature.shape, tables[0].shape[1:])]

    def mix(layer, got, base, after=()):
        inputs = got + [base, mirror, recv_t, ln_gain, ln_bias]
        return call(
            functools.partial(mix_kernel, layer, len(got)),
            "mix",
            inputs,
            [whole, kept],
            after,
            out_specs=[ANY, ANY] if layer == layers - 1 else [HBM, HBM],
            scratch_shapes=[held_whole, held_kept, dma(2)],
        )

    def feed(layer, normed, up, down, *more, after=(), token=False):
        last = layer == layers - 1
        inputs = [normed, up, up_bias, down, down_bias, ln_gain, ln_bias] + list(more)
        outs = [slope_out]
        outs += [minor_out, whole, blocks_out] if last else [whole, whole] + sent_outs + [kept]
        far = 2 if last else 1
        held = [pltpu.VMEM(blocks_out.shape, HIGH), held_whole] if last else [held_kept]
        fetches = [] if last else scratch[2:] + held_tables + [pltpu.SemaphoreType.DMA((2, steps))]
        weights = NEAR if last else HBM
        return call(
            functools.partial(feed_kernel, layer, last),
            "layer_feed" if last else "layer_forward",
            inputs,
            outs,
            after,
            near=last,
            token=token,
            grid=(steps,),
            in_specs=[ANY if last else HBM, weights, bias_spec, weights]
            + [VMEM] * 3
            + ([SMEM, VMEM] if last else [VMEM, HBM, HBM]),
            out_specs=[column] + [VMEM] * (len(outs) - 1 - far) + ([ANY, HBM] if last else [HBM]),
            scratch_shapes=held + scratch[:2] + fetches + [dma(3), dma(2)],
        )

    def backward(layer, delta, slope, up, down, kept, after=(), token=False):
        inputs = [delta, slope, up, down, kept, ln_gain, feature, send_t]
        outs = [whole, minor_out, whole] + sent_outs
        last = layer == layers - 1
        return call(
            functools.partial(backward_kernel, layer, last),
            "layer_backward" if last else "layer_stream",
            inputs,
            outs,
            after,
            near=last,
            token=token,
            grid=(steps,),
            in_specs=[ANY, column, NEAR, NEAR, ANY, VMEM, HBM, HBM]
            if last
            else [HBM, column, HBM, HBM, HBM, VMEM, HBM, HBM],
            out_specs=[VMEM] * len(outs),
            scratch_shapes=scratch[:2]
            + [held_kept]
            + held_tables
            + [dma(4)]
            + ([] if last else scratch[2:] + [pltpu.SemaphoreType.DMA((2, steps))]),
        )

    def delta(layer, got, base, marks, kept, after=()):
        inputs = got + [base, marks, mirror, recv_t, kept, ln_gain]
        return call(
            functools.partial(delta_kernel, layer, len(got)),
            "delta",
            inputs,
            [minor_out, whole],
            after,
            in_specs=[VMEM] * (len(got) + 4) + [HBM, VMEM],
            out_specs=[VMEM, HBM],
            scratch_shapes=[held_whole, held_kept, dma(1)],
        )

    columns = lax.axis_size("x")
    planes, shares = lax.axis_size(PLANES), lax.axis_size(SHARES)
    unit_block = hidden_width // seq
    piece = unit_block // shares
    x, dy, core, zh, zl = (lax.axis_index(a) for a in ("x", "dy", "core", "zh", "zl"))
    swapped = columns == 2

    def pair_pieces():
        nearby = [0, 1] if swapped else list(range(columns))
        own_x, own_dy, own_zh = (x, dy, zh) if swapped else (0, 0, 0)
        blocks = [((own_zh ^ b) * 2 + zl) * columns + (own_x ^ a) for a in nearby for b in (0, 1)]
        order = [(a * 2 + b, c) for a in nearby for c in (0, 1) for b in (0, 1)]
        return blocks, [(own_dy ^ c) * 2 + core for c in (0, 1)], order

    def plane_pieces():
        blocks = [z * columns + x for z in range(planes)]
        return blocks, [dy * 2 + (core ^ c) for c in (1, 0)], [(z, c) for c in (0, 1) for z in range(planes)]

    def bias_of(layer):
        blocks, shared, order = pair_pieces() if layer == layers - 1 else plane_pieces()
        starts = [blocks[b] * unit_block + shared[h] * piece for b, h in order]
        return jnp.concatenate([lax.dynamic_slice(up_bias, (layer, s), (1, piece)) for s in starts], 1)

    biases = [bias_of(layer) for layer in range(layers)]

    def cut(layer, after):
        blocks, shared, order = pair_pieces() if layer == layers - 1 else plane_pieces()
        starts = [blocks[b] * unit_block + shared[h] * piece for b, h in order]
        bias = biases[layer]
        if unit_block % 128:
            up = [lax.dynamic_slice_in_dim(up_weight[layer], s, piece, 1).T for s in starts]
            down = [lax.dynamic_slice_in_dim(down_weight[layer], s, piece, 0) for s in starts]
            return jnp.concatenate(up, 0), bias, jnp.concatenate(down, 0), bias
        out = array(piece * len(order), width, dtype=LOW)
        up, down, token = call(
            functools.partial(cut_kernel, layer, order, piece),
            "cut",
            [jnp.stack(blocks).astype(jnp.int32), jnp.stack(shared).astype(jnp.int32), up_weight, down_weight],
            [out, out],
            after,
            token=True,
            in_specs=[SMEM, SMEM, HBM, HBM],
            out_specs=[HBM, HBM],
            scratch_shapes=[
                pltpu.VMEM((len(blocks), width, unit_block), LOW),
                pltpu.VMEM(out.shape, LOW),
                pltpu.VMEM(out.shape, LOW),
                dma(len(blocks) + 1),
                pltpu.SemaphoreType.DMA((len(order),)),
            ],
        )
        return up, bias, down, token

    def weight_grads(normed, starts, deltas, plan, cuts, places, outs, after=()):
        size = sum(r for _, _, r in plan[0][0])
        chosen = cuts[0].shape[0]
        share = max(384 // piece, 1) * piece
        total = len(plan) * size
        plan = [(plan[b][0] + plan[b + 1][0], plan[b][1] + plan[b + 1][1]) for b in range(0, len(plan), 2)]
        size = 2 * size
        inputs = [jnp.stack(starts).astype(jnp.int32)] + normed + deltas + list(cuts[:3])
        return call(
            functools.partial(grads_kernel, plan, places, (len(normed), len(deltas))),
            "weight_grads",
            inputs,
            outs,
            after,
            token=True,
            limit=56,
            grid=(len(plan) + chosen // share,),
            in_specs=[SMEM] + [HBM] * (len(normed) + len(deltas)) + [HBM, VMEM, HBM],
            out_specs=[HBM] * len(outs),
            scratch_shapes=[pltpu.VMEM(o.shape, HIGH) for o in outs]
            + [pltpu.VMEM((2, size, width), HIGH)] * 2
            + [pltpu.VMEM(cuts[0].shape, LOW)] * 2
            + [pltpu.VMEM((total, width), LOW)] * 2
            + [pltpu.VMEM((total, chosen), LOW)] * 2
            + [pltpu.SemaphoreType.DMA((len(plan), 8)), dma(2), pltpu.SemaphoreType.DMA((len(places), 2))],
        )

    def shared_out(summed):
        along = swap(summed, "dy", 1)
        return [summed, swap(summed, "core", 1), along, swap(along, "core", 1)]

    def pair_grads(normed, deltas, cuts, after):
        plan = [([(b, None, tokens)], [(b, None, tokens)]) for b in range(4)]
        order = [(a, c, b) for a in range(columns) for c in (0, 1) for b in (0, 1)]
        if not swapped:
            places = [((0, p, 0), (0, p, piece)) for p in range(len(order))]
            out = array(len(order), 2 * piece, width)
            return weight_grads(normed, [0], deltas, plan, cuts, places, [out], after)
        places = [((a, 2 * c + b, 0), (2 + c, 2 * a + b, 0)) for a, c, b in order]
        return weight_grads(normed, [0], deltas, plan, cuts, places, [array(4, piece, width)] * 4, after)

    def pair_first(sums):
        if not swapped:
            return [lax.psum_scatter(sums[0], ("x", "dy", "zh"), scatter_dimension=0, tiled=True)], []
        up, up_far, down, down_far = sums
        got_up, got_down = swap(up_far, "x", 1), swap(down_far, "dy", 1)
        return [up[2:] + got_up[2:], down[2:] + got_down[2:]], [up[:2] + got_up[:2], down[:2] + got_down[:2]]

    def pair_step(far, near):
        if not swapped:
            return far, near
        got_up, got_down = swap(far[0], "dy", 1), swap(far[1], "x", 1)
        up, down = near
        far = jnp.concatenate([up[1] + got_up[1], down[1] + got_down[1]], 0)
        return [far], [jnp.concatenate([up[0] + got_up[0], down[0] + got_down[0]], 0)]

    def pair_last(far, near):
        if not swapped:
            summed = far[0].reshape(2 * piece, width)
            return lax.psum(summed, "do") if lax.axis_size("do") > 1 else summed
        return near[0] + swap(far[0], "zh", 1)

    def plane_first(values):
        if not swapped:
            return [lax.all_gather(values, ("dy", "x"), tiled=True)]
        return [swap(values, "x", 1), swap(values, "dy", 1)]

    def plane_rest(found):
        if not swapped:
            return []
        rows = tokens // 2
        return [swap(found[0][:rows], "dy", 1), swap(found[1][rows:], "x", 1)]

    def plane_grads(normed, deltas, cuts, after):
        group = lax.axis_size(("dy", "x"))
        out = array(planes, 2 * piece, width)
        places = [((h, z, 0), (h, z, piece)) for h in range(2) for z in range(planes)]
        rows = tokens // 2
        parts = [[(0, None, tokens)], [(1, None, tokens)], [(2, None, tokens)], [(3, None, rows), (4, None, rows)]]
        starts = [((dy ^ a) * columns + (x ^ b)) * tokens for a, b in ((0, 0), (0, 1), (1, 0), (1, 1))]
        if not swapped:
            parts = [[(0, b, tokens)] for b in range(group)]
            starts = [b * tokens for b in range(group)]
        starts = [jnp.asarray(s, jnp.int32) for s in starts]
        plan = [([(0, b, tokens)], parts[b]) for b in range(group)]
        return weight_grads([normed], starts, deltas, plan, cuts, places, [out, out], after)

    def plane_sum(both):
        summed = lax.psum_scatter(both.reshape(-1, width), PLANES, scatter_dimension=0, tiled=True)
        return lax.psum(summed, "do") if lax.axis_size("do") > 1 else summed

    def alone(stage, *operands):
        shapes = jax.eval_shape(stage, *operands)
        blank = lambda *_: jax.tree.map(lambda a: jnp.zeros(a.shape, a.dtype), shapes)
        return lax.cond(place[0] < 1000000, stage, blank, *operands)

    def send_and_own(sent, spectrum, mixed, marks):
        return exchange(sent, ROW, 1), own(spectrum, mixed, marks, token=True)

    held = call(
        functools.partial(spread_marked_kernel, count),
        "spread_marked",
        [place, inputs, segments, padding, type_table],
        [array(block, width + MARK)] * seq,
        in_specs=[SMEM] + [HBM] * 4,
        scratch_shapes=[pltpu.VMEM((rows, units, step, width + MARK), HIGH)]
        + [pltpu.VMEM(a.shape, a.dtype) for a in (inputs, segments, padding, type_table)]
        + [dma(4)],
    )
    held = exchange(held, SEQ)
    send_t, recv_t, block_t = call(
        pick_kernel,
        "pick",
        [place] + [jnp.asarray(t) for t in tables],
        [array(*t.shape[1:], dtype=LOW) for t in tables],
        held[1:4],
        in_specs=[SMEM] + [HBM] * 3,
        scratch_shapes=[dma(3)],
    )
    cuts = [None] * (layers - 1) + [cut(layers - 1, held[1:4])]
    carried, marks, spectrum, *sent = call(
        functools.partial(enter_kernel, seq),
        "enter",
        held + [feature, send_t],
        [whole, array(tokens, MARK), whole] + sent_outs,
        [cuts[-1][3]] + biases,
        in_specs=[VMEM] + [HBM] * (seq - 1) + [VMEM] * 2,
        scratch_shapes=[pltpu.VMEM((tokens, width + MARK), HIGH), dma(seq)],
    )
    upstream, made = spread(out_grad, sent[:1])
    saved = []
    for layer in range(layers - 1):
        got = exchange(sent, ROW, 1)
        base = own(spectrum, carried, after=[made])[0]
        normed, kept_one = mix(layer, got, base)
        all_normed = lax.all_gather(normed, ("dy", "x"), tiled=True)
        slope, carried, spectrum, *sent, kept_two = feed(layer, normed, up_weight, down_weight, marks, feature, send_t)
        saved.append((all_normed, kept_one, slope, kept_two))
    got = exchange(sent, ROW, 1)
    base, up, down = own(spectrum, carried, after=[upstream], layer=layers - 1)
    normed, kept_one = mix(layers - 1, got, base)

    def feed_stage(normed, kept, up, down, upstream):
        moved = swap(normed, "core", 1), swap(normed, "zl", 1)
        slope, minor_two, delta, outputs = feed(layers - 1, normed, up, down, place, upstream)
        return moved, minor_two, delta, outputs, backward(layers - 1, delta, slope, up, down, kept)

    moved_normed, minor_two, delta_two, outputs, (mixed, minor_one, spectrum, *sent) = alone(
        feed_stage, normed, kept_one, up, down, upstream
    )
    minors = [minor_two, minor_one]

    def send_and_swap(sent, spectrum, mixed, marks, normed_far, delta_two):
        got = exchange(sent, ROW, 1)
        return got, own(spectrum, mixed, marks)[0], swap(normed_far, "core", 1), swap(delta_two, "core", 1)

    got, base, *moved_delta = alone(send_and_swap, sent, spectrum, mixed, marks, moved_normed[1], delta_two)
    there, kept_one, slope, kept_two = saved[0]

    minor_two, delta_one = delta(0, got, base, marks, kept_two)

    def back_stage(delta_two, delta_one, kept_one, slope):
        cuts = cut(0, [delta_one])
        back = backward(0, delta_one, slope, up_weight, down_weight, kept_one, [cuts[3]])
        return swap(delta_two, "zl", 1), plane_first(delta_one), cuts, back

    delta_far, found, cuts[0], (mixed, minor_one, spectrum, *sent) = alone(
        back_stage, delta_two, delta_one, kept_one, slope
    )
    minors += [minor_two, minor_one]

    def grads_stage(normed, delta_two, delta_far, there, found, cuts, outputs):
        found = ([delta_one] if swapped else []) + found + plane_rest(found)
        deltas = delta_two + [delta_far, swap(delta_far, "core", 1)]
        outputs = lax.all_to_all(outputs, SEQ, 0, 0, tiled=True)
        *sums, token = pair_grads(normed, deltas, cuts[1], [])
        return plane_grads(there, found, cuts[0], [token])[:2], sums, outputs

    parts, sums, outputs = alone(
        grads_stage,
        [normed, moved_normed[0], moved_normed[1], moved_delta[0]],
        [delta_two, moved_delta[1]],
        delta_far,
        there,
        found,
        cuts,
        outputs,
    )

    both = parts[1] + swap(parts[0], "core", 1)
    whole_sum = plane_sum(both)

    def first_stage(sums, sent, spectrum, mixed, marks):
        return pair_first(sums), exchange(sent, ROW, 1), own(spectrum, mixed, marks)[0]

    (far, near), got, base = alone(first_stage, sums, sent, spectrum, mixed, marks)

    def middle_stage(far, near, outputs, minors, got, base, marks):
        minor_table, blocks = call(
            functools.partial(leave_kernel, types, len(got)),
            "leave",
            got + [place, base, marks, mirror, recv_t],
            [minor_out, blocks_out],
            out_specs=[VMEM, HBM],
            scratch_shapes=[pltpu.VMEM(blocks_out.shape, HIGH), dma(1)],
        )
        minor = sum_over(jnp.concatenate(minors + [minor_table], 0), [("core",)])
        return pair_step(far, near), minor, collect(outputs, [])[0], blocks

    (far, near), minor, outputs, blocks = alone(middle_stage, far, near, outputs, minors, got, base, marks)

    share = lax.axis_index(SHARES).reshape(1)
    outs = [array(layers, width, unit_block), array(layers, unit_block, width)]

    def finish(layer, pieces, grads):
        return call(
            functools.partial(finish_kernel, layer),
            "finish",
            [share] + pieces + grads,
            outs,
            in_specs=[SMEM] + [VMEM] * len(pieces) + [ANY] * len(grads),
            out_specs=[
                pl.BlockSpec((1,) + o.shape[1:], functools.partial(lambda l, i: (l, 0, 0), layer)) for o in outs
            ],
            grid=(1,),
            input_output_aliases={5: 0, 6: 1} if grads else {},
            scratch_shapes=[pltpu.VMEM((unit_block, width), HIGH)],
        )

    def last_stage(far, near, minor, whole_sum):
        return pair_last(far, near), sum_over(minor, [("dy", "x"), ("do",)]), shared_out(whole_sum)[1:]

    summed, minor, shared = alone(last_stage, far, near, minor, whole_sum)
    grads = finish(0, [whole_sum] + shared, [])

    pieces = shared_out(summed)
    blocks = lax.all_to_all(hold(blocks, [summed]), SEQ, 0, 0, tiled=True)
    minor = sum_over(minor, [PLANES])
    input_grad, _ = collect(blocks, [])
    up_grad, down_grad = finish(1, pieces, grads)
    ends = [minor[16 * (layers - 1 - l) :][:16] for l in range(layers)]
    table_grad = minor[16 * layers :][:types]
    gain_grad = jnp.stack([jnp.stack([e[8], e[0]]) for e in ends])
    shift_grad = jnp.stack([jnp.stack([e[9], e[1]]) for e in ends])
    down_vec = jnp.stack([e[2] for e in ends])
    up_vec = jnp.stack([e[10 : 10 + steps].reshape(-1) for e in ends])
    up_vec = lax.dynamic_slice_in_dim(up_vec, place[0] * unit_block, unit_block, 1)

    return outputs, input_grad, table_grad, gain_grad, shift_grad, up_grad, up_vec, down_grad, down_vec


def solution(mesh):
    dp, seq = mesh.shape["dp"], mesh.shape["seq"]
    shape = (dp // 4, 2, 2, 2, 2, seq // 4)
    finer = Mesh(mesh.devices.reshape(shape), ALL)
    in_specs = (P(DP, SEQ, None), P(DP, SEQ), P(DP, SEQ)) + (P(),) * 7 + (P(DP, SEQ, None),)
    out_specs = (
        P(DP, SEQ, None),
        P(DP, SEQ, None),
        P(),
        P(),
        P(),
        P(None, None, SEQ),
        P(None, SEQ),
        P(None, SEQ, None),
        P(),
    )
    return jax.shard_map(local, mesh=finer, in_specs=in_specs, out_specs=out_specs, check_vma=False)
```

```python
import functools
import math

import jax
import jax.numpy as jnp
import ml_dtypes
import numpy as np
from jax import lax
from jax.experimental import pallas as pl
from jax.experimental.pallas import tpu as pltpu
from jax.sharding import Mesh
from jax.sharding import PartitionSpec as P

EPSILON = 1e-05
DP = ("do", "dy", "core")
SEQ = ("zh", "zl", "x")
ROW = ("zl", "x")
PLANES = ("zh", "zl")
SHARES = ("dy", "core")
PLANE = ("dy", "core", "x")
ALL = DP + SEQ
MARK = 128
LOW = jnp.bfloat16
HIGH = jnp.float32
VMEM = pl.BlockSpec(memory_space=pltpu.VMEM)
NEAR = pl.BlockSpec(memory_space=pltpu.VMEM)
SMEM = pl.BlockSpec(memory_space=pltpu.SMEM)
ANY = pl.BlockSpec(memory_space=pl.ANY)
HBM = pl.BlockSpec(memory_space=pltpu.HBM)


MICROSECONDS = {
    "spread_marked": 2.0,
    "pick": 1.5,
    "cut": 5.9,
    "enter": 1.7,
    "spread": 1.0,
    "own_part": 1.5,
    "own_fetch": 5.5,
    "mix": 2.2,
    "layer_forward": 12.0,
    "layer_backward": 7.5,
    "layer_feed": 7.5,
    "layer_stream": 12.0,
    "delta": 2.8,
    "weight_grads": 3.0,
    "leave": 0.9,
    "collect": 2.2,
    "finish": 3.3,
}


def split_table(values):
    head = values.astype(ml_dtypes.bfloat16)
    return np.stack([head, (values - head.astype(np.float64)).astype(ml_dtypes.bfloat16)])


def feature_table(width):
    half = width // 2
    angle = np.outer(np.arange(width), np.arange(width)) % width * (2.0 * math.pi / width)
    cos, sin = np.cos(angle) / math.sqrt(width), np.sin(angle) / math.sqrt(width)
    return split_table(np.concatenate([cos[:, :half], cos[:, half : half + 1], sin[:, 1:half]], 1))


def mirror_table(half):
    table = np.zeros((half, half), ml_dtypes.bfloat16)
    table[half - np.arange(1, half), np.arange(1, half)] = 1.0
    return table


def pair_of(count, at):
    return at, 2 * count - at if at else count


def owned(count, part, seq, at):
    first, second = pair_of(count, at)
    pos = np.arange(seq * part).reshape(seq, part // (2 * count), 2 * count)
    return np.stack([pos[:, :, first], pos[:, :, second]], 1).reshape(-1)


def position_tables(count, part, seq):
    length = seq * part
    step = 2 * count
    span = length // step
    keep = span // step
    w = 2.0 * math.pi / length
    own = [owned(count, part, seq, i) for i in range(count)]
    local = length // count
    send = np.zeros((2, count, count, 2 * keep, local))
    recv = np.zeros((2, count, count, local, 2 * keep))
    block = np.zeros((2, count, local, local))
    scale = 1.0 / math.sqrt(length)

    def kept(i):
        if i:
            return [(i + step * s, 2) for s in range(keep)]
        ends = [(step * s, 1 if s in (0, keep // 2) else 2) for s in range(keep // 2 + 1)]
        return ends + [(count + step * s, 2) for s in range(keep // 2)]

    for j in range(count):
        n = own[j]
        first = n % step == j
        theta = 2.0 * math.pi * j / step
        for i in range(count):
            if i == j:
                angle = w * (np.outer(n, n) % length)
                block[0, i], block[1, i] = np.cos(angle) * scale, np.sin(angle) * scale
                continue
            at = 0
            slots = {}
            for kap, kinds in kept(i):
                cos, sin = np.cos(w * (kap * n % length)), np.sin(w * (kap * n % length))
                if j:
                    sign = np.where(first, 1.0, -1.0)
                    rows = (cos, sign * sin, sign * cos, sin)
                else:
                    rows = (cos * first, cos * ~first, sin * first, sin * ~first)
                if kinds == 2:
                    send[0, j, i, at], send[0, j, i, at + 1] = rows[:2]
                    send[1, j, i, at], send[1, j, i, at + 1] = rows[2:]
                    slots[kap] = (at, at + 1, 0.0)
                else:
                    phi = w * (kap * j % length)
                    send[0, j, i, at] = math.cos(phi) * rows[0] + math.sin(phi) * rows[1]
                    send[1, j, i, at] = math.cos(phi) * rows[2] + math.sin(phi) * rows[3]
                    slots[kap] = (at, at, phi)
                at += kinds
            for index, k in enumerate(own[i]):
                kap, turn = k % span, k // span
                mirrored = kap not in slots
                p_at, q_at, phi = slots[(span - kap) % span if mirrored else kap]
                pair = np.zeros((2, 2 * keep))
                if p_at == q_at:
                    pair[0, p_at], pair[1, p_at] = math.cos(phi), math.sin(phi)
                else:
                    pair[0, p_at], pair[1, q_at] = 1.0, 1.0
                even, odd = pair, pair
                if j:
                    if mirrored:
                        c, s = math.cos(theta), math.sin(theta)
                        even = odd = np.stack([c * pair[0] + s * pair[1], s * pair[0] - c * pair[1]])
                    c, s = math.cos(theta * turn), math.sin(theta * turn)
                    recv[0, i, j, index] = c * even[0] - s * even[1]
                    recv[1, i, j, index] = s * odd[0] + c * odd[1]
                else:
                    flip = (-1.0) ** turn
                    if mirrored:
                        even, odd = pair * np.array([[1.0], [-1.0]]), pair * np.array([[-1.0], [1.0]])
                    recv[0, i, j, index] = even[0] + flip * even[1]
                    recv[1, i, j, index] = odd[0] + flip * odd[1]
    recv = recv * scale
    sends, recvs, blocks = [], [], []
    for at in range(seq):
        i = at % count
        order = np.arange(local).reshape(seq, -1)[[at ^ k for k in range(seq)]].reshape(-1)
        others = [i ^ k for k in range(1, count)]
        sends.append(send[:, i, others].reshape(2, -1, local)[:, :, order])
        cos = np.concatenate([recv[0, i, j] for j in others], 1)[order]
        sin = np.concatenate([recv[1, i, j] for j in others], 1)[order]
        recvs.append(np.stack([np.concatenate([cos, -sin], 1), np.concatenate([cos, sin], 1)]))
        cos, sin = (block[h, i][order][:, order] for h in range(2))
        blocks.append(np.stack([np.concatenate([cos, -sin], 1), np.concatenate([cos, sin], 1)]))
    return tuple(np.moveaxis(split_table(np.stack(t)), 0, 1) for t in (sends, recvs, blocks))


def wide(left, right, contract=(1, 0)):
    return lax.dot_general(left, right, ((contract[:1], contract[1:]), ((), ())), preferred_element_type=HIGH)


def split(values):
    head = values.astype(LOW)
    return head, (values - head.astype(HIGH)).astype(LOW)


def triple(left, right):
    return wide(left[0], right[0]) + wide(left[0], right[1]) + wide(left[1], right[0])


def first_lane(values):
    return lax.broadcasted_iota(jnp.int32, values.shape, 1) == 0


def mean(values):
    return jnp.mean(values, axis=-1, keepdims=True)


def normalize(values):
    centered = values - mean(values)
    inverse = lax.rsqrt(mean(centered * centered) + EPSILON)
    return centered * inverse, inverse


def norm_back(upstream, unit, inverse, gain):
    scaled = upstream * gain
    return inverse * (scaled - mean(scaled) - unit * mean(scaled * unit))


def gelu_parts(p):
    c = math.sqrt(2.0 / math.pi)
    square = p * p
    t = jnp.tanh(p * (c + 0.044715 * c * square))
    halves = 0.5 + 0.5 * t
    slope = halves + p * (0.5 - 0.5 * (t * t)) * (c + 3.0 * 0.044715 * c * square)
    return p * halves, slope


def stage_one(values, feature_ref, send_ref, spectrum_ref, sent_refs):
    half = values.shape[1] // 2
    parts = split(values)
    spectrum = triple(parts, (feature_ref[0], feature_ref[1]))
    spectrum_ref[...] = spectrum
    head, tail = split(spectrum)
    lanes = half + 128
    even = triple((send_ref[0, 0], send_ref[1, 0]), (head[:, :lanes], tail[:, :lanes]))
    odd = triple((send_ref[0, 1], send_ref[1, 1]), (head[:, half:], tail[:, half:]))
    middle = jnp.where(first_lane(even[:, half:]), even[:, half:], odd[:, :128])
    rows = sent_refs[0].shape[0]
    for k, ref in enumerate(sent_refs):
        at = slice(k * rows, (k + 1) * rows)
        ref[:, :half] = even[at, :half]
        ref[:, half:lanes] = middle[at]
        ref[:, lanes:] = odd[at, 128:]


def unpack(packed, mirror, table_ref):
    half = packed.shape[1] // 2
    head, tail = split(packed)

    def stack(part):
        low, high = part[:, :half], part[:, half:]
        back = wide(jnp.concatenate([low, high], 0), mirror).astype(LOW)
        count = low.shape[0]
        turned = back[:count]
        middle = jnp.where(first_lane(turned[:, :128]), high[:, :128].astype(HIGH), turned[:, :128].astype(HIGH))
        turned = jnp.concatenate([middle.astype(LOW), turned[:, 128:]], 1)
        edge = jnp.where(first_lane(high[:, :128]), 0.0, high[:, :128].astype(HIGH)).astype(LOW)
        high = jnp.concatenate([edge, high[:, 128:]], 1)
        return jnp.concatenate([low, high], 0), jnp.concatenate([turned, back[count:]], 0)

    head_pair, tail_pair = stack(head), stack(tail)
    sides = [
        triple((table_ref[0, side], table_ref[1, side]), (head_pair[side], tail_pair[side])) for side in range(2)
    ]
    return jnp.concatenate(sides, 1)


def stage_two(got_refs, mirror_ref, recv_ref):
    got = jnp.concatenate([ref[...] for ref in got_refs], 0)
    return unpack(got, mirror_ref[...], recv_ref)


def call(kernel, name, inputs, outs, after=(), limit=24, token=False, near=False, **more):
    count, end = len(after), len(after) + len(inputs) + len(outs)

    def body(*refs):
        if token:
            kernel(*refs[count:end], *refs[end + 1 :])
            refs[end][...] = jnp.zeros_like(refs[end])
        else:
            kernel(*refs[count:])

    in_specs = more.pop("in_specs", None)
    if in_specs is None:
        in_specs = [SMEM if a.dtype == jnp.int32 and len(a.shape) == 1 else VMEM for a in inputs]
    out_specs = list(more.pop("out_specs", [VMEM] * len(outs)))
    far = lambda s: s is HBM or s.block_shape is not None and not near
    place = lambda s: pltpu.HBM if far(s) else pltpu.VMEM if s is NEAR else None
    inputs = [pltpu.with_memory_space_constraint(a, place(s)) if place(s) else a for a, s in zip(inputs, in_specs)]
    out_shape = [place(s)(o.shape, o.dtype) if place(s) else o for o, s in zip(outs, out_specs)]
    results = pl.pallas_call(
        body,
        in_specs=[ANY] * count + list(in_specs),
        out_specs=out_specs + [VMEM] * token,
        out_shape=out_shape + [array(8, 128)] * token,
        compiler_params=pltpu.CompilerParams(vmem_limit_bytes=limit * 2**20),
        cost_estimate=pl.CostEstimate(flops=int(MICROSECONDS[name] * 3.45e+09), bytes_accessed=0, transcendentals=0),
        name=name,
        **more,
    )(*after, *inputs)
    return list(results)


def hold(values, after):
    count = len(after)
    after = [pltpu.with_memory_space_constraint(a, pltpu.HBM) if math.prod(a.shape) > 8192 else a for a in after]
    return pl.pallas_call(
        lambda *refs: None,
        in_specs=[ANY] * (count + 1),
        out_specs=ANY,
        out_shape=array(*values.shape),
        input_output_aliases={count: 0},
        compiler_params=pltpu.CompilerParams(vmem_limit_bytes=2**20),
        name="hold",
    )(*after, values)


def array(*shape, dtype=HIGH):
    return jax.ShapeDtypeStruct(shape, dtype)


def pick_kernel(at_ref, *refs):
    *refs, sems = refs
    half = len(refs) // 2
    wait_all(start_all([(source.at[at_ref[0]], target) for source, target in zip(refs[:half], refs[half:])], sems))


def cut_kernel(layer, order, piece, blocks_ref, shares_ref, up_ref, down_ref, up_out, down_out, held, chosen_up, chosen_down, sems, down_sems):
    count, _, block = held.shape
    copies = []
    for b in range(count):
        start = pl.multiple_of(blocks_ref[b] * block, 128)
        copies.append(start_all([(up_ref.at[layer, :, pl.ds(start, block)], held.at[b])], sems.at[pl.ds(b, 1)]))
    downs = []
    for p, (b, h) in enumerate(order):
        start = pl.multiple_of(blocks_ref[b] * block + shares_ref[h] * piece, 16)
        target = chosen_down.at[p * piece : (p + 1) * piece]
        downs.append(pltpu.make_async_copy(down_ref.at[layer, pl.ds(start, piece), :], target, down_sems.at[p]))
        downs[-1].start()
    row = lax.broadcasted_iota(jnp.int32, (piece, block), 0)
    lane = lax.broadcasted_iota(jnp.int32, (piece, block), 1)
    chosen = [(lane == row + share * piece).astype(HIGH).astype(LOW) for share in (shares_ref[0], shares_ref[1])]
    wait_all(downs)
    outs = start_all([(chosen_down, down_out)], sems.at[pl.ds(count, 1)])
    for b in range(count):
        wait_all(copies[b])
        for p, (of, h) in enumerate(order):
            if of == b:
                chosen_up[p * piece : (p + 1) * piece] = wide(chosen[h], held[b], (1, 1)).astype(LOW)
    wait_all(outs + start_all([(chosen_up, up_out)], sems.at[pl.ds(0, 1)]))


def class_rows(count, dest):
    row, i = dest // count, dest % count
    if isinstance(dest, int):
        return row, pair_of(count, i)
    return row, (i, jnp.where(i == 0, count, 2 * count - i))


def spread_marked_kernel(count, at_ref, *rest):
    sources, (*outs, held), targets, sems = rest[:4], rest[4:-5], rest[-5:-1], rest[-1]
    wait_all(start_all(zip(sources, targets), sems))
    values_ref, segments_ref, padding_ref, table_ref = targets
    rows, part, width = values_ref.shape
    units = part // (2 * count)
    flags = jnp.concatenate([padding_ref[...], segments_ref[...], jnp.zeros((8 - 2 * rows, part), jnp.int32)], 0)
    flags = flags.astype(HIGH).astype(LOW)
    at = lax.broadcasted_iota(jnp.int32, (8, MARK), 0)
    lane = lax.broadcasted_iota(jnp.int32, (8, MARK), 1)
    for row in range(rows):
        pick = ((at == row) & (lane == 0)) | ((at == rows + row) & (lane == 1))
        marks = wide(flags, pick.astype(HIGH).astype(LOW), (0, 0))
        kind = marks[:, 1:2]
        values = values_ref[row]
        for t in range(table_ref.shape[0]):
            values = values + jnp.where(kind == float(t), table_ref[t : t + 1, :], 0.0)
        held[row, :, :, :width] = values.reshape(units, 2 * count, width)
        held[row, :, :, width:] = marks.reshape(units, 2 * count, MARK)
    for k, out in enumerate(outs):
        row, classes = class_rows(count, at_ref[0] ^ k)
        for h, at in enumerate(classes):
            out[h * units : (h + 1) * units, :] = held[row, :, at, :]


def spread_kernel(count, values_ref, out):
    rows, units, step, width = values_ref.shape
    for dest in range(rows * count):
        row, classes = class_rows(count, dest)
        for h, at in enumerate(classes):
            out[dest, h * units : (h + 1) * units, :] = values_ref[row, :, at, :]


def collect_kernel(count, blocks, *outs):
    rows, units, step, width = outs[0].shape
    part = blocks.shape[1] // len(outs)
    for source in range(rows * count):
        row, classes = class_rows(count, source)
        for n, out in enumerate(outs):
            for h, at in enumerate(classes):
                first = n * part + h * units
                out[row, :, at, :] = blocks[source, first : first + units, :]


def turned(at_ref, blocks):
    return [at_ref[0] ^ k for k in range(blocks)]


def enter_kernel(blocks, *refs):
    sources = refs[:blocks]
    feature_ref, send_ref, carried_ref, marks_ref, spectrum_ref, *sent_refs, held, sems = refs[blocks:]
    width = carried_ref.shape[1]
    rows = held.shape[0] // blocks
    wait_all(start_all([(ref, held.at[k * rows : (k + 1) * rows]) for k, ref in enumerate(sources)], sems))
    values = held[:, :width]
    carried_ref[...] = values
    marks_ref[...] = held[:, width:]
    stage_one(values * held[:, width : width + 1], feature_ref, send_ref, spectrum_ref, sent_refs)


def own_kernel(masked, layer, *refs):
    if layer is not None:
        *refs, up_in, down_in, out_ref, up_out, down_out, sems = refs
        copies = start_all([(up_in.at[layer], up_out), (down_in.at[layer], down_out)], sems)
    else:
        *refs, out_ref = refs
        copies = []
    spectrum_ref, carried_ref, mirror_ref, block_ref, *marks = refs
    mixed = unpack(spectrum_ref[...], mirror_ref[...], block_ref)
    if masked:
        mixed = mixed * marks[0][:, :1]
    out_ref[...] = carried_ref[...] + mixed
    wait_all(copies)


LANES = 4


def copies_of(pairs, sems):
    found = []
    for k, (source, target) in enumerate(pairs):
        rows = source.shape[0]
        parts = LANES if rows % (16 * LANES) == 0 else 1
        for part in range(parts):
            at = pl.ds(part * (rows // parts), rows // parts)
            found.append(pltpu.make_async_copy(source.at[at], target.at[at], sems.at[k, part]))
    return found


def start_all(pairs, sems):
    copies = copies_of(pairs, sems)
    for copy in copies:
        copy.start()
    return copies


def wait_all(copies):
    for copy in copies:
        copy.wait()


def keep(unit, inverse, held):
    width = unit.shape[1]
    held[:, :width] = unit
    held[:, width:] = jnp.broadcast_to(inverse, (unit.shape[0], held.shape[1] - width))


def weight_copies(layer, up_ref, down_ref, up_held, down_held, sems, chunk):
    width = up_held.shape[1]
    at = pl.ds(pl.multiple_of(chunk * width, 128), width)
    return (
        pltpu.make_async_copy(up_ref.at[layer, :, at], up_held.at[chunk], sems.at[0, chunk]),
        pltpu.make_async_copy(down_ref.at[layer, at, :], down_held.at[chunk], sems.at[1, chunk]),
    )


def next_weights(layer, refs, chunk):
    wait_all(weight_copies(layer, *refs, chunk))

    @pl.when(chunk + 1 < pl.num_programs(0))
    def _():
        for copy in weight_copies(layer, *refs, chunk + 1):
            copy.start()


def mix_kernel(layer, got, *refs):
    got_refs, refs = refs[:got], refs[got:]
    base_ref, mirror_ref, recv_ref, gain_ref, shift_ref, normed_out, unit_out, held_normed, held, sems = refs
    mixed = base_ref[...] + stage_two(got_refs, mirror_ref, recv_ref)
    unit, inverse = normalize(mixed)
    held_normed[...] = unit * gain_ref[layer, 0:1, :] + shift_ref[layer, 0:1, :]
    copies = start_all([(held_normed, normed_out)], sems)
    keep(unit, inverse, held)
    wait_all(copies + start_all([(held, unit_out)], sems.at[pl.ds(1, 1)]))


def chunk_of(chunk, width):
    return pl.ds(pl.multiple_of(chunk * width, 128), width)


def feed_kernel(layer, last, *refs):
    if last:
        *refs, held, delta_ref, low_ref, total_ref, more_sems, out_sems = refs
    else:
        *refs, held, low_ref, total_ref, up_held, down_held, feature_ref, send_ref, sems, more_sems, out_sems = refs
    normed_in, up_ref, up_bias_ref, down_ref, down_bias_ref, gain_ref, shift_ref, *refs = refs
    chunk = pl.program_id(0)
    width = low_ref.shape[1]
    if last:
        at_ref, upstream_ref, slope_ref, minor_ref, delta_far, carried_out = refs
        fetched = [(normed_in, total_ref)]
    else:
        marks_ref, feature_in, send_in, slope_ref, carried_ref, spectrum_ref, *sent_refs, unit_out = refs
        fetched = [(normed_in, total_ref), (feature_in, feature_ref), (send_in, send_ref)]
        weights = (up_ref, down_ref, up_held, down_held, sems)

    @pl.when(chunk == 0)
    def _():
        copies = start_all(fetched[:1], more_sems)
        if not last:
            for copy in weight_copies(layer, *weights, 0):
                copy.start()
        wait_all(copies)
        normed = total_ref[...]
        low_ref[...] = normed.astype(LOW)
        total_ref[...] = normed + down_bias_ref[layer : layer + 1, :]

    if last:
        at = chunk_of(chunk, width)
        up, down = up_ref[:, at], down_ref[at, :]
    else:
        next_weights(layer, weights, chunk)
        up, down = up_held[chunk], down_held[chunk]

        @pl.when(chunk == 1)
        def _():
            start_all(fetched[1:], more_sems.at[pl.ds(1, 2)])

    preact = wide(low_ref[...], up) + up_bias_ref[layer : layer + 1, :]
    value, slope = gelu_parts(preact)
    slope_ref[...] = slope.astype(slope_ref.dtype)
    total_ref[...] += wide(value.astype(LOW), down)

    @pl.when(chunk == pl.num_programs(0) - 1)
    def _():
        unit, inverse = normalize(total_ref[...])
        gain = gain_ref[layer, 1:2, :]
        carried = unit * gain + shift_ref[layer, 1:2, :]
        if last:
            blocks, rows, _ = upstream_ref.shape
            order = turned(at_ref, blocks)
            upstream = jnp.concatenate([upstream_ref[at] for at in order], 0)
            delta_out(upstream, unit, inverse, gain, delta_ref, minor_ref)
            copies = start_all([(delta_ref, delta_far)], out_sems)
            for k, at in enumerate(order):
                held[at] = carried[k * rows : (k + 1) * rows]
            wait_all(copies + start_all([(held, carried_out)], out_sems.at[pl.ds(1, 1)]))
        else:
            keep(unit, inverse, held)
            copies = start_all([(held, unit_out)], out_sems)
            carried_ref[...] = carried
            wait_all(copies_of(fetched[1:], more_sems.at[pl.ds(1, 2)]))
            stage_one(carried * marks_ref[:, :1], feature_ref, send_ref, spectrum_ref, sent_refs)
            wait_all(copies)


def delta_out(upstream, unit, inverse, gain, delta_ref, minor_ref):
    delta = norm_back(upstream, unit, inverse, gain)
    delta_ref[...] = delta
    rows = [upstream * unit, upstream, delta.astype(LOW).astype(HIGH)]
    for at, value in enumerate(rows):
        minor_ref[at : at + 1, :] = jnp.sum(value, 0, keepdims=True)
    minor_ref[len(rows) :, :] = jnp.zeros_like(minor_ref[len(rows) :, :])


def delta_kernel(layer, got, *refs):
    got_refs, refs = refs[:got], refs[got:]
    base_ref, marks_ref, mirror_ref, recv_ref, unit_in, gain_ref, minor_ref, delta_far, delta_ref, held, sems = refs
    copies = start_all([(unit_in, held)], sems)
    upstream = base_ref[...] + marks_ref[:, :1] * stage_two(got_refs, mirror_ref, recv_ref)
    wait_all(copies)
    width = upstream.shape[1]
    unit, inverse = held[:, :width], held[:, width : width + 1]
    delta_out(upstream, unit, inverse, gain_ref[layer, 1:2, :], delta_ref, minor_ref)
    wait_all(start_all([(delta_ref, delta_far)], sems))


def backward_kernel(layer, near, *refs):
    if near:
        *refs, low_ref, total_ref, held_unit, feature_ref, send_ref, more_sems = refs
    else:
        *refs, low_ref, total_ref, held_unit, feature_ref, send_ref, more_sems, up_held, down_held, sems = refs
    delta_in, slope_ref, up_ref, down_ref, unit_in, gain_ref, feature_in, send_in, *refs = refs
    mixed_ref, minor_ref, spectrum_ref, *sent_refs = refs
    chunk = pl.program_id(0)
    width = low_ref.shape[1]
    fetched = [(unit_in, held_unit), (feature_in, feature_ref), (send_in, send_ref)]

    @pl.when(chunk == 0)
    def _():
        copies = start_all([(delta_in, total_ref)], more_sems)
        if not near:
            for copy in weight_copies(layer, up_ref, down_ref, up_held, down_held, sems, 0):
                copy.start()
        wait_all(copies)
        low_ref[...] = total_ref[...].astype(LOW)
        minor_ref[...] = jnp.zeros_like(minor_ref)

    if near:
        at = chunk_of(chunk, width)
        up, down = up_ref[:, at], down_ref[at, :]
    else:
        next_weights(layer, (up_ref, down_ref, up_held, down_held, sems), chunk)
        up, down = up_held[chunk], down_held[chunk]

    @pl.when(chunk == 1)
    def _():
        start_all(fetched, more_sems.at[pl.ds(1, 3)])

    slope = (wide(low_ref[...], down, (1, 1)) * slope_ref[...].astype(HIGH)).astype(LOW)
    minor_ref[pl.ds(2 + chunk, 1), :] = jnp.sum(slope.astype(HIGH), 0, keepdims=True)
    total_ref[...] += wide(slope, up, (1, 1))

    @pl.when(chunk == pl.num_programs(0) - 1)
    def _():
        upstream = total_ref[...]
        wait_all(copies_of(fetched, more_sems.at[pl.ds(1, 3)]))
        unit, inverse = held_unit[:, :width], held_unit[:, width : width + 1]
        minor_ref[0:1, :] = jnp.sum(upstream * unit, 0, keepdims=True)
        minor_ref[1:2, :] = jnp.sum(upstream, 0, keepdims=True)
        mixed = norm_back(upstream, unit, inverse, gain_ref[layer, 0:1, :])
        mixed_ref[...] = mixed
        stage_one(mixed, feature_ref, send_ref, spectrum_ref, sent_refs)


def leave_kernel(types, got, *refs):
    got_refs, refs = refs[:got], refs[got:]
    at_ref, base_ref, marks_ref, mirror_ref, recv_ref, minor_ref, out, held, sems = refs
    upstream = base_ref[...] + marks_ref[:, :1] * stage_two(got_refs, mirror_ref, recv_ref)
    kind = marks_ref[:, 1:2]
    for t in range(types):
        minor_ref[t : t + 1, :] = jnp.sum(jnp.where(kind == float(t), upstream, 0.0), 0, keepdims=True)
    minor_ref[types:, :] = jnp.zeros_like(minor_ref[types:, :])
    blocks, rows, _ = held.shape
    for k, at in enumerate(turned(at_ref, blocks)):
        held[at] = upstream[k * rows : (k + 1) * rows]
    wait_all(start_all([(held, out)], sems))


def grads_kernel(plan, places, counts, *refs):
    starts_ref, refs = refs[0], refs[1:]
    normed_refs, refs = refs[: counts[0]], refs[counts[0] :]
    delta_refs, refs = refs[: counts[1]], refs[counts[1] :]
    up_in, bias_ref, down_in, *refs = refs
    *refs, normed_held, delta_held, up_ref, down_ref, normed_low, delta_low, hidden, back, sems, more_sems, out_sems = refs
    results, outs = refs[: len(refs) // 2], refs[len(refs) // 2 :]
    step = pl.program_id(0)
    blocks = len(plan)
    rows = normed_held.shape[1]
    units = up_ref.shape[0]
    piece = units // len(places)
    share = units // (pl.num_programs(0) - blocks)

    def copies(b):
        found = []
        for refs, held, parts in ((normed_refs, normed_held, plan[b][0]), (delta_refs, delta_held, plan[b][1])):
            at = 0
            for index, start, count in parts:
                source = refs[index]
                if start is not None:
                    source = source.at[pl.ds(pl.multiple_of(starts_ref[start], 8), count)]
                target = held.at[b % 2, at : at + count]
                found.append(pltpu.make_async_copy(source, target, sems.at[b, len(found)]))
                at += count
        return found

    def start(b):
        for copy in copies(b):
            copy.start()

    for b in range(blocks):

        @pl.when(step == b)
        def _():
            if b == 0:
                start(0)
                fetched = start_all([(up_in, up_ref), (down_in, down_ref)], more_sems)
            wait_all(copies(b))
            if b + 1 < blocks:
                start(b + 1)
            if b == 0:
                wait_all(fetched)
            at = slice(b * rows, (b + 1) * rows)
            normed = normed_held[b % 2].astype(LOW)
            delta = delta_held[b % 2].astype(LOW)
            normed_low[at] = normed
            delta_low[at] = delta
            value, slope = gelu_parts(wide(normed, up_ref[...], (1, 1)) + bias_ref[...])
            hidden[at] = value.astype(LOW)
            back[at] = (wide(delta, down_ref[...], (1, 1)) * slope).astype(LOW)

    def sent(c):
        found = []
        for p in range(c * share // piece, (c + 1) * share // piece):
            for h, (out, slot, first) in enumerate(places[p]):
                at = (slot, pl.ds(first, piece))
                found.append(pltpu.make_async_copy(outs[out].at[at], results[out].at[at], out_sems.at[p, h]))
        return found

    chunks = units // share
    for c in range(chunks):

        @pl.when(step == blocks + c)
        def _():
            at = slice(c * share, (c + 1) * share)
            both = (wide(back[:, at], normed_low[...], (0, 0)), wide(hidden[:, at], delta_low[...], (0, 0)))
            for p in range(c * share // piece, (c + 1) * share // piece):
                first_row = p * piece - c * share
                for (out, slot, first), a in zip(places[p], both):
                    outs[out][slot, first : first + piece] = a[first_row : first_row + piece]
            for copy in sent(c):
                copy.start()
            if c == chunks - 1:
                for k in range(chunks):
                    wait_all(sent(k))


def finish_kernel(layer, at_ref, *refs):
    *pieces, up_ref, down_ref, turned_ref = refs
    rows = pieces[0].shape[0] // 2
    for k, ref in enumerate(pieces[:4]):
        at = pl.multiple_of((at_ref[0] ^ k) * rows, 8)
        turned_ref[pl.ds(at, rows), :] = ref[:rows, :]
        down_ref[0, pl.ds(at, rows), :] = ref[rows:, :]
    up_ref[0] = turned_ref[...].T


def swap(values, axes, k):
    count = lax.axis_size(axes)
    return lax.ppermute(values, axes, [(i, i ^ k) for i in range(count)])


def exchange(blocks, axes, first=0):
    return [b if k == 0 else swap(b, axes, k) for k, b in enumerate(blocks, first)]


def sum_over(values, groups):
    for axes in groups:
        moved = [swap(values, axes, k) for k in range(1, lax.axis_size(axes))]
        values = sum(moved, values)
    return values


def local(inputs, segments, padding, type_table, ln_gain, ln_bias, up_weight, up_bias, down_weight, down_bias, out_grad):
    rows, part, width = inputs.shape
    layers, _, hidden_width = up_weight.shape
    types = type_table.shape[0]
    seq, count = lax.axis_size(SEQ), lax.axis_size(ROW)
    step = 2 * count
    units = part // step
    tokens = rows * part
    block = tokens // seq
    half = width // 2
    place = lax.axis_index(SEQ).reshape(1)

    feature = jnp.asarray(feature_table(width))
    mirror = jnp.asarray(mirror_table(half))
    tables = position_tables(count, part, seq)
    chunk = tables[0].shape[3] // (count - 1)
    sent_outs = [array(chunk, width)] * (count - 1)
    whole = array(tokens, width)
    kept = array(tokens, width + MARK)
    blocks_out = array(seq, block, width)
    minor_out = array(8, width)
    steps = hidden_width // width

    def spread(values, after):
        shaped = values.reshape(rows, units, step, width)
        out, token = call(functools.partial(spread_kernel, count), "spread", [shaped], [blocks_out], after, token=True)
        return lax.all_to_all(out, SEQ, 0, 0, tiled=True), token

    def collect(got, after):
        out = array(rows, units, step, width)
        *back, token = call(functools.partial(collect_kernel, count), "collect", [got], [out], after, token=True)
        return [b.reshape(inputs.shape) for b in back] + [token]

    weight_outs = [array(width, hidden_width, dtype=LOW), array(hidden_width, width, dtype=LOW)]

    def own(spectrum, carried, marks=None, after=(), token=False, layer=None):
        inputs = [spectrum, carried, mirror, block_t] + ([] if marks is None else [marks])
        kernel = functools.partial(own_kernel, marks is not None, layer)
        if layer is None:
            return call(kernel, "own_part", inputs, [whole], after, token=token)
        return call(
            kernel,
            "own_fetch",
            inputs + [up_weight, down_weight],
            [whole] + weight_outs,
            after,
            token=token,
            limit=8,
            in_specs=[VMEM] * len(inputs) + [HBM] * 2,
            out_specs=[VMEM, NEAR, NEAR],
            scratch_shapes=[pltpu.SemaphoreType.DMA((2, LANES))],
        )

    column = pl.BlockSpec((tokens, width), lambda c: (0, c))
    slope_out = array(tokens, hidden_width)
    scratch = [pltpu.VMEM((tokens, width), LOW), pltpu.VMEM((tokens, width), HIGH)]
    scratch += [pltpu.VMEM((steps, width, width), LOW)] * 2
    bias_spec = pl.BlockSpec((layers, width), lambda c: (0, c))

    held_kept = pltpu.VMEM(kept.shape, HIGH)
    dma = lambda n: pltpu.SemaphoreType.DMA((n, LANES))

    held_whole = pltpu.VMEM(whole.shape, HIGH)
    held_tables = [pltpu.VMEM(t, LOW) for t in (feature.shape, tables[0].shape[1:])]

    def mix(layer, got, base, after=()):
        inputs = got + [base, mirror, recv_t, ln_gain, ln_bias]
        return call(
            functools.partial(mix_kernel, layer, len(got)),
            "mix",
            inputs,
            [whole, kept],
            after,
            out_specs=[ANY, ANY] if layer == layers - 1 else [HBM, HBM],
            scratch_shapes=[held_whole, held_kept, dma(2)],
        )

    def feed(layer, normed, up, down, *more, after=(), token=False):
        last = layer == layers - 1
        inputs = [normed, up, up_bias, down, down_bias, ln_gain, ln_bias] + list(more)
        outs = [slope_out]
        outs += [minor_out, whole, blocks_out] if last else [whole, whole] + sent_outs + [kept]
        far = 2 if last else 1
        held = [pltpu.VMEM(blocks_out.shape, HIGH), held_whole] if last else [held_kept]
        fetches = [] if last else scratch[2:] + held_tables + [pltpu.SemaphoreType.DMA((2, steps))]
        weights = NEAR if last else HBM
        return call(
            functools.partial(feed_kernel, layer, last),
            "layer_feed" if last else "layer_forward",
            inputs,
            outs,
            after,
            near=last,
            token=token,
            grid=(steps,),
            in_specs=[ANY if last else HBM, weights, bias_spec, weights]
            + [VMEM] * 3
            + ([SMEM, VMEM] if last else [VMEM, HBM, HBM]),
            out_specs=[column] + [VMEM] * (len(outs) - 1 - far) + ([ANY, HBM] if last else [HBM]),
            scratch_shapes=held + scratch[:2] + fetches + [dma(3), dma(2)],
        )

    def backward(layer, delta, slope, up, down, kept, after=(), token=False):
        inputs = [delta, slope, up, down, kept, ln_gain, feature, send_t]
        outs = [whole, minor_out, whole] + sent_outs
        last = layer == layers - 1
        return call(
            functools.partial(backward_kernel, layer, last),
            "layer_backward" if last else "layer_stream",
            inputs,
            outs,
            after,
            near=last,
            token=token,
            grid=(steps,),
            in_specs=[ANY, column, NEAR, NEAR, ANY, VMEM, HBM, HBM]
            if last
            else [HBM, column, HBM, HBM, HBM, VMEM, HBM, HBM],
            out_specs=[VMEM] * len(outs),
            scratch_shapes=scratch[:2]
            + [held_kept]
            + held_tables
            + [dma(4)]
            + ([] if last else scratch[2:] + [pltpu.SemaphoreType.DMA((2, steps))]),
        )

    def delta(layer, got, base, marks, kept, after=()):
        inputs = got + [base, marks, mirror, recv_t, kept, ln_gain]
        return call(
            functools.partial(delta_kernel, layer, len(got)),
            "delta",
            inputs,
            [minor_out, whole],
            after,
            in_specs=[VMEM] * (len(got) + 4) + [HBM, VMEM],
            out_specs=[VMEM, HBM],
            scratch_shapes=[held_whole, held_kept, dma(1)],
        )

    columns = lax.axis_size("x")
    planes, shares = lax.axis_size(PLANES), lax.axis_size(SHARES)
    unit_block = hidden_width // seq
    piece = unit_block // shares
    x, dy, core, zh, zl = (lax.axis_index(a) for a in ("x", "dy", "core", "zh", "zl"))
    swapped = columns == 2

    def pair_pieces():
        nearby = [0, 1] if swapped else list(range(columns))
        own_x, own_dy, own_zh = (x, dy, zh) if swapped else (0, 0, 0)
        blocks = [((own_zh ^ b) * 2 + zl) * columns + (own_x ^ a) for a in nearby for b in (0, 1)]
        order = [(a * 2 + b, c) for a in nearby for c in (0, 1) for b in (0, 1)]
        return blocks, [(own_dy ^ c) * 2 + core for c in (0, 1)], order

    def plane_pieces():
        blocks = [z * columns + x for z in range(planes)]
        return blocks, [dy * 2 + (core ^ c) for c in (1, 0)], [(z, c) for c in (0, 1) for z in range(planes)]

    def bias_of(layer):
        blocks, shared, order = pair_pieces() if layer == layers - 1 else plane_pieces()
        starts = [blocks[b] * unit_block + shared[h] * piece for b, h in order]
        return jnp.concatenate([lax.dynamic_slice(up_bias, (layer, s), (1, piece)) for s in starts], 1)

    biases = [bias_of(layer) for layer in range(layers)]

    def cut(layer, after):
        blocks, shared, order = pair_pieces() if layer == layers - 1 else plane_pieces()
        starts = [blocks[b] * unit_block + shared[h] * piece for b, h in order]
        bias = biases[layer]
        if unit_block % 128:
            up = [lax.dynamic_slice_in_dim(up_weight[layer], s, piece, 1).T for s in starts]
            down = [lax.dynamic_slice_in_dim(down_weight[layer], s, piece, 0) for s in starts]
            return jnp.concatenate(up, 0), bias, jnp.concatenate(down, 0), bias
        out = array(piece * len(order), width, dtype=LOW)
        up, down, token = call(
            functools.partial(cut_kernel, layer, order, piece),
            "cut",
            [jnp.stack(blocks).astype(jnp.int32), jnp.stack(shared).astype(jnp.int32), up_weight, down_weight],
            [out, out],
            after,
            token=True,
            in_specs=[SMEM, SMEM, HBM, HBM],
            out_specs=[HBM, HBM],
            scratch_shapes=[
                pltpu.VMEM((len(blocks), width, unit_block), LOW),
                pltpu.VMEM(out.shape, LOW),
                pltpu.VMEM(out.shape, LOW),
                dma(len(blocks) + 1),
                pltpu.SemaphoreType.DMA((len(order),)),
            ],
        )
        return up, bias, down, token

    def weight_grads(normed, starts, deltas, plan, cuts, places, outs, after=()):
        size = sum(r for _, _, r in plan[0][0])
        chosen = cuts[0].shape[0]
        share = max(384 // piece, 1) * piece
        total = len(plan) * size
        plan = [(plan[b][0] + plan[b + 1][0], plan[b][1] + plan[b + 1][1]) for b in range(0, len(plan), 2)]
        size = 2 * size
        inputs = [jnp.stack(starts).astype(jnp.int32)] + normed + deltas + list(cuts[:3])
        return call(
            functools.partial(grads_kernel, plan, places, (len(normed), len(deltas))),
            "weight_grads",
            inputs,
            outs,
            after,
            token=True,
            limit=56,
            grid=(len(plan) + chosen // share,),
            in_specs=[SMEM] + [HBM] * (len(normed) + len(deltas)) + [HBM, VMEM, HBM],
            out_specs=[HBM] * len(outs),
            scratch_shapes=[pltpu.VMEM(o.shape, HIGH) for o in outs]
            + [pltpu.VMEM((2, size, width), HIGH)] * 2
            + [pltpu.VMEM(cuts[0].shape, LOW)] * 2
            + [pltpu.VMEM((total, width), LOW)] * 2
            + [pltpu.VMEM((total, chosen), LOW)] * 2
            + [pltpu.SemaphoreType.DMA((len(plan), 8)), dma(2), pltpu.SemaphoreType.DMA((len(places), 2))],
        )

    def shared_out(summed):
        along = swap(summed, "dy", 1)
        return [summed, swap(summed, "core", 1), along, swap(along, "core", 1)]

    def pair_grads(normed, deltas, cuts, after):
        plan = [([(b, None, tokens)], [(b, None, tokens)]) for b in range(4)]
        order = [(a, c, b) for a in range(columns) for c in (0, 1) for b in (0, 1)]
        if not swapped:
            places = [((0, p, 0), (0, p, piece)) for p in range(len(order))]
            out = array(len(order), 2 * piece, width)
            return weight_grads(normed, [0], deltas, plan, cuts, places, [out], after)
        places = [((a, 2 * c + b, 0), (2 + c, 2 * a + b, 0)) for a, c, b in order]
        return weight_grads(normed, [0], deltas, plan, cuts, places, [array(4, piece, width)] * 4, after)

    def pair_first(sums):
        if not swapped:
            return [lax.psum_scatter(sums[0], ("x", "dy", "zh"), scatter_dimension=0, tiled=True)], []
        up, up_far, down, down_far = sums
        got_up, got_down = swap(up_far, "x", 1), swap(down_far, "dy", 1)
        return [up[2:] + got_up[2:], down[2:] + got_down[2:]], [up[:2] + got_up[:2], down[:2] + got_down[:2]]

    def pair_step(far, near):
        if not swapped:
            return far, near
        got_up, got_down = swap(far[0], "dy", 1), swap(far[1], "x", 1)
        up, down = near
        far = jnp.concatenate([up[1] + got_up[1], down[1] + got_down[1]], 0)
        return [far], [jnp.concatenate([up[0] + got_up[0], down[0] + got_down[0]], 0)]

    def pair_last(far, near):
        if not swapped:
            summed = far[0].reshape(2 * piece, width)
            return lax.psum(summed, "do") if lax.axis_size("do") > 1 else summed
        return near[0] + swap(far[0], "zh", 1)

    def plane_first(values):
        if not swapped:
            return [lax.all_gather(values, ("dy", "x"), tiled=True)]
        return [swap(values, "x", 1), swap(values, "dy", 1)]

    def plane_rest(found):
        if not swapped:
            return []
        rows = tokens // 2
        return [swap(found[0][:rows], "dy", 1), swap(found[1][rows:], "x", 1)]

    def plane_grads(normed, deltas, cuts, after):
        group = lax.axis_size(("dy", "x"))
        out = array(planes, 2 * piece, width)
        places = [((h, z, 0), (h, z, piece)) for h in range(2) for z in range(planes)]
        rows = tokens // 2
        parts = [[(0, None, tokens)], [(1, None, tokens)], [(2, None, tokens)], [(3, None, rows), (4, None, rows)]]
        starts = [((dy ^ a) * columns + (x ^ b)) * tokens for a, b in ((0, 0), (0, 1), (1, 0), (1, 1))]
        if not swapped:
            parts = [[(0, b, tokens)] for b in range(group)]
            starts = [b * tokens for b in range(group)]
        starts = [jnp.asarray(s, jnp.int32) for s in starts]
        plan = [([(0, b, tokens)], parts[b]) for b in range(group)]
        return weight_grads([normed], starts, deltas, plan, cuts, places, [out, out], after)

    def plane_sum(both):
        summed = lax.psum_scatter(both.reshape(-1, width), PLANES, scatter_dimension=0, tiled=True)
        return lax.psum(summed, "do") if lax.axis_size("do") > 1 else summed

    def alone(stage, *operands):
        shapes = jax.eval_shape(stage, *operands)
        blank = lambda *_: jax.tree.map(lambda a: jnp.zeros(a.shape, a.dtype), shapes)
        return lax.cond(place[0] < 1000000, stage, blank, *operands)

    def send_and_own(sent, spectrum, mixed, marks):
        return exchange(sent, ROW, 1), own(spectrum, mixed, marks, token=True)

    held = call(
        functools.partial(spread_marked_kernel, count),
        "spread_marked",
        [place, inputs, segments, padding, type_table],
        [array(block, width + MARK)] * seq,
        in_specs=[SMEM] + [HBM] * 4,
        scratch_shapes=[pltpu.VMEM((rows, units, step, width + MARK), HIGH)]
        + [pltpu.VMEM(a.shape, a.dtype) for a in (inputs, segments, padding, type_table)]
        + [dma(4)],
    )
    held = exchange(held, SEQ)
    send_t, recv_t, block_t = call(
        pick_kernel,
        "pick",
        [place] + [jnp.asarray(t) for t in tables],
        [array(*t.shape[1:], dtype=LOW) for t in tables],
        held[1:4],
        in_specs=[SMEM] + [HBM] * 3,
        scratch_shapes=[dma(3)],
    )
    cuts = [None] * (layers - 1) + [cut(layers - 1, held[1:4])]
    carried, marks, spectrum, *sent = call(
        functools.partial(enter_kernel, seq),
        "enter",
        held + [feature, send_t],
        [whole, array(tokens, MARK), whole] + sent_outs,
        [cuts[-1][3]] + biases,
        in_specs=[VMEM] + [HBM] * (seq - 1) + [VMEM] * 2,
        scratch_shapes=[pltpu.VMEM((tokens, width + MARK), HIGH), dma(seq)],
    )
    upstream, made = spread(out_grad, sent[:1])
    saved = []
    for layer in range(layers - 1):
        got = exchange(sent, ROW, 1)
        base = own(spectrum, carried, after=[made])[0]
        normed, kept_one = mix(layer, got, base)
        all_normed = lax.all_gather(normed, ("dy", "x"), tiled=True)
        slope, carried, spectrum, *sent, kept_two = feed(layer, normed, up_weight, down_weight, marks, feature, send_t)
        saved.append((all_normed, kept_one, slope, kept_two))
    got = exchange(sent, ROW, 1)
    base, up, down = own(spectrum, carried, after=[upstream], layer=layers - 1)
    normed, kept_one = mix(layers - 1, got, base)

    def feed_stage(normed, kept, up, down, upstream):
        moved = swap(normed, "core", 1), swap(normed, "zl", 1)
        slope, minor_two, delta, outputs = feed(layers - 1, normed, up, down, place, upstream)
        return moved, minor_two, delta, outputs, backward(layers - 1, delta, slope, up, down, kept)

    moved_normed, minor_two, delta_two, outputs, (mixed, minor_one, spectrum, *sent) = alone(
        feed_stage, normed, kept_one, up, down, upstream
    )
    minors = [minor_two, minor_one]

    def send_and_swap(sent, spectrum, mixed, marks, normed_far, delta_two):
        got = exchange(sent, ROW, 1)
        return got, own(spectrum, mixed, marks)[0], swap(normed_far, "core", 1), swap(delta_two, "core", 1)

    got, base, *moved_delta = alone(send_and_swap, sent, spectrum, mixed, marks, moved_normed[1], delta_two)
    there, kept_one, slope, kept_two = saved[0]

    minor_two, delta_one = delta(0, got, base, marks, kept_two)

    def back_stage(delta_two, delta_one, kept_one, slope):
        cuts = cut(0, [delta_one])
        back = backward(0, delta_one, slope, up_weight, down_weight, kept_one, [cuts[3]])
        return swap(delta_two, "zl", 1), plane_first(delta_one), cuts, back

    delta_far, found, cuts[0], (mixed, minor_one, spectrum, *sent) = alone(
        back_stage, delta_two, delta_one, kept_one, slope
    )
    minors += [minor_two, minor_one]

    def grads_stage(normed, delta_two, delta_far, there, found, cuts, outputs):
        found = ([delta_one] if swapped else []) + found + plane_rest(found)
        deltas = delta_two + [delta_far, swap(delta_far, "core", 1)]
        outputs = lax.all_to_all(outputs, SEQ, 0, 0, tiled=True)
        *sums, token = pair_grads(normed, deltas, cuts[1], [])
        return plane_grads(there, found, cuts[0], [token])[:2], sums, outputs

    parts, sums, outputs = alone(
        grads_stage,
        [normed, moved_normed[0], moved_normed[1], moved_delta[0]],
        [delta_two, moved_delta[1]],
        delta_far,
        there,
        found,
        cuts,
        outputs,
    )

    both = parts[1] + swap(parts[0], "core", 1)
    whole_sum = plane_sum(both)

    def first_stage(sums, sent, spectrum, mixed, marks):
        return pair_first(sums), exchange(sent, ROW, 1), own(spectrum, mixed, marks)[0]

    (far, near), got, base = alone(first_stage, sums, sent, spectrum, mixed, marks)

    def middle_stage(far, near, outputs, minors, got, base, marks):
        minor_table, blocks = call(
            functools.partial(leave_kernel, types, len(got)),
            "leave",
            got + [place, base, marks, mirror, recv_t],
            [minor_out, blocks_out],
            out_specs=[VMEM, HBM],
            scratch_shapes=[pltpu.VMEM(blocks_out.shape, HIGH), dma(1)],
        )
        minor = sum_over(jnp.concatenate(minors + [minor_table], 0), [("core",)])
        return pair_step(far, near), minor, collect(outputs, [])[0], blocks

    (far, near), minor, outputs, blocks = alone(middle_stage, far, near, outputs, minors, got, base, marks)

    share = lax.axis_index(SHARES).reshape(1)
    outs = [array(layers, width, unit_block), array(layers, unit_block, width)]

    def finish(layer, pieces, grads):
        return call(
            functools.partial(finish_kernel, layer),
            "finish",
            [share] + pieces + grads,
            outs,
            in_specs=[SMEM] + [VMEM] * len(pieces) + [ANY] * len(grads),
            out_specs=[
                pl.BlockSpec((1,) + o.shape[1:], functools.partial(lambda l, i: (l, 0, 0), layer)) for o in outs
            ],
            grid=(1,),
            input_output_aliases={5: 0, 6: 1} if grads else {},
            scratch_shapes=[pltpu.VMEM((unit_block, width), HIGH)],
        )

    def last_stage(far, near, minor, whole_sum):
        return pair_last(far, near), sum_over(minor, [("dy", "x"), ("do",)]), shared_out(whole_sum)[1:]

    summed, minor, shared = alone(last_stage, far, near, minor, whole_sum)
    grads = finish(0, [whole_sum] + shared, [])

    pieces = shared_out(summed)
    blocks = lax.all_to_all(hold(blocks, [summed]), SEQ, 0, 0, tiled=True)
    minor = sum_over(minor, [PLANES])
    input_grad, _ = collect(blocks, [])
    up_grad, down_grad = finish(1, pieces, grads)
    ends = [minor[16 * (layers - 1 - l) :][:16] for l in range(layers)]
    table_grad = minor[16 * layers :][:types]
    gain_grad = jnp.stack([jnp.stack([e[8], e[0]]) for e in ends])
    shift_grad = jnp.stack([jnp.stack([e[9], e[1]]) for e in ends])
    down_vec = jnp.stack([e[2] for e in ends])
    up_vec = jnp.stack([e[10 : 10 + steps].reshape(-1) for e in ends])
    up_vec = lax.dynamic_slice_in_dim(up_vec, place[0] * unit_block, unit_block, 1)

    return outputs, input_grad, table_grad, gain_grad, shift_grad, up_grad, up_vec, down_grad, down_vec


def solution(mesh):
    dp, seq = mesh.shape["dp"], mesh.shape["seq"]
    shape = (dp // 4, 2, 2, 2, 2, seq // 4)
    finer = Mesh(mesh.devices.reshape(shape), ALL)
    in_specs = (P(DP, SEQ, None), P(DP, SEQ), P(DP, SEQ)) + (P(),) * 7 + (P(DP, SEQ, None),)
    out_specs = (
        P(DP, SEQ, None),
        P(DP, SEQ, None),
        P(),
        P(),
        P(),
        P(None, None, SEQ),
        P(None, SEQ),
        P(None, SEQ, None),
        P(),
    )
    return jax.shard_map(local, mesh=finer, in_specs=in_specs, out_specs=out_specs, check_vma=False)
```

```python
import functools
import math

import jax
import jax.numpy as jnp
import ml_dtypes
import numpy as np
from jax import lax
from jax.experimental import pallas as pl
from jax.experimental.pallas import tpu as pltpu
from jax.sharding import Mesh
from jax.sharding import PartitionSpec as P

EPSILON = 1e-05
DP = ("do", "dy", "core")
SEQ = ("zh", "zl", "x")
ROW = ("zl", "x")
PLANES = ("zh", "zl")
SHARES = ("dy", "core")
PLANE = ("dy", "core", "x")
ALL = DP + SEQ
MARK = 128
LOW = jnp.bfloat16
HIGH = jnp.float32
VMEM = pl.BlockSpec(memory_space=pltpu.VMEM)
NEAR = pl.BlockSpec(memory_space=pltpu.VMEM)
SMEM = pl.BlockSpec(memory_space=pltpu.SMEM)
ANY = pl.BlockSpec(memory_space=pl.ANY)
HBM = pl.BlockSpec(memory_space=pltpu.HBM)


MICROSECONDS = {
    "spread_marked": 2.0,
    "pick": 1.5,
    "cut": 5.9,
    "enter": 1.7,
    "spread": 1.0,
    "own_part": 1.5,
    "own_fetch": 5.5,
    "mix": 2.2,
    "layer_forward": 12.0,
    "layer_backward": 7.5,
    "layer_feed": 7.5,
    "layer_stream": 12.0,
    "delta": 2.8,
    "weight_grads": 3.0,
    "leave": 0.9,
    "collect": 2.2,
    "finish": 3.3,
}


def split_table(values):
    head = values.astype(ml_dtypes.bfloat16)
    return np.stack([head, (values - head.astype(np.float64)).astype(ml_dtypes.bfloat16)])


def feature_table(width):
    half = width // 2
    angle = np.outer(np.arange(width), np.arange(width)) % width * (2.0 * math.pi / width)
    cos, sin = np.cos(angle) / math.sqrt(width), np.sin(angle) / math.sqrt(width)
    return split_table(np.concatenate([cos[:, :half], cos[:, half : half + 1], sin[:, 1:half]], 1))


def mirror_table(half):
    table = np.zeros((half, half), ml_dtypes.bfloat16)
    table[half - np.arange(1, half), np.arange(1, half)] = 1.0
    return table


def pair_of(count, at):
    return at, 2 * count - at if at else count


def owned(count, part, seq, at):
    first, second = pair_of(count, at)
    pos = np.arange(seq * part).reshape(seq, part // (2 * count), 2 * count)
    return np.stack([pos[:, :, first], pos[:, :, second]], 1).reshape(-1)


def position_tables(count, part, seq):
    length = seq * part
    step = 2 * count
    span = length // step
    keep = span // step
    w = 2.0 * math.pi / length
    own = [owned(count, part, seq, i) for i in range(count)]
    local = length // count
    send = np.zeros((2, count, count, 2 * keep, local))
    recv = np.zeros((2, count, count, local, 2 * keep))
    block = np.zeros((2, count, local, local))
    scale = 1.0 / math.sqrt(length)

    def kept(i):
        if i:
            return [(i + step * s, 2) for s in range(keep)]
        ends = [(step * s, 1 if s in (0, keep // 2) else 2) for s in range(keep // 2 + 1)]
        return ends + [(count + step * s, 2) for s in range(keep // 2)]

    for j in range(count):
        n = own[j]
        first = n % step == j
        theta = 2.0 * math.pi * j / step
        for i in range(count):
            if i == j:
                angle = w * (np.outer(n, n) % length)
                block[0, i], block[1, i] = np.cos(angle) * scale, np.sin(angle) * scale
                continue
            at = 0
            slots = {}
            for kap, kinds in kept(i):
                cos, sin = np.cos(w * (kap * n % length)), np.sin(w * (kap * n % length))
                if j:
                    sign = np.where(first, 1.0, -1.0)
                    rows = (cos, sign * sin, sign * cos, sin)
                else:
                    rows = (cos * first, cos * ~first, sin * first, sin * ~first)
                if kinds == 2:
                    send[0, j, i, at], send[0, j, i, at + 1] = rows[:2]
                    send[1, j, i, at], send[1, j, i, at + 1] = rows[2:]
                    slots[kap] = (at, at + 1, 0.0)
                else:
                    phi = w * (kap * j % length)
                    send[0, j, i, at] = math.cos(phi) * rows[0] + math.sin(phi) * rows[1]
                    send[1, j, i, at] = math.cos(phi) * rows[2] + math.sin(phi) * rows[3]
                    slots[kap] = (at, at, phi)
                at += kinds
            for index, k in enumerate(own[i]):
                kap, turn = k % span, k // span
                mirrored = kap not in slots
                p_at, q_at, phi = slots[(span - kap) % span if mirrored else kap]
                pair = np.zeros((2, 2 * keep))
                if p_at == q_at:
                    pair[0, p_at], pair[1, p_at] = math.cos(phi), math.sin(phi)
                else:
                    pair[0, p_at], pair[1, q_at] = 1.0, 1.0
                even, odd = pair, pair
                if j:
                    if mirrored:
                        c, s = math.cos(theta), math.sin(theta)
                        even = odd = np.stack([c * pair[0] + s * pair[1], s * pair[0] - c * pair[1]])
                    c, s = math.cos(theta * turn), math.sin(theta * turn)
                    recv[0, i, j, index] = c * even[0] - s * even[1]
                    recv[1, i, j, index] = s * odd[0] + c * odd[1]
                else:
                    flip = (-1.0) ** turn
                    if mirrored:
                        even, odd = pair * np.array([[1.0], [-1.0]]), pair * np.array([[-1.0], [1.0]])
                    recv[0, i, j, index] = even[0] + flip * even[1]
                    recv[1, i, j, index] = odd[0] + flip * odd[1]
    recv = recv * scale
    sends, recvs, blocks = [], [], []
    for at in range(seq):
        i = at % count
        order = np.arange(local).reshape(seq, -1)[[at ^ k for k in range(seq)]].reshape(-1)
        others = [i ^ k for k in range(1, count)]
        sends.append(send[:, i, others].reshape(2, -1, local)[:, :, order])
        cos = np.concatenate([recv[0, i, j] for j in others], 1)[order]
        sin = np.concatenate([recv[1, i, j] for j in others], 1)[order]
        recvs.append(np.stack([np.concatenate([cos, -sin], 1), np.concatenate([cos, sin], 1)]))
        cos, sin = (block[h, i][order][:, order] for h in range(2))
        blocks.append(np.stack([np.concatenate([cos, -sin], 1), np.concatenate([cos, sin], 1)]))
    return tuple(np.moveaxis(split_table(np.stack(t)), 0, 1) for t in (sends, recvs, blocks))


def wide(left, right, contract=(1, 0)):
    return lax.dot_general(left, right, ((contract[:1], contract[1:]), ((), ())), preferred_element_type=HIGH)


def split(values):
    head = values.astype(LOW)
    return head, (values - head.astype(HIGH)).astype(LOW)


def triple(left, right):
    return wide(left[0], right[0]) + wide(left[0], right[1]) + wide(left[1], right[0])


def first_lane(values):
    return lax.broadcasted_iota(jnp.int32, values.shape, 1) == 0


def mean(values):
    return jnp.mean(values, axis=-1, keepdims=True)


def normalize(values):
    centered = values - mean(values)
    inverse = lax.rsqrt(mean(centered * centered) + EPSILON)
    return centered * inverse, inverse


def norm_back(upstream, unit, inverse, gain):
    scaled = upstream * gain
    return inverse * (scaled - mean(scaled) - unit * mean(scaled * unit))


def gelu_parts(p):
    c = math.sqrt(2.0 / math.pi)
    square = p * p
    t = jnp.tanh(p * (c + 0.044715 * c * square))
    halves = 0.5 + 0.5 * t
    slope = halves + p * (0.5 - 0.5 * (t * t)) * (c + 3.0 * 0.044715 * c * square)
    return p * halves, slope


def stage_one(values, feature_ref, send_ref, spectrum_ref, sent_refs):
    half = values.shape[1] // 2
    parts = split(values)
    spectrum = triple(parts, (feature_ref[0], feature_ref[1]))
    spectrum_ref[...] = spectrum
    head, tail = split(spectrum)
    lanes = half + 128
    even = triple((send_ref[0, 0], send_ref[1, 0]), (head[:, :lanes], tail[:, :lanes]))
    odd = triple((send_ref[0, 1], send_ref[1, 1]), (head[:, half:], tail[:, half:]))
    middle = jnp.where(first_lane(even[:, half:]), even[:, half:], odd[:, :128])
    rows = sent_refs[0].shape[0]
    for k, ref in enumerate(sent_refs):
        at = slice(k * rows, (k + 1) * rows)
        ref[:, :half] = even[at, :half]
        ref[:, half:lanes] = middle[at]
        ref[:, lanes:] = odd[at, 128:]


def unpack(packed, mirror, table_ref):
    half = packed.shape[1] // 2
    head, tail = split(packed)

    def stack(part):
        low, high = part[:, :half], part[:, half:]
        back = wide(jnp.concatenate([low, high], 0), mirror).astype(LOW)
        count = low.shape[0]
        turned = back[:count]
        middle = jnp.where(first_lane(turned[:, :128]), high[:, :128].astype(HIGH), turned[:, :128].astype(HIGH))
        turned = jnp.concatenate([middle.astype(LOW), turned[:, 128:]], 1)
        edge = jnp.where(first_lane(high[:, :128]), 0.0, high[:, :128].astype(HIGH)).astype(LOW)
        high = jnp.concatenate([edge, high[:, 128:]], 1)
        return jnp.concatenate([low, high], 0), jnp.concatenate([turned, back[count:]], 0)

    head_pair, tail_pair = stack(head), stack(tail)
    sides = [
        triple((table_ref[0, side], table_ref[1, side]), (head_pair[side], tail_pair[side])) for side in range(2)
    ]
    return jnp.concatenate(sides, 1)


def stage_two(got_refs, mirror_ref, recv_ref):
    got = jnp.concatenate([ref[...] for ref in got_refs], 0)
    return unpack(got, mirror_ref[...], recv_ref)


def call(kernel, name, inputs, outs, after=(), limit=24, token=False, near=False, **more):
    count, end = len(after), len(after) + len(inputs) + len(outs)

    def body(*refs):
        if token:
            kernel(*refs[count:end], *refs[end + 1 :])
            refs[end][...] = jnp.zeros_like(refs[end])
        else:
            kernel(*refs[count:])

    in_specs = more.pop("in_specs", None)
    if in_specs is None:
        in_specs = [SMEM if a.dtype == jnp.int32 and len(a.shape) == 1 else VMEM for a in inputs]
    out_specs = list(more.pop("out_specs", [VMEM] * len(outs)))
    far = lambda s: s is HBM or s.block_shape is not None and not near
    place = lambda s: pltpu.HBM if far(s) else pltpu.VMEM if s is NEAR else None
    inputs = [pltpu.with_memory_space_constraint(a, place(s)) if place(s) else a for a, s in zip(inputs, in_specs)]
    out_shape = [place(s)(o.shape, o.dtype) if place(s) else o for o, s in zip(outs, out_specs)]
    results = pl.pallas_call(
        body,
        in_specs=[ANY] * count + list(in_specs),
        out_specs=out_specs + [VMEM] * token,
        out_shape=out_shape + [array(8, 128)] * token,
        compiler_params=pltpu.CompilerParams(vmem_limit_bytes=limit * 2**20),
        cost_estimate=pl.CostEstimate(flops=int(MICROSECONDS[name] * 3.45e+09), bytes_accessed=0, transcendentals=0),
        name=name,
        **more,
    )(*after, *inputs)
    return list(results)


def hold(values, after):
    count = len(after)
    after = [pltpu.with_memory_space_constraint(a, pltpu.HBM) if math.prod(a.shape) > 8192 else a for a in after]
    return pl.pallas_call(
        lambda *refs: None,
        in_specs=[ANY] * (count + 1),
        out_specs=ANY,
        out_shape=array(*values.shape),
        input_output_aliases={count: 0},
        compiler_params=pltpu.CompilerParams(vmem_limit_bytes=2**20),
        name="hold",
    )(*after, values)


def array(*shape, dtype=HIGH):
    return jax.ShapeDtypeStruct(shape, dtype)


def pick_kernel(at_ref, *refs):
    *refs, sems = refs
    half = len(refs) // 2
    wait_all(start_all([(source.at[at_ref[0]], target) for source, target in zip(refs[:half], refs[half:])], sems))


def cut_kernel(layer, order, piece, blocks_ref, shares_ref, up_ref, down_ref, up_out, down_out, held, chosen_up, chosen_down, sems, down_sems):
    count, _, block = held.shape
    copies = []
    for b in range(count):
        start = pl.multiple_of(blocks_ref[b] * block, 128)
        copies.append(start_all([(up_ref.at[layer, :, pl.ds(start, block)], held.at[b])], sems.at[pl.ds(b, 1)]))
    downs = []
    for p, (b, h) in enumerate(order):
        start = pl.multiple_of(blocks_ref[b] * block + shares_ref[h] * piece, 16)
        target = chosen_down.at[p * piece : (p + 1) * piece]
        downs.append(pltpu.make_async_copy(down_ref.at[layer, pl.ds(start, piece), :], target, down_sems.at[p]))
        downs[-1].start()
    row = lax.broadcasted_iota(jnp.int32, (piece, block), 0)
    lane = lax.broadcasted_iota(jnp.int32, (piece, block), 1)
    chosen = [(lane == row + share * piece).astype(HIGH).astype(LOW) for share in (shares_ref[0], shares_ref[1])]
    wait_all(downs)
    outs = start_all([(chosen_down, down_out)], sems.at[pl.ds(count, 1)])
    for b in range(count):
        wait_all(copies[b])
        for p, (of, h) in enumerate(order):
            if of == b:
                chosen_up[p * piece : (p + 1) * piece] = wide(chosen[h], held[b], (1, 1)).astype(LOW)
    wait_all(outs + start_all([(chosen_up, up_out)], sems.at[pl.ds(0, 1)]))


def class_rows(count, dest):
    row, i = dest // count, dest % count
    if isinstance(dest, int):
        return row, pair_of(count, i)
    return row, (i, jnp.where(i == 0, count, 2 * count - i))


def spread_marked_kernel(count, at_ref, *rest):
    sources, (*outs, held), targets, sems = rest[:4], rest[4:-5], rest[-5:-1], rest[-1]
    wait_all(start_all(zip(sources, targets), sems))
    values_ref, segments_ref, padding_ref, table_ref = targets
    rows, part, width = values_ref.shape
    units = part // (2 * count)
    flags = jnp.concatenate([padding_ref[...], segments_ref[...], jnp.zeros((8 - 2 * rows, part), jnp.int32)], 0)
    flags = flags.astype(HIGH).astype(LOW)
    at = lax.broadcasted_iota(jnp.int32, (8, MARK), 0)
    lane = lax.broadcasted_iota(jnp.int32, (8, MARK), 1)
    for row in range(rows):
        pick = ((at == row) & (lane == 0)) | ((at == rows + row) & (lane == 1))
        marks = wide(flags, pick.astype(HIGH).astype(LOW), (0, 0))
        kind = marks[:, 1:2]
        values = values_ref[row]
        for t in range(table_ref.shape[0]):
            values = values + jnp.where(kind == float(t), table_ref[t : t + 1, :], 0.0)
        held[row, :, :, :width] = values.reshape(units, 2 * count, width)
        held[row, :, :, width:] = marks.reshape(units, 2 * count, MARK)
    for k, out in enumerate(outs):
        row, classes = class_rows(count, at_ref[0] ^ k)
        for h, at in enumerate(classes):
            out[h * units : (h + 1) * units, :] = held[row, :, at, :]


def spread_kernel(count, values_ref, out):
    rows, units, step, width = values_ref.shape
    for dest in range(rows * count):
        row, classes = class_rows(count, dest)
        for h, at in enumerate(classes):
            out[dest, h * units : (h + 1) * units, :] = values_ref[row, :, at, :]


def collect_kernel(count, blocks, *outs):
    rows, units, step, width = outs[0].shape
    part = blocks.shape[1] // len(outs)
    for source in range(rows * count):
        row, classes = class_rows(count, source)
        for n, out in enumerate(outs):
            for h, at in enumerate(classes):
                first = n * part + h * units
                out[row, :, at, :] = blocks[source, first : first + units, :]


def turned(at_ref, blocks):
    return [at_ref[0] ^ k for k in range(blocks)]


def enter_kernel(blocks, *refs):
    sources = refs[:blocks]
    feature_ref, send_ref, carried_ref, marks_ref, spectrum_ref, *sent_refs, held, sems = refs[blocks:]
    width = carried_ref.shape[1]
    rows = held.shape[0] // blocks
    wait_all(start_all([(ref, held.at[k * rows : (k + 1) * rows]) for k, ref in enumerate(sources)], sems))
    values = held[:, :width]
    carried_ref[...] = values
    marks_ref[...] = held[:, width:]
    stage_one(values * held[:, width : width + 1], feature_ref, send_ref, spectrum_ref, sent_refs)


def own_kernel(masked, layer, *refs):
    if layer is not None:
        *refs, up_in, down_in, out_ref, up_out, down_out, sems = refs
        copies = start_all([(up_in.at[layer], up_out), (down_in.at[layer], down_out)], sems)
    else:
        *refs, out_ref = refs
        copies = []
    spectrum_ref, carried_ref, mirror_ref, block_ref, *marks = refs
    mixed = unpack(spectrum_ref[...], mirror_ref[...], block_ref)
    if masked:
        mixed = mixed * marks[0][:, :1]
    out_ref[...] = carried_ref[...] + mixed
    wait_all(copies)


LANES = 1


def copies_of(pairs, sems):
    found = []
    for k, (source, target) in enumerate(pairs):
        rows = source.shape[0]
        parts = LANES if rows % (16 * LANES) == 0 else 1
        for part in range(parts):
            at = pl.ds(part * (rows // parts), rows // parts)
            found.append(pltpu.make_async_copy(source.at[at], target.at[at], sems.at[k, part]))
    return found


def start_all(pairs, sems):
    copies = copies_of(pairs, sems)
    for copy in copies:
        copy.start()
    return copies


def wait_all(copies):
    for copy in copies:
        copy.wait()


def keep(unit, inverse, held):
    width = unit.shape[1]
    held[:, :width] = unit
    held[:, width:] = jnp.broadcast_to(inverse, (unit.shape[0], held.shape[1] - width))


def weight_copies(layer, up_ref, down_ref, up_held, down_held, sems, chunk):
    width = up_held.shape[1]
    at = pl.ds(pl.multiple_of(chunk * width, 128), width)
    return (
        pltpu.make_async_copy(up_ref.at[layer, :, at], up_held.at[chunk], sems.at[0, chunk]),
        pltpu.make_async_copy(down_ref.at[layer, at, :], down_held.at[chunk], sems.at[1, chunk]),
    )


def next_weights(layer, refs, chunk):
    wait_all(weight_copies(layer, *refs, chunk))

    @pl.when(chunk + 1 < pl.num_programs(0))
    def _():
        for copy in weight_copies(layer, *refs, chunk + 1):
            copy.start()


def mix_kernel(layer, got, *refs):
    got_refs, refs = refs[:got], refs[got:]
    base_ref, mirror_ref, recv_ref, gain_ref, shift_ref, normed_out, unit_out, held_normed, held, sems = refs
    mixed = base_ref[...] + stage_two(got_refs, mirror_ref, recv_ref)
    unit, inverse = normalize(mixed)
    held_normed[...] = unit * gain_ref[layer, 0:1, :] + shift_ref[layer, 0:1, :]
    copies = start_all([(held_normed, normed_out)], sems)
    keep(unit, inverse, held)
    wait_all(copies + start_all([(held, unit_out)], sems.at[pl.ds(1, 1)]))


def chunk_of(chunk, width):
    return pl.ds(pl.multiple_of(chunk * width, 128), width)


def feed_kernel(layer, last, *refs):
    if last:
        *refs, held, delta_ref, low_ref, total_ref, more_sems, out_sems = refs
    else:
        *refs, held, low_ref, total_ref, up_held, down_held, feature_ref, send_ref, sems, more_sems, out_sems = refs
    normed_in, up_ref, up_bias_ref, down_ref, down_bias_ref, gain_ref, shift_ref, *refs = refs
    chunk = pl.program_id(0)
    width = low_ref.shape[1]
    if last:
        at_ref, upstream_ref, slope_ref, minor_ref, delta_far, carried_out = refs
        fetched = [(normed_in, total_ref)]
    else:
        marks_ref, feature_in, send_in, slope_ref, carried_ref, spectrum_ref, *sent_refs, unit_out = refs
        fetched = [(normed_in, total_ref), (feature_in, feature_ref), (send_in, send_ref)]
        weights = (up_ref, down_ref, up_held, down_held, sems)

    @pl.when(chunk == 0)
    def _():
        copies = start_all(fetched[:1], more_sems)
        if not last:
            for copy in weight_copies(layer, *weights, 0):
                copy.start()
        wait_all(copies)
        normed = total_ref[...]
        low_ref[...] = normed.astype(LOW)
        total_ref[...] = normed + down_bias_ref[layer : layer + 1, :]

    if last:
        at = chunk_of(chunk, width)
        up, down = up_ref[:, at], down_ref[at, :]
    else:
        next_weights(layer, weights, chunk)
        up, down = up_held[chunk], down_held[chunk]

        @pl.when(chunk == 1)
        def _():
            start_all(fetched[1:], more_sems.at[pl.ds(1, 2)])

    preact = wide(low_ref[...], up) + up_bias_ref[layer : layer + 1, :]
    value, slope = gelu_parts(preact)
    slope_ref[...] = slope.astype(slope_ref.dtype)
    total_ref[...] += wide(value.astype(LOW), down)

    @pl.when(chunk == pl.num_programs(0) - 1)
    def _():
        unit, inverse = normalize(total_ref[...])
        gain = gain_ref[layer, 1:2, :]
        carried = unit * gain + shift_ref[layer, 1:2, :]
        if last:
            blocks, rows, _ = upstream_ref.shape
            order = turned(at_ref, blocks)
            upstream = jnp.concatenate([upstream_ref[at] for at in order], 0)
            delta_out(upstream, unit, inverse, gain, delta_ref, minor_ref)
            copies = start_all([(delta_ref, delta_far)], out_sems)
            for k, at in enumerate(order):
                held[at] = carried[k * rows : (k + 1) * rows]
            wait_all(copies + start_all([(held, carried_out)], out_sems.at[pl.ds(1, 1)]))
        else:
            keep(unit, inverse, held)
            copies = start_all([(held, unit_out)], out_sems)
            carried_ref[...] = carried
            wait_all(copies_of(fetched[1:], more_sems.at[pl.ds(1, 2)]))
            stage_one(carried * marks_ref[:, :1], feature_ref, send_ref, spectrum_ref, sent_refs)
            wait_all(copies)


def delta_out(upstream, unit, inverse, gain, delta_ref, minor_ref):
    delta = norm_back(upstream, unit, inverse, gain)
    delta_ref[...] = delta
    rows = [upstream * unit, upstream, delta.astype(LOW).astype(HIGH)]
    for at, value in enumerate(rows):
        minor_ref[at : at + 1, :] = jnp.sum(value, 0, keepdims=True)
    minor_ref[len(rows) :, :] = jnp.zeros_like(minor_ref[len(rows) :, :])


def delta_kernel(layer, got, *refs):
    got_refs, refs = refs[:got], refs[got:]
    base_ref, marks_ref, mirror_ref, recv_ref, unit_in, gain_ref, minor_ref, delta_far, delta_ref, held, sems = refs
    copies = start_all([(unit_in, held)], sems)
    upstream = base_ref[...] + marks_ref[:, :1] * stage_two(got_refs, mirror_ref, recv_ref)
    wait_all(copies)
    width = upstream.shape[1]
    unit, inverse = held[:, :width], held[:, width : width + 1]
    delta_out(upstream, unit, inverse, gain_ref[layer, 1:2, :], delta_ref, minor_ref)
    wait_all(start_all([(delta_ref, delta_far)], sems))


def backward_kernel(layer, near, *refs):
    if near:
        *refs, low_ref, total_ref, held_unit, feature_ref, send_ref, more_sems = refs
    else:
        *refs, low_ref, total_ref, held_unit, feature_ref, send_ref, more_sems, up_held, down_held, sems = refs
    delta_in, slope_ref, up_ref, down_ref, unit_in, gain_ref, feature_in, send_in, *refs = refs
    mixed_ref, minor_ref, spectrum_ref, *sent_refs = refs
    chunk = pl.program_id(0)
    width = low_ref.shape[1]
    fetched = [(unit_in, held_unit), (feature_in, feature_ref), (send_in, send_ref)]

    @pl.when(chunk == 0)
    def _():
        copies = start_all([(delta_in, total_ref)], more_sems)
        if not near:
            for copy in weight_copies(layer, up_ref, down_ref, up_held, down_held, sems, 0):
                copy.start()
        wait_all(copies)
        low_ref[...] = total_ref[...].astype(LOW)
        minor_ref[...] = jnp.zeros_like(minor_ref)

    if near:
        at = chunk_of(chunk, width)
        up, down = up_ref[:, at], down_ref[at, :]
    else:
        next_weights(layer, (up_ref, down_ref, up_held, down_held, sems), chunk)
        up, down = up_held[chunk], down_held[chunk]

    @pl.when(chunk == 1)
    def _():
        start_all(fetched, more_sems.at[pl.ds(1, 3)])

    slope = (wide(low_ref[...], down, (1, 1)) * slope_ref[...].astype(HIGH)).astype(LOW)
    minor_ref[pl.ds(2 + chunk, 1), :] = jnp.sum(slope.astype(HIGH), 0, keepdims=True)
    total_ref[...] += wide(slope, up, (1, 1))

    @pl.when(chunk == pl.num_programs(0) - 1)
    def _():
        upstream = total_ref[...]
        wait_all(copies_of(fetched, more_sems.at[pl.ds(1, 3)]))
        unit, inverse = held_unit[:, :width], held_unit[:, width : width + 1]
        minor_ref[0:1, :] = jnp.sum(upstream * unit, 0, keepdims=True)
        minor_ref[1:2, :] = jnp.sum(upstream, 0, keepdims=True)
        mixed = norm_back(upstream, unit, inverse, gain_ref[layer, 0:1, :])
        mixed_ref[...] = mixed
        stage_one(mixed, feature_ref, send_ref, spectrum_ref, sent_refs)


def leave_kernel(types, got, *refs):
    got_refs, refs = refs[:got], refs[got:]
    at_ref, base_ref, marks_ref, mirror_ref, recv_ref, minor_ref, out, held, sems = refs
    upstream = base_ref[...] + marks_ref[:, :1] * stage_two(got_refs, mirror_ref, recv_ref)
    kind = marks_ref[:, 1:2]
    for t in range(types):
        minor_ref[t : t + 1, :] = jnp.sum(jnp.where(kind == float(t), upstream, 0.0), 0, keepdims=True)
    minor_ref[types:, :] = jnp.zeros_like(minor_ref[types:, :])
    blocks, rows, _ = held.shape
    for k, at in enumerate(turned(at_ref, blocks)):
        held[at] = upstream[k * rows : (k + 1) * rows]
    wait_all(start_all([(held, out)], sems))


def grads_kernel(plan, places, counts, *refs):
    starts_ref, refs = refs[0], refs[1:]
    normed_refs, refs = refs[: counts[0]], refs[counts[0] :]
    delta_refs, refs = refs[: counts[1]], refs[counts[1] :]
    up_in, bias_ref, down_in, *refs = refs
    *refs, normed_held, delta_held, up_ref, down_ref, normed_low, delta_low, hidden, back, sems, more_sems, out_sems = refs
    results, outs = refs[: len(refs) // 2], refs[len(refs) // 2 :]
    step = pl.program_id(0)
    blocks = len(plan)
    rows = normed_held.shape[1]
    units = up_ref.shape[0]
    piece = units // len(places)
    share = units // (pl.num_programs(0) - blocks)

    def copies(b):
        found = []
        for refs, held, parts in ((normed_refs, normed_held, plan[b][0]), (delta_refs, delta_held, plan[b][1])):
            at = 0
            for index, start, count in parts:
                source = refs[index]
                if start is not None:
                    source = source.at[pl.ds(pl.multiple_of(starts_ref[start], 8), count)]
                target = held.at[b % 2, at : at + count]
                found.append(pltpu.make_async_copy(source, target, sems.at[b, len(found)]))
                at += count
        return found

    def start(b):
        for copy in copies(b):
            copy.start()

    for b in range(blocks):

        @pl.when(step == b)
        def _():
            if b == 0:
                start(0)
                fetched = start_all([(up_in, up_ref), (down_in, down_ref)], more_sems)
            wait_all(copies(b))
            if b + 1 < blocks:
                start(b + 1)
            if b == 0:
                wait_all(fetched)
            at = slice(b * rows, (b + 1) * rows)
            normed = normed_held[b % 2].astype(LOW)
            delta = delta_held[b % 2].astype(LOW)
            normed_low[at] = normed
            delta_low[at] = delta
            value, slope = gelu_parts(wide(normed, up_ref[...], (1, 1)) + bias_ref[...])
            hidden[at] = value.astype(LOW)
            back[at] = (wide(delta, down_ref[...], (1, 1)) * slope).astype(LOW)

    def sent(c):
        found = []
        for p in range(c * share // piece, (c + 1) * share // piece):
            for h, (out, slot, first) in enumerate(places[p]):
                at = (slot, pl.ds(first, piece))
                found.append(pltpu.make_async_copy(outs[out].at[at], results[out].at[at], out_sems.at[p, h]))
        return found

    chunks = units // share
    for c in range(chunks):

        @pl.when(step == blocks + c)
        def _():
            at = slice(c * share, (c + 1) * share)
            both = (wide(back[:, at], normed_low[...], (0, 0)), wide(hidden[:, at], delta_low[...], (0, 0)))
            for p in range(c * share // piece, (c + 1) * share // piece):
                first_row = p * piece - c * share
                for (out, slot, first), a in zip(places[p], both):
                    outs[out][slot, first : first + piece] = a[first_row : first_row + piece]
            for copy in sent(c):
                copy.start()
            if c == chunks - 1:
                for k in range(chunks):
                    wait_all(sent(k))


def finish_kernel(layer, at_ref, *refs):
    *pieces, up_ref, down_ref, turned_ref = refs
    rows = pieces[0].shape[0] // 2
    for k, ref in enumerate(pieces[:4]):
        at = pl.multiple_of((at_ref[0] ^ k) * rows, 8)
        turned_ref[pl.ds(at, rows), :] = ref[:rows, :]
        down_ref[0, pl.ds(at, rows), :] = ref[rows:, :]
    up_ref[0] = turned_ref[...].T


def swap(values, axes, k):
    count = lax.axis_size(axes)
    return lax.ppermute(values, axes, [(i, i ^ k) for i in range(count)])


def exchange(blocks, axes, first=0):
    return [b if k == 0 else swap(b, axes, k) for k, b in enumerate(blocks, first)]


def sum_over(values, groups):
    for axes in groups:
        moved = [swap(values, axes, k) for k in range(1, lax.axis_size(axes))]
        values = sum(moved, values)
    return values


def local(inputs, segments, padding, type_table, ln_gain, ln_bias, up_weight, up_bias, down_weight, down_bias, out_grad):
    rows, part, width = inputs.shape
    layers, _, hidden_width = up_weight.shape
    types = type_table.shape[0]
    seq, count = lax.axis_size(SEQ), lax.axis_size(ROW)
    step = 2 * count
    units = part // step
    tokens = rows * part
    block = tokens // seq
    half = width // 2
    place = lax.axis_index(SEQ).reshape(1)

    feature = jnp.asarray(feature_table(width))
    mirror = jnp.asarray(mirror_table(half))
    tables = position_tables(count, part, seq)
    chunk = tables[0].shape[3] // (count - 1)
    sent_outs = [array(chunk, width)] * (count - 1)
    whole = array(tokens, width)
    kept = array(tokens, width + MARK)
    blocks_out = array(seq, block, width)
    minor_out = array(8, width)
    steps = hidden_width // width

    def spread(values, after):
        shaped = values.reshape(rows, units, step, width)
        out, token = call(functools.partial(spread_kernel, count), "spread", [shaped], [blocks_out], after, token=True)
        return lax.all_to_all(out, SEQ, 0, 0, tiled=True), token

    def collect(got, after):
        out = array(rows, units, step, width)
        *back, token = call(functools.partial(collect_kernel, count), "collect", [got], [out], after, token=True)
        return [b.reshape(inputs.shape) for b in back] + [token]

    weight_outs = [array(width, hidden_width, dtype=LOW), array(hidden_width, width, dtype=LOW)]

    def own(spectrum, carried, marks=None, after=(), token=False, layer=None):
        inputs = [spectrum, carried, mirror, block_t] + ([] if marks is None else [marks])
        kernel = functools.partial(own_kernel, marks is not None, layer)
        if layer is None:
            return call(kernel, "own_part", inputs, [whole], after, token=token)
        return call(
            kernel,
            "own_fetch",
            inputs + [up_weight, down_weight],
            [whole] + weight_outs,
            after,
            token=token,
            limit=8,
            in_specs=[VMEM] * len(inputs) + [HBM] * 2,
            out_specs=[VMEM, NEAR, NEAR],
            scratch_shapes=[pltpu.SemaphoreType.DMA((2, LANES))],
        )

    column = pl.BlockSpec((tokens, width), lambda c: (0, c))
    slope_out = array(tokens, hidden_width)
    scratch = [pltpu.VMEM((tokens, width), LOW), pltpu.VMEM((tokens, width), HIGH)]
    scratch += [pltpu.VMEM((steps, width, width), LOW)] * 2
    bias_spec = pl.BlockSpec((layers, width), lambda c: (0, c))

    held_kept = pltpu.VMEM(kept.shape, HIGH)
    dma = lambda n: pltpu.SemaphoreType.DMA((n, LANES))

    held_whole = pltpu.VMEM(whole.shape, HIGH)
    held_tables = [pltpu.VMEM(t, LOW) for t in (feature.shape, tables[0].shape[1:])]

    def mix(layer, got, base, after=()):
        inputs = got + [base, mirror, recv_t, ln_gain, ln_bias]
        return call(
            functools.partial(mix_kernel, layer, len(got)),
            "mix",
            inputs,
            [whole, kept],
            after,
            out_specs=[ANY, ANY] if layer == layers - 1 else [HBM, HBM],
            scratch_shapes=[held_whole, held_kept, dma(2)],
        )

    def feed(layer, normed, up, down, *more, after=(), token=False):
        last = layer == layers - 1
        inputs = [normed, up, up_bias, down, down_bias, ln_gain, ln_bias] + list(more)
        outs = [slope_out]
        outs += [minor_out, whole, blocks_out] if last else [whole, whole] + sent_outs + [kept]
        far = 2 if last else 1
        held = [pltpu.VMEM(blocks_out.shape, HIGH), held_whole] if last else [held_kept]
        fetches = [] if last else scratch[2:] + held_tables + [pltpu.SemaphoreType.DMA((2, steps))]
        weights = NEAR if last else HBM
        return call(
            functools.partial(feed_kernel, layer, last),
            "layer_feed" if last else "layer_forward",
            inputs,
            outs,
            after,
            near=last,
            token=token,
            grid=(steps,),
            in_specs=[ANY if last else HBM, weights, bias_spec, weights]
            + [VMEM] * 3
            + ([SMEM, VMEM] if last else [VMEM, HBM, HBM]),
            out_specs=[column] + [VMEM] * (len(outs) - 1 - far) + ([ANY, HBM] if last else [HBM]),
            scratch_shapes=held + scratch[:2] + fetches + [dma(3), dma(2)],
        )

    def backward(layer, delta, slope, up, down, kept, after=(), token=False):
        inputs = [delta, slope, up, down, kept, ln_gain, feature, send_t]
        outs = [whole, minor_out, whole] + sent_outs
        last = layer == layers - 1
        return call(
            functools.partial(backward_kernel, layer, last),
            "layer_backward" if last else "layer_stream",
            inputs,
            outs,
            after,
            near=last,
            token=token,
            grid=(steps,),
            in_specs=[ANY, column, NEAR, NEAR, ANY, VMEM, HBM, HBM]
            if last
            else [HBM, column, HBM, HBM, HBM, VMEM, HBM, HBM],
            out_specs=[VMEM] * len(outs),
            scratch_shapes=scratch[:2]
            + [held_kept]
            + held_tables
            + [dma(4)]
            + ([] if last else scratch[2:] + [pltpu.SemaphoreType.DMA((2, steps))]),
        )

    def delta(layer, got, base, marks, kept, after=()):
        inputs = got + [base, marks, mirror, recv_t, kept, ln_gain]
        return call(
            functools.partial(delta_kernel, layer, len(got)),
            "delta",
            inputs,
            [minor_out, whole],
            after,
            in_specs=[VMEM] * (len(got) + 4) + [HBM, VMEM],
            out_specs=[VMEM, HBM],
            scratch_shapes=[held_whole, held_kept, dma(1)],
        )

    columns = lax.axis_size("x")
    planes, shares = lax.axis_size(PLANES), lax.axis_size(SHARES)
    unit_block = hidden_width // seq
    piece = unit_block // shares
    x, dy, core, zh, zl = (lax.axis_index(a) for a in ("x", "dy", "core", "zh", "zl"))
    swapped = columns == 2

    def pair_pieces():
        nearby = [0, 1] if swapped else list(range(columns))
        own_x, own_dy, own_zh = (x, dy, zh) if swapped else (0, 0, 0)
        blocks = [((own_zh ^ b) * 2 + zl) * columns + (own_x ^ a) for a in nearby for b in (0, 1)]
        order = [(a * 2 + b, c) for a in nearby for c in (0, 1) for b in (0, 1)]
        return blocks, [(own_dy ^ c) * 2 + core for c in (0, 1)], order

    def plane_pieces():
        blocks = [z * columns + x for z in range(planes)]
        return blocks, [dy * 2 + (core ^ c) for c in (1, 0)], [(z, c) for c in (0, 1) for z in range(planes)]

    def bias_of(layer):
        blocks, shared, order = pair_pieces() if layer == layers - 1 else plane_pieces()
        starts = [blocks[b] * unit_block + shared[h] * piece for b, h in order]
        return jnp.concatenate([lax.dynamic_slice(up_bias, (layer, s), (1, piece)) for s in starts], 1)

    biases = [bias_of(layer) for layer in range(layers)]

    def cut(layer, after):
        blocks, shared, order = pair_pieces() if layer == layers - 1 else plane_pieces()
        starts = [blocks[b] * unit_block + shared[h] * piece for b, h in order]
        bias = biases[layer]
        if unit_block % 128:
            up = [lax.dynamic_slice_in_dim(up_weight[layer], s, piece, 1).T for s in starts]
            down = [lax.dynamic_slice_in_dim(down_weight[layer], s, piece, 0) for s in starts]
            return jnp.concatenate(up, 0), bias, jnp.concatenate(down, 0), bias
        out = array(piece * len(order), width, dtype=LOW)
        up, down, token = call(
            functools.partial(cut_kernel, layer, order, piece),
            "cut",
            [jnp.stack(blocks).astype(jnp.int32), jnp.stack(shared).astype(jnp.int32), up_weight, down_weight],
            [out, out],
            after,
            token=True,
            in_specs=[SMEM, SMEM, HBM, HBM],
            out_specs=[HBM, HBM],
            scratch_shapes=[
                pltpu.VMEM((len(blocks), width, unit_block), LOW),
                pltpu.VMEM(out.shape, LOW),
                pltpu.VMEM(out.shape, LOW),
                dma(len(blocks) + 1),
                pltpu.SemaphoreType.DMA((len(order),)),
            ],
        )
        return up, bias, down, token

    def weight_grads(normed, starts, deltas, plan, cuts, places, outs, after=()):
        size = sum(r for _, _, r in plan[0][0])
        chosen = cuts[0].shape[0]
        share = max(384 // piece, 1) * piece
        total = len(plan) * size
        plan = [(plan[b][0] + plan[b + 1][0], plan[b][1] + plan[b + 1][1]) for b in range(0, len(plan), 2)]
        size = 2 * size
        inputs = [jnp.stack(starts).astype(jnp.int32)] + normed + deltas + list(cuts[:3])
        return call(
            functools.partial(grads_kernel, plan, places, (len(normed), len(deltas))),
            "weight_grads",
            inputs,
            outs,
            after,
            token=True,
            limit=56,
            grid=(len(plan) + chosen // share,),
            in_specs=[SMEM] + [HBM] * (len(normed) + len(deltas)) + [HBM, VMEM, HBM],
            out_specs=[HBM] * len(outs),
            scratch_shapes=[pltpu.VMEM(o.shape, HIGH) for o in outs]
            + [pltpu.VMEM((2, size, width), HIGH)] * 2
            + [pltpu.VMEM(cuts[0].shape, LOW)] * 2
            + [pltpu.VMEM((total, width), LOW)] * 2
            + [pltpu.VMEM((total, chosen), LOW)] * 2
            + [pltpu.SemaphoreType.DMA((len(plan), 8)), dma(2), pltpu.SemaphoreType.DMA((len(places), 2))],
        )

    def shared_out(summed):
        along = swap(summed, "dy", 1)
        return [summed, swap(summed, "core", 1), along, swap(along, "core", 1)]

    def pair_grads(normed, deltas, cuts, after):
        plan = [([(b, None, tokens)], [(b, None, tokens)]) for b in range(4)]
        order = [(a, c, b) for a in range(columns) for c in (0, 1) for b in (0, 1)]
        if not swapped:
            places = [((0, p, 0), (0, p, piece)) for p in range(len(order))]
            out = array(len(order), 2 * piece, width)
            return weight_grads(normed, [0], deltas, plan, cuts, places, [out], after)
        places = [((a, 2 * c + b, 0), (2 + c, 2 * a + b, 0)) for a, c, b in order]
        return weight_grads(normed, [0], deltas, plan, cuts, places, [array(4, piece, width)] * 4, after)

    def pair_first(sums):
        if not swapped:
            return [lax.psum_scatter(sums[0], ("x", "dy", "zh"), scatter_dimension=0, tiled=True)], []
        up, up_far, down, down_far = sums
        got_up, got_down = swap(up_far, "x", 1), swap(down_far, "dy", 1)
        return [up[2:] + got_up[2:], down[2:] + got_down[2:]], [up[:2] + got_up[:2], down[:2] + got_down[:2]]

    def pair_step(far, near):
        if not swapped:
            return far, near
        got_up, got_down = swap(far[0], "dy", 1), swap(far[1], "x", 1)
        up, down = near
        far = jnp.concatenate([up[1] + got_up[1], down[1] + got_down[1]], 0)
        return [far], [jnp.concatenate([up[0] + got_up[0], down[0] + got_down[0]], 0)]

    def pair_last(far, near):
        if not swapped:
            summed = far[0].reshape(2 * piece, width)
            return lax.psum(summed, "do") if lax.axis_size("do") > 1 else summed
        return near[0] + swap(far[0], "zh", 1)

    def plane_first(values):
        if not swapped:
            return [lax.all_gather(values, ("dy", "x"), tiled=True)]
        return [swap(values, "x", 1), swap(values, "dy", 1)]

    def plane_rest(found):
        if not swapped:
            return []
        rows = tokens // 2
        return [swap(found[0][:rows], "dy", 1), swap(found[1][rows:], "x", 1)]

    def plane_grads(normed, deltas, cuts, after):
        group = lax.axis_size(("dy", "x"))
        out = array(planes, 2 * piece, width)
        places = [((h, z, 0), (h, z, piece)) for h in range(2) for z in range(planes)]
        rows = tokens // 2
        parts = [[(0, None, tokens)], [(1, None, tokens)], [(2, None, tokens)], [(3, None, rows), (4, None, rows)]]
        starts = [((dy ^ a) * columns + (x ^ b)) * tokens for a, b in ((0, 0), (0, 1), (1, 0), (1, 1))]
        if not swapped:
            parts = [[(0, b, tokens)] for b in range(group)]
            starts = [b * tokens for b in range(group)]
        starts = [jnp.asarray(s, jnp.int32) for s in starts]
        plan = [([(0, b, tokens)], parts[b]) for b in range(group)]
        return weight_grads([normed], starts, deltas, plan, cuts, places, [out, out], after)

    def plane_sum(both):
        summed = lax.psum_scatter(both.reshape(-1, width), PLANES, scatter_dimension=0, tiled=True)
        return lax.psum(summed, "do") if lax.axis_size("do") > 1 else summed

    def alone(stage, *operands):
        shapes = jax.eval_shape(stage, *operands)
        blank = lambda *_: jax.tree.map(lambda a: jnp.zeros(a.shape, a.dtype), shapes)
        return lax.cond(place[0] < 1000000, stage, blank, *operands)

    def send_and_own(sent, spectrum, mixed, marks):
        return exchange(sent, ROW, 1), own(spectrum, mixed, marks, token=True)

    held = call(
        functools.partial(spread_marked_kernel, count),
        "spread_marked",
        [place, inputs, segments, padding, type_table],
        [array(block, width + MARK)] * seq,
        in_specs=[SMEM] + [HBM] * 4,
        scratch_shapes=[pltpu.VMEM((rows, units, step, width + MARK), HIGH)]
        + [pltpu.VMEM(a.shape, a.dtype) for a in (inputs, segments, padding, type_table)]
        + [dma(4)],
    )
    held = exchange(held, SEQ)
    send_t, recv_t, block_t = call(
        pick_kernel,
        "pick",
        [place] + [jnp.asarray(t) for t in tables],
        [array(*t.shape[1:], dtype=LOW) for t in tables],
        held[1:4],
        in_specs=[SMEM] + [HBM] * 3,
        scratch_shapes=[dma(3)],
    )
    cuts = [None] * (layers - 1) + [cut(layers - 1, held[1:4])]
    carried, marks, spectrum, *sent = call(
        functools.partial(enter_kernel, seq),
        "enter",
        held + [feature, send_t],
        [whole, array(tokens, MARK), whole] + sent_outs,
        [cuts[-1][3]] + biases,
        in_specs=[VMEM] + [HBM] * (seq - 1) + [VMEM] * 2,
        scratch_shapes=[pltpu.VMEM((tokens, width + MARK), HIGH), dma(seq)],
    )
    upstream, made = spread(out_grad, sent[:1])
    saved = []
    for layer in range(layers - 1):
        got = exchange(sent, ROW, 1)
        base = own(spectrum, carried, after=[made])[0]
        normed, kept_one = mix(layer, got, base)
        all_normed = lax.all_gather(normed, ("dy", "x"), tiled=True)
        slope, carried, spectrum, *sent, kept_two = feed(layer, normed, up_weight, down_weight, marks, feature, send_t)
        saved.append((all_normed, kept_one, slope, kept_two))
    got = exchange(sent, ROW, 1)
    base, up, down = own(spectrum, carried, after=[upstream], layer=layers - 1)
    normed, kept_one = mix(layers - 1, got, base)

    def feed_stage(normed, kept, up, down, upstream):
        moved = swap(normed, "core", 1), swap(normed, "zl", 1)
        slope, minor_two, delta, outputs = feed(layers - 1, normed, up, down, place, upstream)
        return moved, minor_two, delta, outputs, backward(layers - 1, delta, slope, up, down, kept)

    moved_normed, minor_two, delta_two, outputs, (mixed, minor_one, spectrum, *sent) = alone(
        feed_stage, normed, kept_one, up, down, upstream
    )
    minors = [minor_two, minor_one]

    def send_and_swap(sent, spectrum, mixed, marks, normed_far, delta_two):
        got = exchange(sent, ROW, 1)
        return got, own(spectrum, mixed, marks)[0], swap(normed_far, "core", 1), swap(delta_two, "core", 1)

    got, base, *moved_delta = alone(send_and_swap, sent, spectrum, mixed, marks, moved_normed[1], delta_two)
    there, kept_one, slope, kept_two = saved[0]

    minor_two, delta_one = delta(0, got, base, marks, kept_two)

    def back_stage(delta_two, delta_one, kept_one, slope):
        cuts = cut(0, [delta_one])
        back = backward(0, delta_one, slope, up_weight, down_weight, kept_one, [cuts[3]])
        return swap(delta_two, "zl", 1), plane_first(delta_one), cuts, back

    delta_far, found, cuts[0], (mixed, minor_one, spectrum, *sent) = alone(
        back_stage, delta_two, delta_one, kept_one, slope
    )
    minors += [minor_two, minor_one]

    def grads_stage(normed, delta_two, delta_far, there, found, cuts, outputs):
        found = ([delta_one] if swapped else []) + found + plane_rest(found)
        deltas = delta_two + [delta_far, swap(delta_far, "core", 1)]
        outputs = lax.all_to_all(outputs, SEQ, 0, 0, tiled=True)
        *sums, token = pair_grads(normed, deltas, cuts[1], [])
        return plane_grads(there, found, cuts[0], [token])[:2], sums, outputs

    parts, sums, outputs = alone(
        grads_stage,
        [normed, moved_normed[0], moved_normed[1], moved_delta[0]],
        [delta_two, moved_delta[1]],
        delta_far,
        there,
        found,
        cuts,
        outputs,
    )

    both = parts[1] + swap(parts[0], "core", 1)
    whole_sum = plane_sum(both)

    def first_stage(sums, sent, spectrum, mixed, marks):
        return pair_first(sums), exchange(sent, ROW, 1), own(spectrum, mixed, marks)[0]

    (far, near), got, base = alone(first_stage, sums, sent, spectrum, mixed, marks)

    def middle_stage(far, near, outputs, minors, got, base, marks):
        minor_table, blocks = call(
            functools.partial(leave_kernel, types, len(got)),
            "leave",
            got + [place, base, marks, mirror, recv_t],
            [minor_out, blocks_out],
            out_specs=[VMEM, HBM],
            scratch_shapes=[pltpu.VMEM(blocks_out.shape, HIGH), dma(1)],
        )
        minor = sum_over(jnp.concatenate(minors + [minor_table], 0), [("core",)])
        return pair_step(far, near), minor, collect(outputs, [])[0], blocks

    (far, near), minor, outputs, blocks = alone(middle_stage, far, near, outputs, minors, got, base, marks)

    share = lax.axis_index(SHARES).reshape(1)
    outs = [array(layers, width, unit_block), array(layers, unit_block, width)]

    def finish(layer, pieces, grads):
        return call(
            functools.partial(finish_kernel, layer),
            "finish",
            [share] + pieces + grads,
            outs,
            in_specs=[SMEM] + [VMEM] * len(pieces) + [ANY] * len(grads),
            out_specs=[
                pl.BlockSpec((1,) + o.shape[1:], functools.partial(lambda l, i: (l, 0, 0), layer)) for o in outs
            ],
            grid=(1,),
            input_output_aliases={5: 0, 6: 1} if grads else {},
            scratch_shapes=[pltpu.VMEM((unit_block, width), HIGH)],
        )

    def last_stage(far, near, minor, whole_sum):
        return pair_last(far, near), sum_over(minor, [("dy", "x"), ("do",)]), shared_out(whole_sum)[1:]

    summed, minor, shared = alone(last_stage, far, near, minor, whole_sum)
    grads = finish(0, [whole_sum] + shared, [])

    pieces = shared_out(summed)
    blocks = lax.all_to_all(hold(blocks, [summed]), SEQ, 0, 0, tiled=True)
    minor = sum_over(minor, [PLANES])
    input_grad, _ = collect(blocks, [])
    up_grad, down_grad = finish(1, pieces, grads)
    ends = [minor[16 * (layers - 1 - l) :][:16] for l in range(layers)]
    table_grad = minor[16 * layers :][:types]
    gain_grad = jnp.stack([jnp.stack([e[8], e[0]]) for e in ends])
    shift_grad = jnp.stack([jnp.stack([e[9], e[1]]) for e in ends])
    down_vec = jnp.stack([e[2] for e in ends])
    up_vec = jnp.stack([e[10 : 10 + steps].reshape(-1) for e in ends])
    up_vec = lax.dynamic_slice_in_dim(up_vec, place[0] * unit_block, unit_block, 1)

    return outputs, input_grad, table_grad, gain_grad, shift_grad, up_grad, up_vec, down_grad, down_vec


def solution(mesh):
    dp, seq = mesh.shape["dp"], mesh.shape["seq"]
    shape = (dp // 4, 2, 2, 2, 2, seq // 4)
    finer = Mesh(mesh.devices.reshape(shape), ALL)
    in_specs = (P(DP, SEQ, None), P(DP, SEQ), P(DP, SEQ)) + (P(),) * 7 + (P(DP, SEQ, None),)
    out_specs = (
        P(DP, SEQ, None),
        P(DP, SEQ, None),
        P(),
        P(),
        P(),
        P(None, None, SEQ),
        P(None, SEQ),
        P(None, SEQ, None),
        P(),
    )
    return jax.shard_map(local, mesh=finer, in_specs=in_specs, out_specs=out_specs, check_vma=False)
```

```python
import functools
import math

import jax
import jax.numpy as jnp
import ml_dtypes
import numpy as np
from jax import lax
from jax.experimental import pallas as pl
from jax.experimental.pallas import tpu as pltpu
from jax.sharding import Mesh
from jax.sharding import PartitionSpec as P

EPSILON = 1e-05
DP = ("do", "dy", "core")
SEQ = ("zh", "zl", "x")
ROW = ("zl", "x")
PLANES = ("zh", "zl")
SHARES = ("dy", "core")
PLANE = ("dy", "core", "x")
ALL = DP + SEQ
MARK = 128
LOW = jnp.bfloat16
HIGH = jnp.float32
VMEM = pl.BlockSpec(memory_space=pltpu.VMEM)
NEAR = pl.BlockSpec(memory_space=pltpu.VMEM)
SMEM = pl.BlockSpec(memory_space=pltpu.SMEM)
ANY = pl.BlockSpec(memory_space=pl.ANY)
HBM = pl.BlockSpec(memory_space=pltpu.HBM)


MICROSECONDS = {
    "spread_marked": 2.0,
    "pick": 1.5,
    "cut": 5.9,
    "enter": 1.7,
    "spread": 1.0,
    "own_part": 1.5,
    "own_fetch": 5.5,
    "mix": 2.2,
    "layer_forward": 12.0,
    "layer_backward": 7.5,
    "layer_feed": 7.5,
    "layer_stream": 12.0,
    "delta": 2.8,
    "weight_grads": 3.0,
    "leave": 0.9,
    "collect": 2.2,
    "finish": 3.3,
}


def split_table(values):
    head = values.astype(ml_dtypes.bfloat16)
    return np.stack([head, (values - head.astype(np.float64)).astype(ml_dtypes.bfloat16)])


def feature_table(width):
    half = width // 2
    angle = np.outer(np.arange(width), np.arange(width)) % width * (2.0 * math.pi / width)
    cos, sin = np.cos(angle) / math.sqrt(width), np.sin(angle) / math.sqrt(width)
    return split_table(np.concatenate([cos[:, :half], cos[:, half : half + 1], sin[:, 1:half]], 1))


def mirror_table(half):
    table = np.zeros((half, half), ml_dtypes.bfloat16)
    table[half - np.arange(1, half), np.arange(1, half)] = 1.0
    return table


def pair_of(count, at):
    return at, 2 * count - at if at else count


def owned(count, part, seq, at):
    first, second = pair_of(count, at)
    pos = np.arange(seq * part).reshape(seq, part // (2 * count), 2 * count)
    return np.stack([pos[:, :, first], pos[:, :, second]], 1).reshape(-1)


def position_tables(count, part, seq):
    length = seq * part
    step = 2 * count
    span = length // step
    keep = span // step
    w = 2.0 * math.pi / length
    own = [owned(count, part, seq, i) for i in range(count)]
    local = length // count
    send = np.zeros((2, count, count, 2 * keep, local))
    recv = np.zeros((2, count, count, local, 2 * keep))
    block = np.zeros((2, count, local, local))
    scale = 1.0 / math.sqrt(length)

    def kept(i):
        if i:
            return [(i + step * s, 2) for s in range(keep)]
        ends = [(step * s, 1 if s in (0, keep // 2) else 2) for s in range(keep // 2 + 1)]
        return ends + [(count + step * s, 2) for s in range(keep // 2)]

    for j in range(count):
        n = own[j]
        first = n % step == j
        theta = 2.0 * math.pi * j / step
        for i in range(count):
            if i == j:
                angle = w * (np.outer(n, n) % length)
                block[0, i], block[1, i] = np.cos(angle) * scale, np.sin(angle) * scale
                continue
            at = 0
            slots = {}
            for kap, kinds in kept(i):
                cos, sin = np.cos(w * (kap * n % length)), np.sin(w * (kap * n % length))
                if j:
                    sign = np.where(first, 1.0, -1.0)
                    rows = (cos, sign * sin, sign * cos, sin)
                else:
                    rows = (cos * first, cos * ~first, sin * first, sin * ~first)
                if kinds == 2:
                    send[0, j, i, at], send[0, j, i, at + 1] = rows[:2]
                    send[1, j, i, at], send[1, j, i, at + 1] = rows[2:]
                    slots[kap] = (at, at + 1, 0.0)
                else:
                    phi = w * (kap * j % length)
                    send[0, j, i, at] = math.cos(phi) * rows[0] + math.sin(phi) * rows[1]
                    send[1, j, i, at] = math.cos(phi) * rows[2] + math.sin(phi) * rows[3]
                    slots[kap] = (at, at, phi)
                at += kinds
            for index, k in enumerate(own[i]):
                kap, turn = k % span, k // span
                mirrored = kap not in slots
                p_at, q_at, phi = slots[(span - kap) % span if mirrored else kap]
                pair = np.zeros((2, 2 * keep))
                if p_at == q_at:
                    pair[0, p_at], pair[1, p_at] = math.cos(phi), math.sin(phi)
                else:
                    pair[0, p_at], pair[1, q_at] = 1.0, 1.0
                even, odd = pair, pair
                if j:
                    if mirrored:
                        c, s = math.cos(theta), math.sin(theta)
                        even = odd = np.stack([c * pair[0] + s * pair[1], s * pair[0] - c * pair[1]])
                    c, s = math.cos(theta * turn), math.sin(theta * turn)
                    recv[0, i, j, index] = c * even[0] - s * even[1]
                    recv[1, i, j, index] = s * odd[0] + c * odd[1]
                else:
                    flip = (-1.0) ** turn
                    if mirrored:
                        even, odd = pair * np.array([[1.0], [-1.0]]), pair * np.array([[-1.0], [1.0]])
                    recv[0, i, j, index] = even[0] + flip * even[1]
                    recv[1, i, j, index] = odd[0] + flip * odd[1]
    recv = recv * scale
    sends, recvs, blocks = [], [], []
    for at in range(seq):
        i = at % count
        order = np.arange(local).reshape(seq, -1)[[at ^ k for k in range(seq)]].reshape(-1)
        others = [i ^ k for k in range(1, count)]
        sends.append(send[:, i, others].reshape(2, -1, local)[:, :, order])
        cos = np.concatenate([recv[0, i, j] for j in others], 1)[order]
        sin = np.concatenate([recv[1, i, j] for j in others], 1)[order]
        recvs.append(np.stack([np.concatenate([cos, -sin], 1), np.concatenate([cos, sin], 1)]))
        cos, sin = (block[h, i][order][:, order] for h in range(2))
        blocks.append(np.stack([np.concatenate([cos, -sin], 1), np.concatenate([cos, sin], 1)]))
    return tuple(np.moveaxis(split_table(np.stack(t)), 0, 1) for t in (sends, recvs, blocks))


def wide(left, right, contract=(1, 0)):
    return lax.dot_general(left, right, ((contract[:1], contract[1:]), ((), ())), preferred_element_type=HIGH)


def split(values):
    head = values.astype(LOW)
    return head, (values - head.astype(HIGH)).astype(LOW)


def triple(left, right):
    return wide(left[0], right[0]) + wide(left[0], right[1]) + wide(left[1], right[0])


def first_lane(values):
    return lax.broadcasted_iota(jnp.int32, values.shape, 1) == 0


def mean(values):
    return jnp.mean(values, axis=-1, keepdims=True)


def normalize(values):
    centered = values - mean(values)
    inverse = lax.rsqrt(mean(centered * centered) + EPSILON)
    return centered * inverse, inverse


def norm_back(upstream, unit, inverse, gain):
    scaled = upstream * gain
    return inverse * (scaled - mean(scaled) - unit * mean(scaled * unit))


def gelu_parts(p):
    c = math.sqrt(2.0 / math.pi)
    square = p * p
    t = jnp.tanh(p * (c + 0.044715 * c * square))
    halves = 0.5 + 0.5 * t
    slope = halves + p * (0.5 - 0.5 * (t * t)) * (c + 3.0 * 0.044715 * c * square)
    return p * halves, slope


def stage_one(values, feature_ref, send_ref, spectrum_ref, sent_refs):
    half = values.shape[1] // 2
    parts = split(values)
    spectrum = triple(parts, (feature_ref[0], feature_ref[1]))
    spectrum_ref[...] = spectrum
    head, tail = split(spectrum)
    lanes = half + 128
    even = triple((send_ref[0, 0], send_ref[1, 0]), (head[:, :lanes], tail[:, :lanes]))
    odd = triple((send_ref[0, 1], send_ref[1, 1]), (head[:, half:], tail[:, half:]))
    middle = jnp.where(first_lane(even[:, half:]), even[:, half:], odd[:, :128])
    rows = sent_refs[0].shape[0]
    for k, ref in enumerate(sent_refs):
        at = slice(k * rows, (k + 1) * rows)
        ref[:, :half] = even[at, :half]
        ref[:, half:lanes] = middle[at]
        ref[:, lanes:] = odd[at, 128:]


def unpack(packed, mirror, table_ref):
    half = packed.shape[1] // 2
    head, tail = split(packed)

    def stack(part):
        low, high = part[:, :half], part[:, half:]
        back = wide(jnp.concatenate([low, high], 0), mirror).astype(LOW)
        count = low.shape[0]
        turned = back[:count]
        middle = jnp.where(first_lane(turned[:, :128]), high[:, :128].astype(HIGH), turned[:, :128].astype(HIGH))
        turned = jnp.concatenate([middle.astype(LOW), turned[:, 128:]], 1)
        edge = jnp.where(first_lane(high[:, :128]), 0.0, high[:, :128].astype(HIGH)).astype(LOW)
        high = jnp.concatenate([edge, high[:, 128:]], 1)
        return jnp.concatenate([low, high], 0), jnp.concatenate([turned, back[count:]], 0)

    head_pair, tail_pair = stack(head), stack(tail)
    sides = [
        triple((table_ref[0, side], table_ref[1, side]), (head_pair[side], tail_pair[side])) for side in range(2)
    ]
    return jnp.concatenate(sides, 1)


def stage_two(got_refs, mirror_ref, recv_ref):
    got = jnp.concatenate([ref[...] for ref in got_refs], 0)
    return unpack(got, mirror_ref[...], recv_ref)


def call(kernel, name, inputs, outs, after=(), limit=24, token=False, near=False, **more):
    count, end = len(after), len(after) + len(inputs) + len(outs)

    def body(*refs):
        if token:
            kernel(*refs[count:end], *refs[end + 1 :])
            refs[end][...] = jnp.zeros_like(refs[end])
        else:
            kernel(*refs[count:])

    in_specs = more.pop("in_specs", None)
    if in_specs is None:
        in_specs = [SMEM if a.dtype == jnp.int32 and len(a.shape) == 1 else VMEM for a in inputs]
    out_specs = list(more.pop("out_specs", [VMEM] * len(outs)))
    far = lambda s: s is HBM or s.block_shape is not None and not near
    place = lambda s: pltpu.HBM if far(s) else pltpu.VMEM if s is NEAR else None
    inputs = [pltpu.with_memory_space_constraint(a, place(s)) if place(s) else a for a, s in zip(inputs, in_specs)]
    out_shape = [place(s)(o.shape, o.dtype) if place(s) else o for o, s in zip(outs, out_specs)]
    results = pl.pallas_call(
        body,
        in_specs=[ANY] * count + list(in_specs),
        out_specs=out_specs + [VMEM] * token,
        out_shape=out_shape + [array(8, 128)] * token,
        compiler_params=pltpu.CompilerParams(vmem_limit_bytes=limit * 2**20),
        cost_estimate=pl.CostEstimate(flops=int(MICROSECONDS[name] * 3.45e+09), bytes_accessed=0, transcendentals=0),
        name=name,
        **more,
    )(*after, *inputs)
    return list(results)


def hold(values, after):
    count = len(after)
    after = [pltpu.with_memory_space_constraint(a, pltpu.HBM) if math.prod(a.shape) > 8192 else a for a in after]
    return pl.pallas_call(
        lambda *refs: None,
        in_specs=[ANY] * (count + 1),
        out_specs=ANY,
        out_shape=array(*values.shape),
        input_output_aliases={count: 0},
        compiler_params=pltpu.CompilerParams(vmem_limit_bytes=2**20),
        name="hold",
    )(*after, values)


def array(*shape, dtype=HIGH):
    return jax.ShapeDtypeStruct(shape, dtype)


def pick_kernel(at_ref, *refs):
    *refs, sems = refs
    half = len(refs) // 2
    wait_all(start_all([(source.at[at_ref[0]], target) for source, target in zip(refs[:half], refs[half:])], sems))


def cut_kernel(layer, order, piece, blocks_ref, shares_ref, up_ref, down_ref, up_out, down_out, held, chosen_up, chosen_down, sems, down_sems):
    count, _, block = held.shape
    copies = []
    for b in range(count):
        start = pl.multiple_of(blocks_ref[b] * block, 128)
        copies.append(start_all([(up_ref.at[layer, :, pl.ds(start, block)], held.at[b])], sems.at[pl.ds(b, 1)]))
    downs = []
    for p, (b, h) in enumerate(order):
        start = pl.multiple_of(blocks_ref[b] * block + shares_ref[h] * piece, 16)
        target = chosen_down.at[p * piece : (p + 1) * piece]
        downs.append(pltpu.make_async_copy(down_ref.at[layer, pl.ds(start, piece), :], target, down_sems.at[p]))
        downs[-1].start()
    row = lax.broadcasted_iota(jnp.int32, (piece, block), 0)
    lane = lax.broadcasted_iota(jnp.int32, (piece, block), 1)
    chosen = [(lane == row + share * piece).astype(HIGH).astype(LOW) for share in (shares_ref[0], shares_ref[1])]
    wait_all(downs)
    outs = start_all([(chosen_down, down_out)], sems.at[pl.ds(count, 1)])
    for b in range(count):
        wait_all(copies[b])
        for p, (of, h) in enumerate(order):
            if of == b:
                chosen_up[p * piece : (p + 1) * piece] = wide(chosen[h], held[b], (1, 1)).astype(LOW)
    wait_all(outs + start_all([(chosen_up, up_out)], sems.at[pl.ds(0, 1)]))


def class_rows(count, dest):
    row, i = dest // count, dest % count
    if isinstance(dest, int):
        return row, pair_of(count, i)
    return row, (i, jnp.where(i == 0, count, 2 * count - i))


def spread_marked_kernel(count, at_ref, *rest):
    sources, (*outs, held), targets, sems = rest[:4], rest[4:-5], rest[-5:-1], rest[-1]
    wait_all(start_all(zip(sources, targets), sems))
    values_ref, segments_ref, padding_ref, table_ref = targets
    rows, part, width = values_ref.shape
    units = part // (2 * count)
    flags = jnp.concatenate([padding_ref[...], segments_ref[...], jnp.zeros((8 - 2 * rows, part), jnp.int32)], 0)
    flags = flags.astype(HIGH).astype(LOW)
    at = lax.broadcasted_iota(jnp.int32, (8, MARK), 0)
    lane = lax.broadcasted_iota(jnp.int32, (8, MARK), 1)
    for row in range(rows):
        pick = ((at == row) & (lane == 0)) | ((at == rows + row) & (lane == 1))
        marks = wide(flags, pick.astype(HIGH).astype(LOW), (0, 0))
        kind = marks[:, 1:2]
        values = values_ref[row]
        for t in range(table_ref.shape[0]):
            values = values + jnp.where(kind == float(t), table_ref[t : t + 1, :], 0.0)
        held[row, :, :, :width] = values.reshape(units, 2 * count, width)
        held[row, :, :, width:] = marks.reshape(units, 2 * count, MARK)
    for k, out in enumerate(outs):
        row, classes = class_rows(count, at_ref[0] ^ k)
        for h, at in enumerate(classes):
            out[h * units : (h + 1) * units, :] = held[row, :, at, :]


def spread_kernel(count, values_ref, out):
    rows, units, step, width = values_ref.shape
    for dest in range(rows * count):
        row, classes = class_rows(count, dest)
        for h, at in enumerate(classes):
            out[dest, h * units : (h + 1) * units, :] = values_ref[row, :, at, :]


def collect_kernel(count, blocks, *outs):
    rows, units, step, width = outs[0].shape
    part = blocks.shape[1] // len(outs)
    for source in range(rows * count):
        row, classes = class_rows(count, source)
        for n, out in enumerate(outs):
            for h, at in enumerate(classes):
                first = n * part + h * units
                out[row, :, at, :] = blocks[source, first : first + units, :]


def turned(at_ref, blocks):
    return [at_ref[0] ^ k for k in range(blocks)]


def enter_kernel(blocks, *refs):
    sources = refs[:blocks]
    feature_ref, send_ref, carried_ref, marks_ref, spectrum_ref, *sent_refs, held, sems = refs[blocks:]
    width = carried_ref.shape[1]
    rows = held.shape[0] // blocks
    wait_all(start_all([(ref, held.at[k * rows : (k + 1) * rows]) for k, ref in enumerate(sources)], sems))
    values = held[:, :width]
    carried_ref[...] = values
    marks_ref[...] = held[:, width:]
    stage_one(values * held[:, width : width + 1], feature_ref, send_ref, spectrum_ref, sent_refs)


def own_kernel(masked, layer, *refs):
    if layer is not None:
        *refs, up_in, down_in, out_ref, up_out, down_out, sems = refs
        copies = start_all([(up_in.at[layer], up_out), (down_in.at[layer], down_out)], sems)
    else:
        *refs, out_ref = refs
        copies = []
    spectrum_ref, carried_ref, mirror_ref, block_ref, *marks = refs
    mixed = unpack(spectrum_ref[...], mirror_ref[...], block_ref)
    if masked:
        mixed = mixed * marks[0][:, :1]
    out_ref[...] = carried_ref[...] + mixed
    wait_all(copies)


LANES = 1


def copies_of(pairs, sems):
    found = []
    for k, (source, target) in enumerate(pairs):
        rows = source.shape[0]
        parts = LANES if rows % (16 * LANES) == 0 else 1
        for part in range(parts):
            at = pl.ds(part * (rows // parts), rows // parts)
            found.append(pltpu.make_async_copy(source.at[at], target.at[at], sems.at[k, part]))
    return found


def start_all(pairs, sems):
    copies = copies_of(pairs, sems)
    for copy in copies:
        copy.start()
    return copies


def wait_all(copies):
    for copy in copies:
        copy.wait()


def keep(unit, inverse, held):
    width = unit.shape[1]
    held[:, :width] = unit
    held[:, width:] = jnp.broadcast_to(inverse, (unit.shape[0], held.shape[1] - width))


def weight_copies(layer, up_ref, down_ref, up_held, down_held, sems, chunk):
    width = up_held.shape[1]
    at = pl.ds(pl.multiple_of(chunk * width, 128), width)
    return (
        pltpu.make_async_copy(up_ref.at[layer, :, at], up_held.at[chunk], sems.at[0, chunk]),
        pltpu.make_async_copy(down_ref.at[layer, at, :], down_held.at[chunk], sems.at[1, chunk]),
    )


def next_weights(layer, refs, chunk):
    wait_all(weight_copies(layer, *refs, chunk))

    @pl.when(chunk + 1 < pl.num_programs(0))
    def _():
        for copy in weight_copies(layer, *refs, chunk + 1):
            copy.start()


def mix_kernel(layer, got, *refs):
    got_refs, refs = refs[:got], refs[got:]
    base_ref, mirror_ref, recv_ref, gain_ref, shift_ref, normed_out, unit_out, held_normed, held, sems = refs
    mixed = base_ref[...] + stage_two(got_refs, mirror_ref, recv_ref)
    unit, inverse = normalize(mixed)
    held_normed[...] = unit * gain_ref[layer, 0:1, :] + shift_ref[layer, 0:1, :]
    copies = start_all([(held_normed, normed_out)], sems)
    keep(unit, inverse, held)
    wait_all(copies + start_all([(held, unit_out)], sems.at[pl.ds(1, 1)]))


def chunk_of(chunk, width):
    return pl.ds(pl.multiple_of(chunk * width, 128), width)


def feed_kernel(layer, last, *refs):
    if last:
        *refs, held, delta_ref, low_ref, total_ref, more_sems, out_sems = refs
    else:
        *refs, held, low_ref, total_ref, up_held, down_held, feature_ref, send_ref, sems, more_sems, out_sems = refs
    normed_in, up_ref, up_bias_ref, down_ref, down_bias_ref, gain_ref, shift_ref, *refs = refs
    chunk = pl.program_id(0)
    width = low_ref.shape[1]
    if last:
        at_ref, upstream_ref, slope_ref, minor_ref, delta_far, carried_out = refs
        fetched = [(normed_in, total_ref)]
    else:
        marks_ref, feature_in, send_in, slope_ref, carried_ref, spectrum_ref, *sent_refs, unit_out = refs
        fetched = [(normed_in, total_ref), (feature_in, feature_ref), (send_in, send_ref)]
        weights = (up_ref, down_ref, up_held, down_held, sems)

    @pl.when(chunk == 0)
    def _():
        copies = start_all(fetched[:1], more_sems)
        if not last:
            for copy in weight_copies(layer, *weights, 0):
                copy.start()
        wait_all(copies)
        normed = total_ref[...]
        low_ref[...] = normed.astype(LOW)
        total_ref[...] = normed + down_bias_ref[layer : layer + 1, :]

    if last:
        at = chunk_of(chunk, width)
        up, down = up_ref[:, at], down_ref[at, :]
    else:
        next_weights(layer, weights, chunk)
        up, down = up_held[chunk], down_held[chunk]

        @pl.when(chunk == 1)
        def _():
            start_all(fetched[1:], more_sems.at[pl.ds(1, 2)])

    preact = wide(low_ref[...], up) + up_bias_ref[layer : layer + 1, :]
    value, slope = gelu_parts(preact)
    slope_ref[...] = slope.astype(slope_ref.dtype)
    total_ref[...] += wide(value.astype(LOW), down)

    @pl.when(chunk == pl.num_programs(0) - 1)
    def _():
        unit, inverse = normalize(total_ref[...])
        gain = gain_ref[layer, 1:2, :]
        carried = unit * gain + shift_ref[layer, 1:2, :]
        if last:
            blocks, rows, _ = upstream_ref.shape
            order = turned(at_ref, blocks)
            upstream = jnp.concatenate([upstream_ref[at] for at in order], 0)
            delta_out(upstream, unit, inverse, gain, delta_ref, minor_ref)
            copies = start_all([(delta_ref, delta_far)], out_sems)
            for k, at in enumerate(order):
                held[at] = carried[k * rows : (k + 1) * rows]
            wait_all(copies + start_all([(held, carried_out)], out_sems.at[pl.ds(1, 1)]))
        else:
            keep(unit, inverse, held)
            copies = start_all([(held, unit_out)], out_sems)
            carried_ref[...] = carried
            wait_all(copies_of(fetched[1:], more_sems.at[pl.ds(1, 2)]))
            stage_one(carried * marks_ref[:, :1], feature_ref, send_ref, spectrum_ref, sent_refs)
            wait_all(copies)


def delta_out(upstream, unit, inverse, gain, delta_ref, minor_ref):
    delta = norm_back(upstream, unit, inverse, gain)
    delta_ref[...] = delta
    rows = [upstream * unit, upstream, delta.astype(LOW).astype(HIGH)]
    for at, value in enumerate(rows):
        minor_ref[at : at + 1, :] = jnp.sum(value, 0, keepdims=True)
    minor_ref[len(rows) :, :] = jnp.zeros_like(minor_ref[len(rows) :, :])


def delta_kernel(layer, got, *refs):
    got_refs, refs = refs[:got], refs[got:]
    base_ref, marks_ref, mirror_ref, recv_ref, unit_in, gain_ref, minor_ref, delta_far, delta_ref, held, sems = refs
    copies = start_all([(unit_in, held)], sems)
    upstream = base_ref[...] + marks_ref[:, :1] * stage_two(got_refs, mirror_ref, recv_ref)
    wait_all(copies)
    width = upstream.shape[1]
    unit, inverse = held[:, :width], held[:, width : width + 1]
    delta_out(upstream, unit, inverse, gain_ref[layer, 1:2, :], delta_ref, minor_ref)
    wait_all(start_all([(delta_ref, delta_far)], sems))


def backward_kernel(layer, near, *refs):
    if near:
        *refs, low_ref, total_ref, held_unit, feature_ref, send_ref, more_sems = refs
    else:
        *refs, low_ref, total_ref, held_unit, feature_ref, send_ref, more_sems, up_held, down_held, sems = refs
    delta_in, slope_ref, up_ref, down_ref, unit_in, gain_ref, feature_in, send_in, *refs = refs
    mixed_ref, minor_ref, spectrum_ref, *sent_refs = refs
    chunk = pl.program_id(0)
    width = low_ref.shape[1]
    fetched = [(unit_in, held_unit), (feature_in, feature_ref), (send_in, send_ref)]

    @pl.when(chunk == 0)
    def _():
        copies = start_all([(delta_in, total_ref)], more_sems)
        if not near:
            for copy in weight_copies(layer, up_ref, down_ref, up_held, down_held, sems, 0):
                copy.start()
        wait_all(copies)
        low_ref[...] = total_ref[...].astype(LOW)
        minor_ref[...] = jnp.zeros_like(minor_ref)

    if near:
        at = chunk_of(chunk, width)
        up, down = up_ref[:, at], down_ref[at, :]
    else:
        next_weights(layer, (up_ref, down_ref, up_held, down_held, sems), chunk)
        up, down = up_held[chunk], down_held[chunk]

    @pl.when(chunk == (0 if near else 2))
    def _():
        start_all(fetched, more_sems.at[pl.ds(1, 3)])

    slope = (wide(low_ref[...], down, (1, 1)) * slope_ref[...].astype(HIGH)).astype(LOW)
    minor_ref[pl.ds(2 + chunk, 1), :] = jnp.sum(slope.astype(HIGH), 0, keepdims=True)
    total_ref[...] += wide(slope, up, (1, 1))

    @pl.when(chunk == pl.num_programs(0) - 1)
    def _():
        upstream = total_ref[...]
        wait_all(copies_of(fetched, more_sems.at[pl.ds(1, 3)]))
        unit, inverse = held_unit[:, :width], held_unit[:, width : width + 1]
        minor_ref[0:1, :] = jnp.sum(upstream * unit, 0, keepdims=True)
        minor_ref[1:2, :] = jnp.sum(upstream, 0, keepdims=True)
        mixed = norm_back(upstream, unit, inverse, gain_ref[layer, 0:1, :])
        mixed_ref[...] = mixed
        stage_one(mixed, feature_ref, send_ref, spectrum_ref, sent_refs)


def leave_kernel(types, got, *refs):
    got_refs, refs = refs[:got], refs[got:]
    at_ref, base_ref, marks_ref, mirror_ref, recv_ref, minor_ref, out, held, sems = refs
    upstream = base_ref[...] + marks_ref[:, :1] * stage_two(got_refs, mirror_ref, recv_ref)
    kind = marks_ref[:, 1:2]
    for t in range(types):
        minor_ref[t : t + 1, :] = jnp.sum(jnp.where(kind == float(t), upstream, 0.0), 0, keepdims=True)
    minor_ref[types:, :] = jnp.zeros_like(minor_ref[types:, :])
    blocks, rows, _ = held.shape
    for k, at in enumerate(turned(at_ref, blocks)):
        held[at] = upstream[k * rows : (k + 1) * rows]
    wait_all(start_all([(held, out)], sems))


def grads_kernel(plan, places, counts, *refs):
    starts_ref, refs = refs[0], refs[1:]
    normed_refs, refs = refs[: counts[0]], refs[counts[0] :]
    delta_refs, refs = refs[: counts[1]], refs[counts[1] :]
    up_in, bias_ref, down_in, *refs = refs
    *refs, normed_held, delta_held, up_ref, down_ref, normed_low, delta_low, hidden, back, sems, more_sems, out_sems = refs
    results, outs = refs[: len(refs) // 2], refs[len(refs) // 2 :]
    step = pl.program_id(0)
    blocks = len(plan)
    rows = normed_held.shape[1]
    units = up_ref.shape[0]
    piece = units // len(places)
    share = units // (pl.num_programs(0) - blocks)

    def copies(b):
        found = []
        for refs, held, parts in ((normed_refs, normed_held, plan[b][0]), (delta_refs, delta_held, plan[b][1])):
            at = 0
            for index, start, count in parts:
                source = refs[index]
                if start is not None:
                    source = source.at[pl.ds(pl.multiple_of(starts_ref[start], 8), count)]
                target = held.at[b % 2, at : at + count]
                found.append(pltpu.make_async_copy(source, target, sems.at[b, len(found)]))
                at += count
        return found

    def start(b):
        for copy in copies(b):
            copy.start()

    for b in range(blocks):

        @pl.when(step == b)
        def _():
            if b == 0:
                start(0)
                fetched = start_all([(up_in, up_ref), (down_in, down_ref)], more_sems)
            wait_all(copies(b))
            if b + 1 < blocks:
                start(b + 1)
            if b == 0:
                wait_all(fetched)
            at = slice(b * rows, (b + 1) * rows)
            normed = normed_held[b % 2].astype(LOW)
            delta = delta_held[b % 2].astype(LOW)
            normed_low[at] = normed
            delta_low[at] = delta
            value, slope = gelu_parts(wide(normed, up_ref[...], (1, 1)) + bias_ref[...])
            hidden[at] = value.astype(LOW)
            back[at] = (wide(delta, down_ref[...], (1, 1)) * slope).astype(LOW)

    def sent(c):
        found = []
        for p in range(c * share // piece, (c + 1) * share // piece):
            for h, (out, slot, first) in enumerate(places[p]):
                at = (slot, pl.ds(first, piece))
                found.append(pltpu.make_async_copy(outs[out].at[at], results[out].at[at], out_sems.at[p, h]))
        return found

    chunks = units // share
    for c in range(chunks):

        @pl.when(step == blocks + c)
        def _():
            at = slice(c * share, (c + 1) * share)
            both = (wide(back[:, at], normed_low[...], (0, 0)), wide(hidden[:, at], delta_low[...], (0, 0)))
            for p in range(c * share // piece, (c + 1) * share // piece):
                first_row = p * piece - c * share
                for (out, slot, first), a in zip(places[p], both):
                    outs[out][slot, first : first + piece] = a[first_row : first_row + piece]
            for copy in sent(c):
                copy.start()
            if c == chunks - 1:
                for k in range(chunks):
                    wait_all(sent(k))


def finish_kernel(layer, at_ref, *refs):
    *pieces, up_ref, down_ref, turned_ref = refs
    rows = pieces[0].shape[0] // 2
    for k, ref in enumerate(pieces[:4]):
        at = pl.multiple_of((at_ref[0] ^ k) * rows, 8)
        turned_ref[pl.ds(at, rows), :] = ref[:rows, :]
        down_ref[0, pl.ds(at, rows), :] = ref[rows:, :]
    up_ref[0] = turned_ref[...].T


def swap(values, axes, k):
    count = lax.axis_size(axes)
    return lax.ppermute(values, axes, [(i, i ^ k) for i in range(count)])


def exchange(blocks, axes, first=0):
    return [b if k == 0 else swap(b, axes, k) for k, b in enumerate(blocks, first)]


def sum_over(values, groups):
    for axes in groups:
        moved = [swap(values, axes, k) for k in range(1, lax.axis_size(axes))]
        values = sum(moved, values)
    return values


def local(inputs, segments, padding, type_table, ln_gain, ln_bias, up_weight, up_bias, down_weight, down_bias, out_grad):
    rows, part, width = inputs.shape
    layers, _, hidden_width = up_weight.shape
    types = type_table.shape[0]
    seq, count = lax.axis_size(SEQ), lax.axis_size(ROW)
    step = 2 * count
    units = part // step
    tokens = rows * part
    block = tokens // seq
    half = width // 2
    place = lax.axis_index(SEQ).reshape(1)

    feature = jnp.asarray(feature_table(width))
    mirror = jnp.asarray(mirror_table(half))
    tables = position_tables(count, part, seq)
    chunk = tables[0].shape[3] // (count - 1)
    sent_outs = [array(chunk, width)] * (count - 1)
    whole = array(tokens, width)
    kept = array(tokens, width + MARK)
    blocks_out = array(seq, block, width)
    minor_out = array(8, width)
    steps = hidden_width // width

    def spread(values, after):
        shaped = values.reshape(rows, units, step, width)
        out, token = call(functools.partial(spread_kernel, count), "spread", [shaped], [blocks_out], after, token=True)
        return lax.all_to_all(out, SEQ, 0, 0, tiled=True), token

    def collect(got, after):
        out = array(rows, units, step, width)
        *back, token = call(functools.partial(collect_kernel, count), "collect", [got], [out], after, token=True)
        return [b.reshape(inputs.shape) for b in back] + [token]

    weight_outs = [array(width, hidden_width, dtype=LOW), array(hidden_width, width, dtype=LOW)]

    def own(spectrum, carried, marks=None, after=(), token=False, layer=None):
        inputs = [spectrum, carried, mirror, block_t] + ([] if marks is None else [marks])
        kernel = functools.partial(own_kernel, marks is not None, layer)
        if layer is None:
            return call(kernel, "own_part", inputs, [whole], after, token=token)
        return call(
            kernel,
            "own_fetch",
            inputs + [up_weight, down_weight],
            [whole] + weight_outs,
            after,
            token=token,
            limit=8,
            in_specs=[VMEM] * len(inputs) + [HBM] * 2,
            out_specs=[VMEM, NEAR, NEAR],
            scratch_shapes=[pltpu.SemaphoreType.DMA((2, LANES))],
        )

    column = pl.BlockSpec((tokens, width), lambda c: (0, c))
    slope_out = array(tokens, hidden_width)
    scratch = [pltpu.VMEM((tokens, width), LOW), pltpu.VMEM((tokens, width), HIGH)]
    scratch += [pltpu.VMEM((steps, width, width), LOW)] * 2
    bias_spec = pl.BlockSpec((layers, width), lambda c: (0, c))

    held_kept = pltpu.VMEM(kept.shape, HIGH)
    dma = lambda n: pltpu.SemaphoreType.DMA((n, LANES))

    held_whole = pltpu.VMEM(whole.shape, HIGH)
    held_tables = [pltpu.VMEM(t, LOW) for t in (feature.shape, tables[0].shape[1:])]

    def mix(layer, got, base, after=()):
        inputs = got + [base, mirror, recv_t, ln_gain, ln_bias]
        return call(
            functools.partial(mix_kernel, layer, len(got)),
            "mix",
            inputs,
            [whole, kept],
            after,
            out_specs=[ANY, ANY] if layer == layers - 1 else [HBM, HBM],
            scratch_shapes=[held_whole, held_kept, dma(2)],
        )

    def feed(layer, normed, up, down, *more, after=(), token=False):
        last = layer == layers - 1
        inputs = [normed, up, up_bias, down, down_bias, ln_gain, ln_bias] + list(more)
        outs = [slope_out]
        outs += [minor_out, whole, blocks_out] if last else [whole, whole] + sent_outs + [kept]
        far = 2 if last else 1
        held = [pltpu.VMEM(blocks_out.shape, HIGH), held_whole] if last else [held_kept]
        fetches = [] if last else scratch[2:] + held_tables + [pltpu.SemaphoreType.DMA((2, steps))]
        weights = NEAR if last else HBM
        return call(
            functools.partial(feed_kernel, layer, last),
            "layer_feed" if last else "layer_forward",
            inputs,
            outs,
            after,
            near=last,
            token=token,
            grid=(steps,),
            in_specs=[ANY if last else HBM, weights, bias_spec, weights]
            + [VMEM] * 3
            + ([SMEM, VMEM] if last else [VMEM, HBM, HBM]),
            out_specs=[column] + [VMEM] * (len(outs) - 1 - far) + ([ANY, HBM] if last else [HBM]),
            scratch_shapes=held + scratch[:2] + fetches + [dma(3), dma(2)],
        )

    def backward(layer, delta, slope, up, down, kept, after=(), token=False):
        inputs = [delta, slope, up, down, kept, ln_gain, feature, send_t]
        outs = [whole, minor_out, whole] + sent_outs
        last = layer == layers - 1
        return call(
            functools.partial(backward_kernel, layer, last),
            "layer_backward" if last else "layer_stream",
            inputs,
            outs,
            after,
            near=last,
            token=token,
            grid=(steps,),
            in_specs=[ANY, column, NEAR, NEAR, ANY, VMEM, HBM, HBM]
            if last
            else [HBM, column, HBM, HBM, HBM, VMEM, HBM, HBM],
            out_specs=[VMEM] * len(outs),
            scratch_shapes=scratch[:2]
            + [held_kept]
            + held_tables
            + [dma(4)]
            + ([] if last else scratch[2:] + [pltpu.SemaphoreType.DMA((2, steps))]),
        )

    def delta(layer, got, base, marks, kept, after=()):
        inputs = got + [base, marks, mirror, recv_t, kept, ln_gain]
        return call(
            functools.partial(delta_kernel, layer, len(got)),
            "delta",
            inputs,
            [minor_out, whole],
            after,
            in_specs=[VMEM] * (len(got) + 4) + [HBM, VMEM],
            out_specs=[VMEM, HBM],
            scratch_shapes=[held_whole, held_kept, dma(1)],
        )

    columns = lax.axis_size("x")
    planes, shares = lax.axis_size(PLANES), lax.axis_size(SHARES)
    unit_block = hidden_width // seq
    piece = unit_block // shares
    x, dy, core, zh, zl = (lax.axis_index(a) for a in ("x", "dy", "core", "zh", "zl"))
    swapped = columns == 2

    def pair_pieces():
        nearby = [0, 1] if swapped else list(range(columns))
        own_x, own_dy, own_zh = (x, dy, zh) if swapped else (0, 0, 0)
        blocks = [((own_zh ^ b) * 2 + zl) * columns + (own_x ^ a) for a in nearby for b in (0, 1)]
        order = [(a * 2 + b, c) for a in nearby for c in (0, 1) for b in (0, 1)]
        return blocks, [(own_dy ^ c) * 2 + core for c in (0, 1)], order

    def plane_pieces():
        blocks = [z * columns + x for z in range(planes)]
        return blocks, [dy * 2 + (core ^ c) for c in (1, 0)], [(z, c) for c in (0, 1) for z in range(planes)]

    def bias_of(layer):
        blocks, shared, order = pair_pieces() if layer == layers - 1 else plane_pieces()
        starts = [blocks[b] * unit_block + shared[h] * piece for b, h in order]
        return jnp.concatenate([lax.dynamic_slice(up_bias, (layer, s), (1, piece)) for s in starts], 1)

    biases = [bias_of(layer) for layer in range(layers)]

    def cut(layer, after):
        blocks, shared, order = pair_pieces() if layer == layers - 1 else plane_pieces()
        starts = [blocks[b] * unit_block + shared[h] * piece for b, h in order]
        bias = biases[layer]
        if unit_block % 128:
            up = [lax.dynamic_slice_in_dim(up_weight[layer], s, piece, 1).T for s in starts]
            down = [lax.dynamic_slice_in_dim(down_weight[layer], s, piece, 0) for s in starts]
            return jnp.concatenate(up, 0), bias, jnp.concatenate(down, 0), bias
        out = array(piece * len(order), width, dtype=LOW)
        up, down, token = call(
            functools.partial(cut_kernel, layer, order, piece),
            "cut",
            [jnp.stack(blocks).astype(jnp.int32), jnp.stack(shared).astype(jnp.int32), up_weight, down_weight],
            [out, out],
            after,
            token=True,
            in_specs=[SMEM, SMEM, HBM, HBM],
            out_specs=[HBM, HBM],
            scratch_shapes=[
                pltpu.VMEM((len(blocks), width, unit_block), LOW),
                pltpu.VMEM(out.shape, LOW),
                pltpu.VMEM(out.shape, LOW),
                dma(len(blocks) + 1),
                pltpu.SemaphoreType.DMA((len(order),)),
            ],
        )
        return up, bias, down, token

    def weight_grads(normed, starts, deltas, plan, cuts, places, outs, after=()):
        size = sum(r for _, _, r in plan[0][0])
        chosen = cuts[0].shape[0]
        share = max(384 // piece, 1) * piece
        total = len(plan) * size
        plan = [(plan[b][0] + plan[b + 1][0], plan[b][1] + plan[b + 1][1]) for b in range(0, len(plan), 2)]
        size = 2 * size
        inputs = [jnp.stack(starts).astype(jnp.int32)] + normed + deltas + list(cuts[:3])
        return call(
            functools.partial(grads_kernel, plan, places, (len(normed), len(deltas))),
            "weight_grads",
            inputs,
            outs,
            after,
            token=True,
            limit=56,
            grid=(len(plan) + chosen // share,),
            in_specs=[SMEM] + [HBM] * (len(normed) + len(deltas)) + [HBM, VMEM, HBM],
            out_specs=[HBM] * len(outs),
            scratch_shapes=[pltpu.VMEM(o.shape, HIGH) for o in outs]
            + [pltpu.VMEM((2, size, width), HIGH)] * 2
            + [pltpu.VMEM(cuts[0].shape, LOW)] * 2
            + [pltpu.VMEM((total, width), LOW)] * 2
            + [pltpu.VMEM((total, chosen), LOW)] * 2
            + [pltpu.SemaphoreType.DMA((len(plan), 8)), dma(2), pltpu.SemaphoreType.DMA((len(places), 2))],
        )

    def shared_out(summed):
        along = swap(summed, "dy", 1)
        return [summed, swap(summed, "core", 1), along, swap(along, "core", 1)]

    def pair_grads(normed, deltas, cuts, after):
        plan = [([(b, None, tokens)], [(b, None, tokens)]) for b in range(4)]
        order = [(a, c, b) for a in range(columns) for c in (0, 1) for b in (0, 1)]
        if not swapped:
            places = [((0, p, 0), (0, p, piece)) for p in range(len(order))]
            out = array(len(order), 2 * piece, width)
            return weight_grads(normed, [0], deltas, plan, cuts, places, [out], after)
        places = [((a, 2 * c + b, 0), (2 + c, 2 * a + b, 0)) for a, c, b in order]
        return weight_grads(normed, [0], deltas, plan, cuts, places, [array(4, piece, width)] * 4, after)

    def pair_first(sums):
        if not swapped:
            return [lax.psum_scatter(sums[0], ("x", "dy", "zh"), scatter_dimension=0, tiled=True)], []
        up, up_far, down, down_far = sums
        got_up, got_down = swap(up_far, "x", 1), swap(down_far, "dy", 1)
        return [up[2:] + got_up[2:], down[2:] + got_down[2:]], [up[:2] + got_up[:2], down[:2] + got_down[:2]]

    def pair_step(far, near):
        if not swapped:
            return far, near
        got_up, got_down = swap(far[0], "dy", 1), swap(far[1], "x", 1)
        up, down = near
        far = jnp.concatenate([up[1] + got_up[1], down[1] + got_down[1]], 0)
        return [far], [jnp.concatenate([up[0] + got_up[0], down[0] + got_down[0]], 0)]

    def pair_last(far, near):
        if not swapped:
            summed = far[0].reshape(2 * piece, width)
            return lax.psum(summed, "do") if lax.axis_size("do") > 1 else summed
        return near[0] + swap(far[0], "zh", 1)

    def plane_first(values):
        if not swapped:
            return [lax.all_gather(values, ("dy", "x"), tiled=True)]
        return [swap(values, "x", 1), swap(values, "dy", 1)]

    def plane_rest(found):
        if not swapped:
            return []
        rows = tokens // 2
        return [swap(found[0][:rows], "dy", 1), swap(found[1][rows:], "x", 1)]

    def plane_grads(normed, deltas, cuts, after):
        group = lax.axis_size(("dy", "x"))
        out = array(planes, 2 * piece, width)
        places = [((h, z, 0), (h, z, piece)) for h in range(2) for z in range(planes)]
        rows = tokens // 2
        parts = [[(0, None, tokens)], [(1, None, tokens)], [(2, None, tokens)], [(3, None, rows), (4, None, rows)]]
        starts = [((dy ^ a) * columns + (x ^ b)) * tokens for a, b in ((0, 0), (0, 1), (1, 0), (1, 1))]
        if not swapped:
            parts = [[(0, b, tokens)] for b in range(group)]
            starts = [b * tokens for b in range(group)]
        starts = [jnp.asarray(s, jnp.int32) for s in starts]
        plan = [([(0, b, tokens)], parts[b]) for b in range(group)]
        return weight_grads([normed], starts, deltas, plan, cuts, places, [out, out], after)

    def plane_sum(both):
        summed = lax.psum_scatter(both.reshape(-1, width), PLANES, scatter_dimension=0, tiled=True)
        return lax.psum(summed, "do") if lax.axis_size("do") > 1 else summed

    def alone(stage, *operands):
        shapes = jax.eval_shape(stage, *operands)
        blank = lambda *_: jax.tree.map(lambda a: jnp.zeros(a.shape, a.dtype), shapes)
        return lax.cond(place[0] < 1000000, stage, blank, *operands)

    def send_and_own(sent, spectrum, mixed, marks):
        return exchange(sent, ROW, 1), own(spectrum, mixed, marks, token=True)

    held = call(
        functools.partial(spread_marked_kernel, count),
        "spread_marked",
        [place, inputs, segments, padding, type_table],
        [array(block, width + MARK)] * seq,
        in_specs=[SMEM] + [HBM] * 4,
        scratch_shapes=[pltpu.VMEM((rows, units, step, width + MARK), HIGH)]
        + [pltpu.VMEM(a.shape, a.dtype) for a in (inputs, segments, padding, type_table)]
        + [dma(4)],
    )
    held = exchange(held, SEQ)
    send_t, recv_t, block_t = call(
        pick_kernel,
        "pick",
        [place] + [jnp.asarray(t) for t in tables],
        [array(*t.shape[1:], dtype=LOW) for t in tables],
        held[1:4],
        in_specs=[SMEM] + [HBM] * 3,
        scratch_shapes=[dma(3)],
    )
    cuts = [None] * (layers - 1) + [cut(layers - 1, held[1:4])]
    carried, marks, spectrum, *sent = call(
        functools.partial(enter_kernel, seq),
        "enter",
        held + [feature, send_t],
        [whole, array(tokens, MARK), whole] + sent_outs,
        [cuts[-1][3]] + biases,
        in_specs=[VMEM] + [HBM] * (seq - 1) + [VMEM] * 2,
        scratch_shapes=[pltpu.VMEM((tokens, width + MARK), HIGH), dma(seq)],
    )
    upstream, made = spread(out_grad, sent[:1])
    saved = []
    for layer in range(layers - 1):
        got = exchange(sent, ROW, 1)
        base = own(spectrum, carried, after=[made])[0]
        normed, kept_one = mix(layer, got, base)
        all_normed = lax.all_gather(normed, ("dy", "x"), tiled=True)
        slope, carried, spectrum, *sent, kept_two = feed(layer, normed, up_weight, down_weight, marks, feature, send_t)
        saved.append((all_normed, kept_one, slope, kept_two))
    got = exchange(sent, ROW, 1)
    base, up, down = own(spectrum, carried, after=[upstream], layer=layers - 1)
    normed, kept_one = mix(layers - 1, got, base)

    def feed_stage(normed, kept, up, down, upstream):
        moved = swap(normed, "core", 1), swap(normed, "zl", 1)
        slope, minor_two, delta, outputs = feed(layers - 1, normed, up, down, place, upstream)
        return moved, minor_two, delta, outputs, backward(layers - 1, delta, slope, up, down, kept)

    moved_normed, minor_two, delta_two, outputs, (mixed, minor_one, spectrum, *sent) = alone(
        feed_stage, normed, kept_one, up, down, upstream
    )
    minors = [minor_two, minor_one]

    def send_and_swap(sent, spectrum, mixed, marks, normed_far, delta_two):
        got = exchange(sent, ROW, 1)
        return got, own(spectrum, mixed, marks)[0], swap(normed_far, "core", 1), swap(delta_two, "core", 1)

    got, base, *moved_delta = alone(send_and_swap, sent, spectrum, mixed, marks, moved_normed[1], delta_two)
    there, kept_one, slope, kept_two = saved[0]

    minor_two, delta_one = delta(0, got, base, marks, kept_two)

    def back_stage(delta_two, delta_one, kept_one, slope):
        cuts = cut(0, [delta_one])
        back = backward(0, delta_one, slope, up_weight, down_weight, kept_one, [cuts[3]])
        return swap(delta_two, "zl", 1), plane_first(delta_one), cuts, back

    delta_far, found, cuts[0], (mixed, minor_one, spectrum, *sent) = alone(
        back_stage, delta_two, delta_one, kept_one, slope
    )
    minors += [minor_two, minor_one]

    def grads_stage(normed, delta_two, delta_far, there, found, cuts, outputs):
        found = ([delta_one] if swapped else []) + found + plane_rest(found)
        deltas = delta_two + [delta_far, swap(delta_far, "core", 1)]
        outputs = lax.all_to_all(outputs, SEQ, 0, 0, tiled=True)
        *sums, token = pair_grads(normed, deltas, cuts[1], [])
        return plane_grads(there, found, cuts[0], [token])[:2], sums, outputs

    parts, sums, outputs = alone(
        grads_stage,
        [normed, moved_normed[0], moved_normed[1], moved_delta[0]],
        [delta_two, moved_delta[1]],
        delta_far,
        there,
        found,
        cuts,
        outputs,
    )

    both = parts[1] + swap(parts[0], "core", 1)
    whole_sum = plane_sum(both)

    def first_stage(sums, sent, spectrum, mixed, marks):
        return pair_first(sums), exchange(sent, ROW, 1), own(spectrum, mixed, marks)[0]

    (far, near), got, base = alone(first_stage, sums, sent, spectrum, mixed, marks)

    def middle_stage(far, near, outputs, minors, got, base, marks):
        minor_table, blocks = call(
            functools.partial(leave_kernel, types, len(got)),
            "leave",
            got + [place, base, marks, mirror, recv_t],
            [minor_out, blocks_out],
            out_specs=[VMEM, HBM],
            scratch_shapes=[pltpu.VMEM(blocks_out.shape, HIGH), dma(1)],
        )
        minor = sum_over(jnp.concatenate(minors + [minor_table], 0), [("core",)])
        return pair_step(far, near), minor, collect(outputs, [])[0], blocks

    (far, near), minor, outputs, blocks = alone(middle_stage, far, near, outputs, minors, got, base, marks)

    share = lax.axis_index(SHARES).reshape(1)
    outs = [array(layers, width, unit_block), array(layers, unit_block, width)]

    def finish(layer, pieces, grads):
        return call(
            functools.partial(finish_kernel, layer),
            "finish",
            [share] + pieces + grads,
            outs,
            in_specs=[SMEM] + [VMEM] * len(pieces) + [ANY] * len(grads),
            out_specs=[
                pl.BlockSpec((1,) + o.shape[1:], functools.partial(lambda l, i: (l, 0, 0), layer)) for o in outs
            ],
            grid=(1,),
            input_output_aliases={5: 0, 6: 1} if grads else {},
            scratch_shapes=[pltpu.VMEM((unit_block, width), HIGH)],
        )

    def last_stage(far, near, minor, whole_sum):
        return pair_last(far, near), sum_over(minor, [("dy", "x"), ("do",)]), shared_out(whole_sum)[1:]

    summed, minor, shared = alone(last_stage, far, near, minor, whole_sum)
    grads = finish(0, [whole_sum] + shared, [])

    pieces = shared_out(summed)
    blocks = lax.all_to_all(hold(blocks, [summed]), SEQ, 0, 0, tiled=True)
    minor = sum_over(minor, [PLANES])
    input_grad, _ = collect(blocks, [])
    up_grad, down_grad = finish(1, pieces, grads)
    ends = [minor[16 * (layers - 1 - l) :][:16] for l in range(layers)]
    table_grad = minor[16 * layers :][:types]
    gain_grad = jnp.stack([jnp.stack([e[8], e[0]]) for e in ends])
    shift_grad = jnp.stack([jnp.stack([e[9], e[1]]) for e in ends])
    down_vec = jnp.stack([e[2] for e in ends])
    up_vec = jnp.stack([e[10 : 10 + steps].reshape(-1) for e in ends])
    up_vec = lax.dynamic_slice_in_dim(up_vec, place[0] * unit_block, unit_block, 1)

    return outputs, input_grad, table_grad, gain_grad, shift_grad, up_grad, up_vec, down_grad, down_vec


def solution(mesh):
    dp, seq = mesh.shape["dp"], mesh.shape["seq"]
    shape = (dp // 4, 2, 2, 2, 2, seq // 4)
    finer = Mesh(mesh.devices.reshape(shape), ALL)
    in_specs = (P(DP, SEQ, None), P(DP, SEQ), P(DP, SEQ)) + (P(),) * 7 + (P(DP, SEQ, None),)
    out_specs = (
        P(DP, SEQ, None),
        P(DP, SEQ, None),
        P(),
        P(),
        P(),
        P(None, None, SEQ),
        P(None, SEQ),
        P(None, SEQ, None),
        P(),
    )
    return jax.shard_map(local, mesh=finer, in_specs=in_specs, out_specs=out_specs, check_vma=False)
```
